32 devices in a mesh: rep: 2 (over x), shard: 16 (over z, y, core).
Axes of the slice: x: 2, y: 2, z: 4, core: 2. Of those that a mesh axis runs over, the one named last changes fastest.
Arguments:
- hidden_in: bfloat16 [2, 2048, 2048], P('rep', 'shard'), may hold values from -6 to 6
- segments: int32 [2, 2048], P('rep'), may hold values from 0 to 7, never falling along the last dimension, each value on 1 to 1024 neighbouring positions
- cotangent: bfloat16 [2, 2048, 2048], P('rep', 'shard'), may hold values from -6 to 6
- qkv_weight: bfloat16 [2048, 2560], P('shard'), may hold values from -0.125 to 0.125
- out_weight: bfloat16 [2048, 2048], P('shard'), may hold values from -0.5 to 0.5
- gate_up_weight: bfloat16 [2048, 11264], P('shard'), may hold values from -0.125 to 0.125
- down_weight: bfloat16 [5632, 2048], P('shard'), may hold values from -0.078125 to 0.078125
- attn_gain: bfloat16 [2048], P('shard'), may hold values from 0.099609375 to 1.8984375
- ffn_gain: bfloat16 [2048], P('shard'), may hold values from 0.099609375 to 1.8984375
Outputs:
- hidden_out: bfloat16 [2, 2048, 2048], P('rep', 'shard')
- grad_hidden: bfloat16 [2, 2048, 2048], P('rep', 'shard')
- grad_qkv_weight: float32 [2048, 2560], P('shard')
- grad_out_weight: float32 [2048, 2048], P('shard')
- grad_gate_up_weight: float32 [2048, 11264], P('shard')
- grad_down_weight: float32 [5632, 2048], P('shard')
- grad_attn_gain: float32 [2048], P('shard')
- grad_ffn_gain: float32 [2048], P('shard')
The draws below stay inside these ranges and needn't reach their ends.
Inputs may be any that keep to these rules, and one draw needn't show every extreme that they name: `segments`: segment numbers never fall along a sequence; a document holds at most 1024 tokens, and some document holds exactly that many.
All inputs are finite; a program needn't handle non-finite values.
Results may differ from the reference program's by a relative error of at most 0.014.
Values may be sent and summed in bfloat16 or wider, within the bound.
No kernel may reach another device: no remote copies, remote signals or barrier semaphores. Data moves between devices by JAX's collectives and lax.ppermute only.
A program may use at most 448 MiB of HBM per device.

```python
import math
import jax
import jax.numpy as jnp
import numpy as np
from jax import lax

D = 2048
HEADS = 32
KV_HEADS = 4
HEAD_DIM = 64
FF = 5632
LENGTH = 2048
SEQS = 2
QKVW = 2560


def shard_levels(stream_key, shape, shards, low, top_value):
    level, own = 1.0, jax.random.fold_in(stream_key, 6)
    for axis_at, shards_of in shards:
        heights = jnp.exp(jax.random.uniform(jax.random.fold_in(own, axis_at), (shards_of,), jnp.float32, low / len(shards), top_value / len(shards)))
        level = level * jnp.repeat(heights, shape[axis_at] // shards_of).reshape([-1 if axis == axis_at else 1 for axis in range(len(shape))])
    return level


def split_up(count, total, reach, skew):
    portions = [(1 << 20) // math.isqrt(standing ** skew) + 1 for standing in range(2, count + 1)]
    rest, counts = total - reach - (count - 1), [1] * (count - 1)
    while rest > 0:
        movable = [i for i in range(count - 1) if counts[i] < reach]
        whole, remaining = sum([portions[i] for i in movable]), rest
        for i in movable:
            addition = min(reach - counts[i], max(1, remaining * portions[i] // whole), rest)
            counts[i] = counts[i] + addition
            rest = rest - addition
    return np.array([reach] + counts)


def ragged(own_key, amount, total, reach, skew):
    if amount == 2:
        one = jax.random.randint(own_key, (), max(1, total - reach), min(reach, total - 1) + 1)
        return jnp.stack([one, total - one])
    tallies = jnp.asarray(split_up(amount, total, reach, skew), jnp.int32)
    twos = (amount - 1) // 2
    source_of, receiver = tallies[1:1 + 2 * twos:2], tallies[2:2 + 2 * twos:2]
    room = jnp.minimum(source_of - 1, reach - receiver)
    passed = jax.random.randint(jax.random.fold_in(own_key, 1), (twos,), 0, 1 << 20) % (room + 1)
    tallies = tallies.at[1:1 + 2 * twos:2].set(source_of - passed).at[2:2 + 2 * twos:2].set(receiver + passed)
    return tallies[jax.random.permutation(jax.random.fold_in(own_key, 2), amount)]


def centred(key, dims, scale, bound, shards=(), kind=jnp.bfloat16):
    array = jax.random.normal(key, dims, jnp.float32) * scale
    if len(shards) > 0:
        array = shard_levels(key, dims, shards, -0.22, 0.18) * array
    return jnp.clip(array, min=-bound, max=bound).astype(kind)


def setup_inputs(seed: int = 0) -> dict:
    seeds = jax.random.split(jax.random.key(seed), 10)
    hidden_in = centred(seeds[0], (SEQS, LENGTH, D), 1.0, 6.0, ((0, 2), (1, 16)))
    segments = jax.vmap(lambda own: jnp.searchsorted(jnp.cumsum(ragged(own, 8, LENGTH, LENGTH // 2, 2)), jnp.arange(LENGTH), side="right"))(jax.random.split(seeds[1], SEQS)).reshape((SEQS, LENGTH)).astype(jnp.int32)
    cotangent = centred(seeds[2], (SEQS, LENGTH, D), 1.0, 6.0, ((0, 2), (1, 16)))
    qkv_weight = centred(seeds[3], (D, QKVW), D ** -0.5, 0.125, ((0, 16),))
    out_weight = centred(seeds[4], (HEADS * HEAD_DIM, D), (HEADS * HEAD_DIM // 16) ** -0.5, 0.5, ((0, 16),))
    gate_up_weight = centred(seeds[5], (D, 2 * FF), D ** -0.5, 0.125, ((0, 16),))
    down_weight = centred(seeds[6], (FF, D), FF ** -0.5, 0.078125, ((0, 16),))
    attn_gain = jnp.clip(1.0 + 0.18 * jax.random.normal(seeds[7], (D,), jnp.float32), 0.099609375, 1.8984375).astype(jnp.bfloat16)
    ffn_gain = jnp.clip(1.0 + 0.18 * jax.random.normal(seeds[8], (D,), jnp.float32), 0.099609375, 1.8984375).astype(jnp.bfloat16)
    return {"hidden_in": hidden_in, "segments": segments, "cotangent": cotangent, "qkv_weight": qkv_weight, "out_weight": out_weight, "gate_up_weight": gate_up_weight, "down_weight": down_weight, "attn_gain": attn_gain, "ffn_gain": ffn_gain}


EPS = 1e-05

def rms_forward(values, gain):
    factor = lax.rsqrt(lax.optimization_barrier(jnp.mean(values * values, -1, keepdims=True)) + EPS)
    normed = values * factor
    return (factor, normed, (normed * gain).astype(jnp.bfloat16))

def rms_backward(grad_normed, factor, normed, gain):
    gain_grad = lax.optimization_barrier(jnp.sum(grad_normed * normed, 0))
    scaled = grad_normed * gain
    return (gain_grad, factor * (scaled - normed * lax.optimization_barrier(jnp.mean(scaled * normed, -1, keepdims=True))))

def rope_tables(positions):
    freqs = jnp.exp(jnp.arange(HEAD_DIM // 2, dtype=jnp.float32) * (-2.0 * math.log(10000.0) / HEAD_DIM))
    angles = positions.astype(jnp.float32)[:, None] * freqs[None, :]
    return (jnp.cos(angles)[:, None, :], jnp.sin(angles)[:, None, :])

def rope_apply(values, cosine, sine):
    half = values.shape[-1] // 2
    first = values[..., :half]
    second = values[..., half:]
    return jnp.concatenate([first * cosine - second * sine, second * cosine + first * sine], -1)

def rope_revert(values, cosine, sine):
    half = values.shape[-1] // 2
    first = values[..., :half]
    second = values[..., half:]
    return jnp.concatenate([first * cosine + second * sine, second * cosine - first * sine], -1)

def pair_scores(pair_queries, key_head, allowed):
    scores = jnp.dot(pair_queries, key_head.T, preferred_element_type=jnp.float32) * HEAD_DIM ** (-0.5)
    return jnp.where(allowed, scores, -jnp.inf)

def pair_forward(pair_queries, key_head, value_head, allowed):
    scores = pair_scores(pair_queries, key_head, allowed)
    top = lax.optimization_barrier(jnp.max(scores, -1, keepdims=True))
    expon = jnp.exp(scores - top)
    total = lax.optimization_barrier(jnp.sum(expon, -1, keepdims=True))
    weights_half = (expon / total).astype(jnp.bfloat16)
    attended = jnp.dot(weights_half, value_head, preferred_element_type=jnp.float32).astype(jnp.bfloat16)
    return (attended, (top + jnp.log(total))[:, 0])

def pair_backward(pair_queries, key_head, value_head, allowed, logsum, attended, grad_att):
    scores = pair_scores(pair_queries, key_head, allowed)
    probs = jnp.where(allowed, jnp.exp(scores - logsum[:, None]), 0.0)
    delta = lax.optimization_barrier(jnp.sum(grad_att.astype(jnp.float32) * attended.astype(jnp.float32), -1, keepdims=True))
    grad_probs = jnp.dot(grad_att, value_head.T, preferred_element_type=jnp.float32)
    grad_scores = (probs * (grad_probs - delta) * HEAD_DIM ** (-0.5)).astype(jnp.bfloat16)
    grad_query = jnp.dot(grad_scores, key_head, preferred_element_type=jnp.float32)
    grad_key = jnp.dot(grad_scores.T, pair_queries, preferred_element_type=jnp.float32)
    grad_value = jnp.dot(probs.astype(jnp.bfloat16).T, grad_att, preferred_element_type=jnp.float32)
    return (grad_query, grad_key, grad_value)

def sequence_layer(hidden_row, seg_row, cot_row, qkv_weight, out_weight, gate_up_weight, down_weight, gain_one, gain_two):
    length = hidden_row.shape[0]
    qsize = HEADS * HEAD_DIM
    ksize = KV_HEADS * HEAD_DIM
    pairs = HEADS // 2
    per_group = HEADS // KV_HEADS // 2
    token_index = jnp.arange(length, dtype=jnp.int32)
    starts = lax.optimization_barrier(jnp.sum((seg_row[None, :] < seg_row[:, None]).astype(jnp.int32), 1))
    cosine, sine = rope_tables(token_index - starts)
    hidden32 = hidden_row.astype(jnp.float32)
    factor_one, normed_one, input_one = rms_forward(hidden32, gain_one)
    projections = jnp.dot(input_one, qkv_weight, preferred_element_type=jnp.float32)
    queries = rope_apply(projections[:, :qsize].reshape(length, HEADS, HEAD_DIM), cosine, sine).astype(jnp.bfloat16)
    keys = rope_apply(projections[:, qsize:qsize + ksize].reshape(length, KV_HEADS, HEAD_DIM), cosine, sine).astype(jnp.bfloat16)
    values = projections[:, qsize + ksize:].astype(jnp.bfloat16).reshape(length, KV_HEADS, HEAD_DIM)
    key_heads = keys.transpose(1, 0, 2)
    value_heads = values.transpose(1, 0, 2)
    query_index = jnp.concatenate([token_index, token_index])
    query_seg = jnp.concatenate([seg_row, seg_row])
    allowed = (token_index[None, :] <= query_index[:, None]) & (seg_row[None, :] == query_seg[:, None])
    query_pairs = queries.reshape(length, pairs, 2, HEAD_DIM).transpose(1, 2, 0, 3).reshape(pairs, 2 * length, HEAD_DIM)
    pair_ids = jnp.arange(pairs, dtype=jnp.int32)

    def forward_pair(carry, item):
        pair_queries, pair_index = item
        group = pair_index // per_group
        out, logsum = pair_forward(pair_queries, key_heads[group], value_heads[group], allowed)
        return (carry, (out, logsum))
    _, (pair_out, pair_logsum) = lax.scan(forward_pair, None, (query_pairs, pair_ids))
    attended = pair_out.reshape(pairs, 2, length, HEAD_DIM).transpose(2, 0, 1, 3).reshape(length, qsize)
    residual = hidden32 + jnp.dot(attended, out_weight, preferred_element_type=jnp.float32)
    factor_two, normed_two, input_two = rms_forward(residual, gain_two)
    gate_up = jnp.dot(input_two, gate_up_weight, preferred_element_type=jnp.float32)
    gate = gate_up[:, :FF]
    upward = gate_up[:, FF:]
    sigma = jax.nn.sigmoid(gate)
    activation = (gate * sigma * upward).astype(jnp.bfloat16)
    hidden_out = (residual + jnp.dot(activation, down_weight, preferred_element_type=jnp.float32)).astype(jnp.bfloat16)
    down_term = jnp.dot(activation.T, cot_row, preferred_element_type=jnp.float32)
    grad_activation = jnp.dot(cot_row, down_weight.T, preferred_element_type=jnp.float32)
    grad_gate = grad_activation * upward * (sigma * (1.0 + gate * (1.0 - sigma)))
    grad_up = grad_activation * gate * sigma
    grad_gate_up = jnp.concatenate([grad_gate, grad_up], -1).astype(jnp.bfloat16)
    gate_up_term = jnp.dot(input_two.T, grad_gate_up, preferred_element_type=jnp.float32)
    grad_input_two = jnp.dot(grad_gate_up, gate_up_weight.T, preferred_element_type=jnp.float32)
    gain_two_term, grad_back_two = rms_backward(grad_input_two, factor_two, normed_two, gain_two)
    grad_residual = cot_row.astype(jnp.float32) + grad_back_two
    residual_half = grad_residual.astype(jnp.bfloat16)
    out_term = jnp.dot(attended.T, residual_half, preferred_element_type=jnp.float32)
    grad_attended = jnp.dot(residual_half, out_weight.T, preferred_element_type=jnp.float32).astype(jnp.bfloat16)
    grad_pairs = grad_attended.reshape(length, pairs, 2, HEAD_DIM).transpose(1, 2, 0, 3).reshape(pairs, 2 * length, HEAD_DIM)

    def backward_pair(carry, item):
        pair_queries, pair_grad, pair_att, pair_log, pair_index = item
        group = pair_index // per_group
        grad_query, grad_key, grad_value = pair_backward(pair_queries, key_heads[group], value_heads[group], allowed, pair_log, pair_att, pair_grad)
        key_acc = carry[0].at[:, group].add(grad_key)
        value_acc = carry[1].at[:, group].add(grad_value)
        return ((key_acc, value_acc), grad_query)
    zero_acc = jnp.zeros((length, KV_HEADS, HEAD_DIM), jnp.float32)
    (key_sums, value_sums), query_grads = lax.scan(backward_pair, (zero_acc, zero_acc), (query_pairs, grad_pairs, pair_out, pair_logsum, pair_ids))
    grad_queries = query_grads.reshape(pairs, 2, length, HEAD_DIM).transpose(2, 0, 1, 3).reshape(length, HEADS, HEAD_DIM)
    grad_queries = rope_revert(grad_queries, cosine, sine).reshape(length, qsize)
    grad_keys = rope_revert(key_sums, cosine, sine).reshape(length, ksize)
    grad_projections = jnp.concatenate([grad_queries, grad_keys, value_sums.reshape(length, ksize)], -1).astype(jnp.bfloat16)
    qkv_term = jnp.dot(input_one.T, grad_projections, preferred_element_type=jnp.float32)
    grad_input_one = jnp.dot(grad_projections, qkv_weight.T, preferred_element_type=jnp.float32)
    gain_one_term, grad_back_one = rms_backward(grad_input_one, factor_one, normed_one, gain_one)
    grad_hidden = (grad_residual + grad_back_one).astype(jnp.bfloat16)
    return (hidden_out, grad_hidden, (qkv_term, out_term, gate_up_term, down_term, gain_one_term, gain_two_term))

def reference(hidden_in, segments, cotangent, qkv_weight, out_weight, gate_up_weight, down_weight, attn_gain, ffn_gain):
    gain_one = attn_gain.astype(jnp.float32)
    gain_two = ffn_gain.astype(jnp.float32)

    def per_sequence(carry, item):
        hidden_row, seg_row, cot_row = item
        hidden_out, grad_hidden, terms = sequence_layer(hidden_row, seg_row, cot_row, qkv_weight, out_weight, gate_up_weight, down_weight, gain_one, gain_two)
        carry = tuple((total + term for total, term in zip(carry, terms)))
        return (carry, (hidden_out, grad_hidden))
    zeros = (jnp.zeros(qkv_weight.shape, jnp.float32), jnp.zeros(out_weight.shape, jnp.float32), jnp.zeros(gate_up_weight.shape, jnp.float32), jnp.zeros(down_weight.shape, jnp.float32), jnp.zeros(attn_gain.shape, jnp.float32), jnp.zeros(ffn_gain.shape, jnp.float32))
    sums, (hidden_out, grad_hidden) = lax.scan(per_sequence, zeros, (hidden_in, segments, cotangent))
    return (hidden_out, grad_hidden, sums[0], sums[1], sums[2], sums[3], sums[4], sums[5])
```

```python
import math

import jax
import jax.numpy as jnp
from jax import lax
from jax.experimental import pallas as pl
from jax.experimental.pallas import tpu as pltpu
from jax.sharding import PartitionSpec as P

HEADS = 32
KV_HEADS = 4
HEAD_DIM = 64
REACH = 1024
EPS = 1e-05
F32 = jnp.float32
BF16 = jnp.bfloat16
LANES = 128
SCALE = HEAD_DIM**-0.5


def dot(a, b, dims=((1,), (0,))):
    return lax.dot_general(a, b, (dims, ((), ())), preferred_element_type=F32)


def after(value, *others):
    return lax.optimization_barrier((value, *others))[0]


def pick(flag, one, other):
    return jnp.where(flag == 0, one, other)


class Ring:
    def __init__(self, size):
        self.size = size
        self.chips = size // 2
        rows = self.chips // 2
        self.order = [2 * i for i in range(rows)] + [2 * i + 1 for i in reversed(range(rows))]
        self.place = {chip: at for at, chip in enumerate(self.order)}
        self.half = self.chips // 2

        def turned(step):
            return [
                (s, self.order[(self.place[s // 2] + step) % self.chips] * 2 + s % 2)
                for s in range(size)
            ]

        self.ahead = turned(1)
        self.back = turned(-1)
        self.sibling = [(s, s ^ 1) for s in range(size)]
        self.core_groups = [list(range(core, size, 2)) for core in range(2)]
        self.index = lax.axis_index("shard")
        self.core = self.index % 2
        self.at = jnp.asarray([self.place[i] for i in range(self.chips)], jnp.int32)[
            self.index // 2
        ]

    def swap(self, value):
        return lax.ppermute(value, "shard", self.sibling)

    def gather(self, block):
        n, h = self.chips, block.shape[0] // 2
        found = [None] * n
        found[0] = cw = ccw = block
        for k in range(1, self.half):
            cw = lax.ppermute(cw, "shard", self.ahead)
            found[n - k] = cw
            ccw = lax.ppermute(ccw, "shard", self.back)
            found[k] = ccw
        top = lax.ppermute(cw[:h], "shard", self.ahead)
        low = lax.ppermute(ccw[h:], "shard", self.back)
        found[self.half] = jnp.concatenate([top, low], 0)
        return found

    def gather_both(self, block):
        own = self.gather(block)
        return own, [self.swap(b) for b in own]

    def scatter(self, parts):
        n, m = self.chips, self.half
        h = parts[0].shape[0] // 2
        cw = lax.ppermute(parts[m][:h].astype(BF16), "shard", self.ahead).astype(F32)
        ccw = lax.ppermute(parts[m][h:].astype(BF16), "shard", self.back).astype(F32)
        for k in range(m - 1, 0, -1):
            ahead, back = parts[k].astype(F32), parts[n - k].astype(F32)
            if k == m - 1:
                ahead = jnp.concatenate([ahead[:h] + cw, ahead[h:]], 0)
                back = jnp.concatenate([back[:h], back[h:] + ccw], 0)
            else:
                ahead, back = ahead + cw, back + ccw
            cw = lax.ppermute(ahead.astype(BF16), "shard", self.ahead).astype(F32)
            ccw = lax.ppermute(back.astype(BF16), "shard", self.back).astype(F32)
        return parts[0].astype(F32) + cw + ccw

    def split_cores(self, value, axis):
        shape = value.shape
        width = shape[axis] // self.size
        cut = value.reshape(shape[:axis] + (self.chips, 2, width) + shape[axis + 1 :])
        zero = lax.index_in_dim(cut, 0, axis + 1, False)
        one = lax.index_in_dim(cut, 1, axis + 1, False)
        flat = shape[:axis] + (self.chips * width,) + shape[axis + 1 :]
        return (
            pick(self.core, zero, one).reshape(flat),
            pick(self.core, one, zero).reshape(flat),
        )

    def join_cores(self, own, other, axis):
        shape = own.shape
        width = shape[axis] // self.chips
        cut = shape[:axis] + (self.chips, width) + shape[axis + 1 :]
        own, other = own.reshape(cut), other.reshape(cut)
        joined = jnp.stack([pick(self.core, own, other), pick(self.core, other, own)], axis + 1)
        return joined.reshape(shape[:axis] + (2 * shape[axis],) + shape[axis + 1 :])

    def to_ring(self, value, axis):
        width = value.shape[axis] // self.chips
        pieces = [
            lax.slice_in_dim(value, i * width, (i + 1) * width, axis=axis) for i in self.order
        ]
        double = jnp.concatenate(pieces + pieces[:-1], axis)
        return lax.dynamic_slice_in_dim(double, self.at * width, self.chips * width, axis)

    def from_ring(self, value, axis):
        width = value.shape[axis] // self.chips
        double = jnp.concatenate([value, value], axis)
        start = (self.chips - self.at) * width
        turned = lax.dynamic_slice_in_dim(double, start, self.chips * width, axis)
        pieces = [
            lax.slice_in_dim(turned, self.place[i] * width, (self.place[i] + 1) * width, axis=axis)
            for i in range(self.chips)
        ]
        return jnp.concatenate(pieces, axis)


def lane_low(shape):
    return lax.broadcasted_iota(jnp.int32, shape, len(shape) - 1) % LANES < HEAD_DIM


def rotated(values):
    quarter = HEAD_DIM // 2
    first = lax.broadcasted_iota(jnp.int32, values.shape, 1) % HEAD_DIM < quarter
    return jnp.where(
        first, -pltpu.roll(values, LANES - quarter, 1), pltpu.roll(values, quarter, 1)
    )


def kv_prepare_kernel(proj_ref, cos_ref, sin_ref, out_ref):
    for pair in range(KV_HEADS // 2):
        keys = proj_ref[:, pair * LANES : (pair + 1) * LANES]
        keys = keys * cos_ref[...] + rotated(keys) * sin_ref[...]
        at = KV_HEADS // 2 + pair
        values = proj_ref[:, at * LANES : (at + 1) * LANES]
        low = lane_low(keys.shape)
        one = jnp.where(low, keys, pltpu.roll(values, HEAD_DIM, 1))
        two = jnp.where(low, pltpu.roll(keys, HEAD_DIM, 1), values)
        out_ref[:, 2 * pair * LANES : (2 * pair + 1) * LANES] = one.astype(BF16)
        out_ref[:, (2 * pair + 1) * LANES : (2 * pair + 2) * LANES] = two.astype(BF16)


def kv_finish_kernel(grad_ref, cos_ref, sin_ref, out_ref):
    for pair in range(KV_HEADS // 2):
        one = grad_ref[:, 2 * pair * LANES : (2 * pair + 1) * LANES]
        two = grad_ref[:, (2 * pair + 1) * LANES : (2 * pair + 2) * LANES]
        low = lane_low(one.shape)
        keys = jnp.where(low, one, pltpu.roll(two, HEAD_DIM, 1))
        values = jnp.where(low, pltpu.roll(one, HEAD_DIM, 1), two)
        keys = keys * cos_ref[...] - rotated(keys) * sin_ref[...]
        at = KV_HEADS // 2 + pair
        out_ref[:, pair * LANES : (pair + 1) * LANES] = keys.astype(BF16)
        out_ref[:, at * LANES : (at + 1) * LANES] = values.astype(BF16)


def load_window(places_ref, kv_ref, window, rows):
    for b in range(window.shape[0] // rows):
        window[b * rows : (b + 1) * rows, :] = kv_ref[places_ref[b]]


def allowed_pairs(first_ref, reach, keys, rows):
    key = lax.broadcasted_iota(jnp.int32, (keys, rows), 0)
    token = lax.broadcasted_iota(jnp.int32, (keys, rows), 1)
    allowed = (key >= first_ref[...]) & (key <= token + reach)
    return jnp.concatenate([allowed, allowed], 1)


def stacked(block, low_side):
    turned = pltpu.roll(block, HEAD_DIM, 1)
    low = lane_low(block.shape)
    if low_side:
        one, two = jnp.where(low, block, 0.0), jnp.where(low, turned, 0.0)
    else:
        one, two = jnp.where(low, 0.0, turned), jnp.where(low, 0.0, block)
    return jnp.concatenate([one, two], 0).astype(BF16)


def attend_kernel(
    places_ref, proj_ref, kv_ref, first_ref, cos_ref, sin_ref, q_ref, out_ref, log_ref, window
):
    rows = proj_ref.shape[0]
    keys = window.shape[0]

    @pl.when(pl.program_id(1) == 0)
    def _():
        load_window(places_ref, kv_ref, window, rows)

    block = proj_ref[...]
    block = block * cos_ref[...] + rotated(block) * sin_ref[...]
    q_ref[...] = block.astype(BF16)
    queries = stacked(block, True)
    score = dot(window[...], queries, ((1,), (1,))) * SCALE
    allowed = allowed_pairs(first_ref, keys - rows, keys, rows)
    score = jnp.where(allowed, score, -jnp.inf)
    top = jnp.max(score, 0, keepdims=True)
    expon = jnp.exp(score - top)
    total = jnp.sum(expon, 0, keepdims=True)
    log_ref[0] = top + jnp.log(total)
    probs = (expon * (1.0 / total)).astype(BF16)
    out = dot(probs, window[...], ((0,), (0,)))
    one, two = out[:rows], out[rows:]
    out_ref[...] = jnp.where(lane_low(one.shape), pltpu.roll(one, HEAD_DIM, 1), two).astype(BF16)


def attend_back_kernel(
    places_ref,
    q_ref,
    grad_ref,
    att_ref,
    log_ref,
    kv_ref,
    first_ref,
    cos_ref,
    sin_ref,
    gq_ref,
    gkv_ref,
    window,
    total,
):
    rows = q_ref.shape[0]
    keys = window.shape[0]
    step = pl.program_id(1)

    @pl.when(step == 0)
    def _():
        load_window(places_ref, kv_ref, window, rows)
        total[...] = jnp.zeros_like(total)

    grad = grad_ref[...].astype(F32)
    queries = stacked(q_ref[...].astype(F32), True)
    grads = stacked(grad, False)
    product = jnp.transpose(grad * att_ref[...].astype(F32))
    delta = jnp.concatenate(
        [
            jnp.sum(product[:HEAD_DIM], 0, keepdims=True),
            jnp.sum(product[HEAD_DIM:], 0, keepdims=True),
        ],
        1,
    )
    score = dot(window[...], queries, ((1,), (1,))) * SCALE
    allowed = allowed_pairs(first_ref, keys - rows, keys, rows)
    probs = jnp.where(allowed, jnp.exp(score - log_ref[0]), 0.0)
    grad_probs = dot(window[...], grads, ((1,), (1,)))
    grad_scores = (probs * (grad_probs - delta) * SCALE).astype(BF16)
    total[...] += dot(grad_scores, queries) + dot(probs.astype(BF16), grads)
    grad_queries = dot(grad_scores, window[...], ((0,), (0,)))
    one, two = grad_queries[:rows], grad_queries[rows:]
    block = jnp.where(lane_low(one.shape), one, pltpu.roll(two, HEAD_DIM, 1))
    gq_ref[...] = (block * cos_ref[...] - rotated(block) * sin_ref[...]).astype(BF16)

    @pl.when(step == pl.num_programs(1) - 1)
    def _():
        gkv_ref[...] = jnp.zeros_like(gkv_ref)
        for b in range(keys // rows):
            gkv_ref[places_ref[b]] = total[b * rows : (b + 1) * rows, :]


def whole(shape):
    return pl.BlockSpec(shape, lambda *_: (0,) * len(shape))


def small_kernel(kernel, width, dtype, *args):
    rows = args[0].shape[0]
    return pl.pallas_call(kernel, out_shape=jax.ShapeDtypeStruct((rows, width), dtype))(*args)


def attend(places, proj, kv, first, cosine, sine):
    rows = proj.shape[0]
    keys = places.shape[0] * rows
    inner = HEADS // KV_HEADS // 2
    pairs = HEADS // 2
    pair_spec = pl.BlockSpec((rows, LANES), lambda g, i, _: (0, g * inner + i))
    return pl.pallas_call(
        attend_kernel,
        grid_spec=pltpu.PrefetchScalarGridSpec(
            num_scalar_prefetch=1,
            grid=(KV_HEADS, inner),
            in_specs=[
                pair_spec,
                pl.BlockSpec((kv.shape[0], rows, LANES), lambda g, i, _: (0, 0, g)),
                whole((1, rows)),
                whole((rows, LANES)),
                whole((rows, LANES)),
            ],
            out_specs=[
                pair_spec,
                pair_spec,
                pl.BlockSpec((1, 1, 2 * rows), lambda g, i, _: (g * inner + i, 0, 0)),
            ],
            scratch_shapes=[pltpu.VMEM((keys, LANES), BF16)],
        ),
        out_shape=[
            jax.ShapeDtypeStruct((rows, pairs * LANES), BF16),
            jax.ShapeDtypeStruct((rows, pairs * LANES), BF16),
            jax.ShapeDtypeStruct((pairs, 1, 2 * rows), F32),
        ],
        compiler_params=pltpu.CompilerParams(vmem_limit_bytes=32 * 1024 * 1024),
    )(places, proj, kv, first, cosine, sine)


def attend_back(places, queries, grad, attended, logs, kv, first, cosine, sine):
    rows = queries.shape[0]
    keys = places.shape[0] * rows
    inner = HEADS // KV_HEADS // 2
    pair_spec = pl.BlockSpec((rows, LANES), lambda g, i, _: (0, g * inner + i))
    kv_spec = pl.BlockSpec((kv.shape[0], rows, LANES), lambda g, i, _: (0, 0, g))
    return pl.pallas_call(
        attend_back_kernel,
        grid_spec=pltpu.PrefetchScalarGridSpec(
            num_scalar_prefetch=1,
            grid=(KV_HEADS, inner),
            in_specs=[
                pair_spec,
                pair_spec,
                pair_spec,
                pl.BlockSpec((1, 1, 2 * rows), lambda g, i, _: (g * inner + i, 0, 0)),
                kv_spec,
                whole((1, rows)),
                whole((rows, LANES)),
                whole((rows, LANES)),
            ],
            out_specs=[pair_spec, kv_spec],
            scratch_shapes=[pltpu.VMEM((keys, LANES), BF16), pltpu.VMEM((keys, LANES), F32)],
        ),
        out_shape=[
            jax.ShapeDtypeStruct(queries.shape, BF16),
            jax.ShapeDtypeStruct(kv.shape, F32),
        ],
        compiler_params=pltpu.CompilerParams(vmem_limit_bytes=40 * 1024 * 1024),
    )(places, queries, grad, attended, logs, kv, first, cosine, sine)


def rms_forward(values, gain):
    factor = lax.rsqrt(jnp.mean(values * values, -1, keepdims=True) + EPS)
    normed = values * factor
    return factor, normed, (normed * gain).astype(BF16)


def rms_backward(grad_normed, factor, normed, gain):
    gain_grad = jnp.sum(grad_normed * normed, 0)
    scaled = grad_normed * gain
    return gain_grad, factor * (scaled - normed * jnp.mean(scaled * normed, -1, keepdims=True))


def on_device(
    reps,
    shards,
    hidden_in,
    segments,
    cotangent,
    qkv_weight,
    out_weight,
    gate_up_weight,
    down_weight,
    attn_gain,
    ffn_gain,
):
    ring = Ring(shards)
    chips = ring.chips
    twin_map = [(i, i ^ 1) for i in range(reps)]
    side = lax.axis_index("rep") % 2
    side_groups = [list(range(s, reps, 2)) for s in range(2)]

    def twin(value):
        return lax.ppermute(value, "rep", twin_map)

    def rest_of_reps(value):
        if reps == 2:
            return value
        return lax.psum(value, "rep", axis_index_groups=side_groups)

    def over_reps(value):
        mine = rest_of_reps(value).astype(BF16)
        return mine.astype(F32) + twin(mine).astype(F32)

    tok = hidden_in.shape[1]
    model = hidden_in.shape[2]
    rows = model // shards
    seg_row = segments[0]
    length = seg_row.shape[0]
    qsize = HEADS * HEAD_DIM
    ff = down_weight.shape[0] * shards
    wide = ff // chips

    gains = lax.all_gather(jnp.stack([attn_gain, ffn_gain]), "shard", axis=1, tiled=True)
    gain_one = gains[0].astype(F32)
    gain_two = gains[1].astype(F32)
    qkv_own, qkv_sib = ring.gather_both(qkv_weight)

    offset = ring.index * tok
    local_seg = lax.dynamic_slice_in_dim(seg_row, offset, tok)
    starts = jnp.sum((seg_row[None, :] < local_seg[:, None]).astype(jnp.int32), 1)
    positions = offset + jnp.arange(tok, dtype=jnp.int32) - starts
    freqs = jnp.exp(
        (jnp.arange(LANES) % (HEAD_DIM // 2)).astype(F32) * (-2.0 * math.log(10000.0) / HEAD_DIM)
    )
    angles = positions.astype(F32)[:, None] * freqs[None, :]
    cosine, sine = jnp.cos(angles), jnp.sin(angles)
    blocks = min(REACH // tok, shards - 1) + 1
    first = (starts - offset + (blocks - 1) * tok)[None, :]
    device = (ring.index + jnp.arange(1 - blocks, 1)) % shards
    place_of = jnp.asarray([ring.place[i] for i in range(chips)], jnp.int32)
    places = (
        jnp.abs(device % 2 - ring.core) * chips + (place_of[device // 2] - ring.at) % chips
    ).astype(jnp.int32)

    hidden32 = hidden_in[0].astype(F32)
    factor_one, normed_one, input_one = rms_forward(hidden32, gain_one)
    in_own, in_sib = (ring.to_ring(v, 1) for v in ring.split_cores(input_one, 1))

    def by_blocks(own, sib, own_blocks, sib_blocks):
        total = None
        for k in sorted(range(chips), key=lambda k: min(k, chips - k)):
            for value, weights in ((own, own_blocks), (sib, sib_blocks)):
                term = dot(value[:, k * rows : (k + 1) * rows], weights[k])
                total = term if total is None else total + term
        return total

    projections = by_blocks(in_own, in_sib, qkv_own, qkv_sib)
    kv_local = small_kernel(
        kv_prepare_kernel, KV_HEADS * LANES, BF16, projections[:, qsize:], cosine, sine
    )
    kv_own, kv_sib = ring.gather_both(kv_local)
    kv = jnp.stack(kv_own + kv_sib)
    out_own, out_sib = ring.gather_both(after(out_weight, qkv_own[ring.half]))
    queries, attended, logs = attend(places, projections[:, :qsize], kv, first, cosine, sine)
    att_own, att_sib = (ring.to_ring(v, 1) for v in ring.split_cores(attended, 1))
    residual = hidden32 + by_blocks(att_own, att_sib, out_own, out_sib)
    factor_two, normed_two, input_two = rms_forward(residual, gain_two)

    half = rows // 2
    mine = lax.dynamic_slice_in_dim(
        after(gate_up_weight, out_own[ring.half]), side * half, half, 0
    )
    mine = mine.reshape(half, 2, chips, wide).transpose(2, 1, 0, 3)
    mine = lax.all_to_all(mine, "shard", 0, 0, axis_index_groups=ring.core_groups, tiled=True)
    theirs = twin(mine)
    gu_own = jnp.concatenate([pick(side, mine, theirs), pick(side, theirs, mine)], 2)
    gu_own = gu_own.transpose(1, 0, 2, 3).reshape(2, chips * rows, wide)
    gu_sib = ring.swap(gu_own)
    gate_up = jnp.concatenate([gu_own, gu_sib], 1)
    down_sib = ring.swap(down_weight)
    down = jnp.concatenate(
        [pick(ring.core, down_weight, down_sib), pick(ring.core, down_sib, down_weight)], 0
    )

    cot = jnp.concatenate(ring.gather(after(cotangent[0], out_own[ring.half])), 0)
    two = jnp.concatenate(ring.gather(jnp.concatenate(ring.split_cores(input_two, 1), 1)), 0)
    gate = dot(two, gate_up[0])
    upward = dot(two, gate_up[1])
    sigma = jax.nn.sigmoid(gate)
    activation = (gate * sigma * upward).astype(BF16)
    grad_activation = dot(cot, down, ((1,), (1,)))
    grad_gate = (grad_activation * upward * (sigma * (1.0 + gate * (1.0 - sigma)))).astype(BF16)
    grad_up = (grad_activation * gate * sigma).astype(BF16)
    grad_two = dot(grad_gate, gate_up[0], ((1,), (1,))) + dot(grad_up, gate_up[1], ((1,), (1,)))

    def cut(value):
        return [value[k * tok : (k + 1) * tok] for k in range(chips)]

    grad_two = ring.scatter(cut(grad_two))
    grad_input_two = ring.join_cores(grad_two[:, : model // 2], grad_two[:, model // 2 :], 1)
    ffn_out = ring.scatter(cut(after(dot(activation, down), grad_two)))
    hidden_out = (residual + ffn_out).astype(BF16)
    gain_two_term, grad_back_two = rms_backward(grad_input_two, factor_two, normed_two, gain_two)
    grad_residual = cotangent[0].astype(F32) + grad_back_two
    residual_half = grad_residual.astype(BF16)

    down_term = dot(activation, cot, ((0,), (0,)))
    down_rows = down_weight.shape[0]
    keep = pick(ring.core, down_term[:down_rows], down_term[down_rows:])
    give = pick(ring.core, down_term[down_rows:], down_term[:down_rows]).astype(BF16)
    grad_down = over_reps(keep + ring.swap(give).astype(F32))
    gu_term = jnp.stack([dot(two, grad_gate, ((0,), (0,))), dot(two, grad_up, ((0,), (0,)))])
    middle = chips * rows
    gu_term = gu_term[:, :middle] + ring.swap(gu_term[:, middle:].astype(BF16)).astype(F32)
    gu_term = gu_term.reshape(2, chips, rows, wide)
    keep = pick(side, gu_term[:, :, :half], gu_term[:, :, half:])
    give = pick(side, gu_term[:, :, half:], gu_term[:, :, :half]).astype(BF16)
    keep = rest_of_reps(keep + twin(give).astype(F32)).astype(BF16)
    keep = lax.all_to_all(
        keep.transpose(1, 0, 2, 3), "shard", 0, 0, axis_index_groups=ring.core_groups, tiled=True
    )
    keep = keep.transpose(2, 1, 0, 3).reshape(half, 2 * ff)
    give = twin(keep)
    grad_gate_up = jnp.concatenate([pick(side, keep, give), pick(side, give, keep)], 0)
    grad_gate_up = grad_gate_up.astype(F32)

    def token_terms(inputs, grads, gain_term):
        own, sib = (ring.to_ring(v, 1) for v in ring.split_cores(inputs, 1))
        gain_own, gain_sib = (ring.to_ring(v, 0) for v in ring.split_cores(gain_term, 0))

        def with_gain(term, gain):
            extra = jnp.concatenate([gain[:, None], jnp.zeros((gain.shape[0], LANES - 1), F32)], 1)
            return jnp.concatenate([term, extra], 1)

        give = with_gain(dot(sib, grads, ((0,), (0,))), gain_sib).astype(BF16)
        keep = with_gain(dot(own, grads, ((0,), (0,))), gain_own) + ring.swap(give).astype(F32)
        parts = [keep[k * rows : (k + 1) * rows] for k in range(chips)]
        total = over_reps(ring.scatter(parts))
        return total[:, :-LANES], total[:, -LANES]

    out_all = jnp.concatenate(out_own + out_sib, 0)
    grad_att = dot(residual_half, out_all, ((1,), (1,)))
    grad_attended = ring.join_cores(
        ring.from_ring(grad_att[:, : qsize // 2], 1),
        ring.from_ring(grad_att[:, qsize // 2 :], 1),
        1,
    ).astype(BF16)
    grad_out, grad_ffn_gain = token_terms(attended, residual_half, gain_two_term)
    grad_queries, grad_kv = attend_back(
        places, queries, grad_attended, attended, logs, kv, first, cosine, sine
    )
    grad_kv = grad_kv[:chips] + ring.swap(grad_kv[chips:].astype(BF16)).astype(F32)
    grad_kv = ring.scatter([grad_kv[k] for k in range(chips)])
    grad_kv = small_kernel(
        kv_finish_kernel, 2 * KV_HEADS * HEAD_DIM, BF16, grad_kv, cosine, sine
    )
    grad_projections = jnp.concatenate([grad_queries, grad_kv], 1)
    qkv_all = jnp.concatenate(qkv_own + qkv_sib, 0)
    grad_one = dot(grad_projections, qkv_all, ((1,), (1,)))
    grad_input_one = ring.join_cores(
        ring.from_ring(grad_one[:, : model // 2], 1),
        ring.from_ring(grad_one[:, model // 2 :], 1),
        1,
    )
    gain_one_term, grad_back_one = rms_backward(grad_input_one, factor_one, normed_one, gain_one)
    grad_hidden = (grad_residual + grad_back_one).astype(BF16)
    grad_qkv, grad_attn_gain = token_terms(input_one, grad_projections, gain_one_term)
    return (
        hidden_out[None],
        grad_hidden[None],
        grad_qkv,
        grad_out,
        grad_gate_up,
        grad_down,
        grad_attn_gain,
        grad_ffn_gain,
    )


def solution(mesh):
    reps, shards = mesh.shape["rep"], mesh.shape["shard"]

    def layer(*args):
        return on_device(reps, shards, *args)

    return jax.shard_map(
        layer,
        mesh=mesh,
        in_specs=(
            P("rep", "shard", None),
            P("rep", None),
            P("rep", "shard", None),
            P("shard", None),
            P("shard", None),
            P("shard", None),
            P("shard", None),
            P("shard"),
            P("shard"),
        ),
        out_specs=(
            P("rep", "shard", None),
            P("rep", "shard", None),
            P("shard", None),
            P("shard", None),
            P("shard", None),
            P("shard", None),
            P("shard"),
            P("shard"),
        ),
        check_vma=False,
    )
```

```python
import math

import jax
import jax.numpy as jnp
import numpy as np
from jax import lax
from jax.experimental import pallas as pl
from jax.experimental.pallas import tpu as pltpu
from jax.sharding import PartitionSpec as P

HEADS = 32
KV_HEADS = 4
HEAD_DIM = 64
REACH = 1024
EPS = 1e-05
F32 = jnp.float32
BF16 = jnp.bfloat16
LANES = 128
SCALE = HEAD_DIM**-0.5
LIMIT = 58 * 1024 * 1024
ROOMY = pltpu.CompilerParams(vmem_limit_bytes=LIMIT)
HELD = pl.BlockSpec(memory_space=pl.ANY)


def dot(a, b, dims=((1,), (0,))):
    return lax.dot_general(a, b, (dims, ((), ())), preferred_element_type=F32)


LAST = ((1,), (1,))
FIRST = ((0,), (0,))


def pick(flag, one, other):
    return jnp.where(flag == 0, one, other)


class Ring:
    def __init__(self, size, window):
        self.size = size
        self.chips = chips = size // 2
        rows = chips // 2
        self.order = [2 * i for i in range(rows)] + [2 * i + 1 for i in reversed(range(rows))]
        self.place = [self.order.index(chip) for chip in range(chips)]
        self.half = chips // 2

        def turned(step):
            return [
                (s, self.order[(self.place[s // 2] + step) % chips] * 2 + s % 2)
                for s in range(size)
            ]

        self.ahead = turned(1)
        self.back = turned(-1)
        self.sibling = [(s, s ^ 1) for s in range(size)]
        self.core_groups = [list(range(core, size, 2)) for core in range(2)]
        self.near, self.place_near, self.cores, self.place_cores, self.window = (
            k * size for k in range(5)
        )
        self.core_at = self.window + window
        self.side_at = self.core_at + 1
        table = []
        for side in range(2):
            for s in range(size):
                chip, core = s // 2, s % 2
                at = self.place[chip]
                near = [
                    self.order[(at + j) % chips] * 2 + (core ^ other)
                    for other in range(2)
                    for j in range(chips)
                ]
                cores = [j * 2 + (core ^ other) for other in range(2) for j in range(chips)]
                place_near = [near.index(d) for d in range(size)]
                place_cores = [cores.index(d) for d in range(size)]
                seen = [place_near[(s + 1 - window + b) % size] for b in range(window)]
                table.append(near + place_near + cores + place_cores + seen + [core, side])
        self.index = lax.axis_index("shard")
        self.side = lax.axis_index("rep") % 2
        self.table = lax.dynamic_index_in_dim(
            jnp.asarray(np.array(table, np.int32)), self.side * size + self.index, 0, False
        )

    def swap(self, value):
        return lax.ppermute(value, "shard", self.sibling)

    def gather(self, block, ties=None):
        n, h = self.chips, block.shape[0] // 2
        cw = ccw = block
        found = [(0, 0, block)]
        for k in range(1, self.half):
            if ties and k in ties:
                cw, ccw = after(cw, *ties[k]), after(ccw, *ties[k])
            cw = lax.ppermute(cw, "shard", self.ahead)
            ccw = lax.ppermute(ccw, "shard", self.back)
            found += [(n - k, 0, cw), (k, 0, ccw)]
        top = lax.ppermute(cw[:h], "shard", self.ahead)
        low = lax.ppermute(ccw[h:], "shard", self.back)
        return found + [(self.half, 0, top), (self.half, h, low)]

    def gather_both(self, block):
        own = self.gather(block)
        other = [(k + self.chips, row, self.swap(piece)) for k, row, piece in own]
        return own + other, [piece for _, _, piece in own]

    def scatter(self, parts, ties=None):
        n, m = self.chips, self.half
        h = parts[0].shape[0] // 2
        cw, ccw = parts[m][:h].astype(BF16), parts[m][h:].astype(BF16)
        marks = []
        for k in range(m - 1, -1, -1):
            if ties:
                others = ties(m - k, marks)
                if others:
                    cw, ccw = after(cw, *others), after(ccw, *others)
            cw = lax.ppermute(cw, "shard", self.ahead)
            ccw = lax.ppermute(ccw, "shard", self.back)
            marks.append((cw, ccw))
            if k == 0:
                return parts[0].astype(F32) + cw.astype(F32) + ccw.astype(F32), marks
            ahead, back = parts[k].astype(F32), parts[n - k].astype(F32)
            if k == m - 1:
                ahead = jnp.concatenate([ahead[:h] + cw.astype(F32), ahead[h:]], 0)
                back = jnp.concatenate([back[:h], back[h:] + ccw.astype(F32)], 0)
            else:
                ahead, back = ahead + cw.astype(F32), back + ccw.astype(F32)
            cw, ccw = ahead.astype(BF16), back.astype(BF16)


def whole(shape):
    return pl.BlockSpec(shape, lambda *_: (0,) * len(shape))


def shaped(shape, kind):
    return jax.ShapeDtypeStruct(shape, kind)


def call(kernel, table, ins, outs, pieces=(), scratch=(), others=()):
    count, more, extra = len(ins), len(pieces), len(others)

    def body(table_ref, *refs):
        behind = count + more + extra
        kernel(
            table_ref,
            refs[:count],
            refs[count : count + more],
            refs[behind : behind + len(outs)],
            refs[behind + len(outs) :],
        )

    return pl.pallas_call(
        body,
        grid_spec=pltpu.PrefetchScalarGridSpec(
            num_scalar_prefetch=1,
            grid=(1,),
            in_specs=[whole(v.shape) for v in ins] + [HELD] * (more + extra),
            out_specs=[whole(v.shape) for v in outs],
            scratch_shapes=list(scratch),
        ),
        out_shape=list(outs),
        compiler_params=ROOMY,
    )(table, *ins, *pieces, *others)


def after(value, *others):
    return pl.pallas_call(
        lambda *refs: None,
        in_specs=[HELD] * (1 + len(others)),
        out_specs=HELD,
        out_shape=shaped(value.shape, value.dtype),
        input_output_aliases={0: 0},
    )(value, *others)


def fetches(pieces, refs, buffer, sems):
    return [
        pltpu.make_async_copy(
            ref, buffer.at[k, pl.ds(row, ref.shape[0])], sems.at[n]
        )
        for n, ((k, row, _), ref) in enumerate(zip(pieces, refs))
    ]


def block_at(place):
    return pl.ds(pl.multiple_of(place * LANES, LANES), LANES)


def columns(block):
    return slice(block * LANES, (block + 1) * LANES)


def lane_low(shape):
    return lax.broadcasted_iota(jnp.int32, shape, len(shape) - 1) % LANES < HEAD_DIM


def rotated(values):
    quarter = HEAD_DIM // 2
    first = lax.broadcasted_iota(jnp.int32, values.shape, 1) % HEAD_DIM < quarter
    return jnp.where(
        first, -pltpu.roll(values, LANES - quarter, 1), pltpu.roll(values, quarter, 1)
    )


def pack_weight(weight, gain_one, gain_two, table):
    def kernel(_, ins, pieces, outs, scratch):
        weight_ref, one_ref, two_ref = ins
        width = weight_ref.shape[1]
        outs[0][:, :width] = weight_ref[...]
        lane = lax.broadcasted_iota(jnp.int32, (weight_ref.shape[0], LANES), 1)
        block = jnp.where(lane == 0, one_ref[...], jnp.where(lane == 1, two_ref[...], 0.0))
        outs[0][:, width:] = block.astype(BF16)

    rows, width = weight.shape
    gains = [g.astype(F32)[:, None] for g in (gain_one, gain_two)]
    return call(kernel, table, [weight, *gains], [shaped((rows, width + LANES), BF16)])[0]


def project(ring, hidden, cosine, sine, pieces, width, others):
    size = ring.size
    rows, model = hidden.shape
    qsize = HEADS * HEAD_DIM
    step = 2 * LANES

    def kernel(table, ins, refs, outs, scratch):
        hidden_ref, cos_ref, sin_ref = ins
        q_ref, kv_ref, input_ref, factor_ref, gain_ref = outs
        buffer, sems = scratch
        copies = fetches(pieces, refs, buffer, sems)
        for copy in copies:
            copy.start()
        values = hidden_ref[...].astype(F32)
        factor = lax.rsqrt(jnp.mean(values * values, -1, keepdims=True) + EPS)
        factor_ref[...] = jnp.broadcast_to(factor, factor_ref.shape)
        for copy in copies:
            copy.wait()
        for k in range(size):
            gains = jnp.transpose(buffer[k, :, width : width + LANES].astype(F32))
            gain_ref[:, columns(k)] = gains[:8]
            part = hidden_ref[:, block_at(table[ring.near + k])].astype(F32)
            input_ref[:, columns(k)] = (part * factor * gains[:1]).astype(BF16)
        inputs = input_ref[...]
        for start in range(0, qsize, step):
            weights = buffer[:, :, start : start + step].reshape(model, step)
            q_ref[:, start : start + step] = dot(inputs, weights)
        weights = buffer[:, :, qsize:width].reshape(model, width - qsize)
        proj = dot(inputs, weights)
        for pair in range(KV_HEADS // 2):
            keys = proj[:, columns(pair)]
            keys = keys * cos_ref[...] + rotated(keys) * sin_ref[...]
            heads = proj[:, columns(KV_HEADS // 2 + pair)]
            low = lane_low(keys.shape)
            one = jnp.where(low, keys, pltpu.roll(heads, HEAD_DIM, 1))
            two = jnp.where(low, pltpu.roll(keys, HEAD_DIM, 1), heads)
            kv_ref[:, columns(2 * pair)] = one.astype(BF16)
            kv_ref[:, columns(2 * pair + 1)] = two.astype(BF16)

    return call(
        kernel,
        ring.table,
        [hidden, cosine, sine],
        [
            shaped((rows, qsize), F32),
            shaped((rows, KV_HEADS * LANES), BF16),
            shaped((rows, model), BF16),
            shaped((rows, LANES), F32),
            shaped((8, model), F32),
        ],
        [piece for _, _, piece in pieces],
        [
            pltpu.VMEM((size, rows, width + LANES), BF16),
            pltpu.SemaphoreType.DMA((len(pieces),)),
        ],
        others,
    )


def stack_blocks(ring, pieces, others):
    rows, width = pieces[0][2].shape

    def body(*refs):
        copies = fetches(pieces, refs[: len(pieces)], refs[-2], refs[-1])
        for copy in copies:
            copy.start()
        for copy in copies:
            copy.wait()

    return pl.pallas_call(
        body,
        in_specs=[HELD] * (len(pieces) + len(others)),
        out_specs=pl.BlockSpec(memory_space=pltpu.VMEM),
        out_shape=shaped((ring.chips, rows, width), pieces[0][2].dtype),
        scratch_shapes=[pltpu.SemaphoreType.DMA((len(pieces),))],
        compiler_params=ROOMY,
    )(*[piece for _, _, piece in pieces], *others)


def project_out(ring, attended, hidden, gains, pieces, others):
    size = ring.size
    rows, model = hidden.shape
    step = 2 * LANES

    def kernel(table, ins, refs, outs, scratch):
        att_ref, hidden_ref, gain_ref = ins
        residual_ref, factor_ref, input_ref = outs
        buffer, sems = scratch
        copies = fetches(pieces, refs, buffer, sems)
        for copy in copies:
            copy.start()
        for copy in copies:
            copy.wait()
        inputs = att_ref[...]
        squares = jnp.zeros((rows, 1), F32)
        for start in range(0, model, step):
            weights = buffer[:, :, start : start + step].reshape(model, step)
            part = hidden_ref[:, start : start + step].astype(F32) + dot(inputs, weights)
            residual_ref[:, start : start + step] = part
            squares += jnp.sum(part * part, -1, keepdims=True)
        factor = lax.rsqrt(squares * (1.0 / model) + EPS)
        factor_ref[...] = jnp.broadcast_to(factor, factor_ref.shape)
        for k in range(size):
            device = table[ring.cores + k]
            gain = gain_ref[1:2, block_at(table[ring.place_near + device])]
            part = residual_ref[:, block_at(device)] * factor
            input_ref[:, columns(k)] = (part * gain).astype(BF16)

    return call(
        kernel,
        ring.table,
        [attended, hidden, gains],
        [shaped((rows, model), F32), shaped((rows, LANES), F32), shaped((rows, model), BF16)],
        [piece for _, _, piece in pieces],
        [
            pltpu.VMEM((size, rows, model), BF16),
            pltpu.SemaphoreType.DMA((len(pieces),)),
        ],
        others,
    )


def back_out(ring, grad_two, residual, factor, gains, cot, pieces, others):
    size = ring.size
    rows, model = residual.shape

    def kernel(table, ins, refs, outs, scratch):
        grad_ref, residual_ref, factor_ref, gain_ref, cot_ref = ins
        grad_res_ref, half_ref, att_ref, term_ref = outs
        buffer, sems = scratch
        copies = fetches(pieces, refs, buffer, sems)
        for copy in copies:
            copy.start()
        factor = factor_ref[...]
        mean = jnp.zeros((rows, 1), F32)
        for d in range(size):
            place = block_at(table[ring.place_near + d])
            grad = grad_ref[:, block_at(table[ring.place_cores + d])]
            normed = residual_ref[:, columns(d)] * factor
            product = grad * normed
            term_ref[:, place] = jnp.broadcast_to(
                jnp.sum(product, 0, keepdims=True), (8, LANES)
            )
            mean += jnp.sum(product * gain_ref[1:2, place], -1, keepdims=True)
        mean *= 1.0 / model
        for d in range(size):
            place = block_at(table[ring.place_near + d])
            grad = grad_ref[:, block_at(table[ring.place_cores + d])] * gain_ref[1:2, place]
            normed = residual_ref[:, columns(d)] * factor
            total = cot_ref[:, columns(d)].astype(F32) + factor * (grad - normed * mean)
            grad_res_ref[:, columns(d)] = total
            half_ref[:, columns(d)] = total.astype(BF16)
        for copy in copies:
            copy.wait()
        halves = half_ref[...]
        for k in range(0, size, 2):
            weights = buffer[k : k + 2].reshape(2 * rows, model)
            att_ref[:, k * LANES : (k + 2) * LANES] = dot(halves, weights, LAST).astype(BF16)

    return call(
        kernel,
        ring.table,
        [grad_two, residual, factor, gains, cot],
        [
            shaped((rows, model), F32),
            shaped((rows, model), BF16),
            shaped((rows, model), BF16),
            shaped((8, model), F32),
        ],
        [piece for _, _, piece in pieces],
        [
            pltpu.VMEM((size, rows, model), BF16),
            pltpu.SemaphoreType.DMA((len(pieces),)),
        ],
        others,
    )


def finish_kv(ring, grad, cosine, sine, others):
    def kernel(table, ins, refs, outs, scratch):
        grad_ref, cos_ref, sin_ref = ins
        for pair in range(KV_HEADS // 2):
            one = grad_ref[:, columns(2 * pair)]
            two = grad_ref[:, columns(2 * pair + 1)]
            low = lane_low(one.shape)
            keys = jnp.where(low, one, pltpu.roll(two, HEAD_DIM, 1))
            values = jnp.where(low, pltpu.roll(one, HEAD_DIM, 1), two)
            keys = keys * cos_ref[...] - rotated(keys) * sin_ref[...]
            outs[0][:, columns(pair)] = keys.astype(BF16)
            outs[0][:, columns(KV_HEADS // 2 + pair)] = values.astype(BF16)

    rows = grad.shape[0]
    return call(
        kernel,
        ring.table,
        [grad, cosine, sine],
        [shaped((rows, 2 * KV_HEADS * HEAD_DIM), BF16)],
        others=others,
    )[0]


def back_project(
    ring, grad_queries, grad_kv, hidden, factor, gains, grad_residual, pieces, width, others
):
    size = ring.size
    rows, model = hidden.shape
    qsize = grad_queries.shape[1]

    def kernel(table, ins, refs, outs, scratch):
        gq_ref, gkv_ref, hidden_ref, factor_ref, gain_ref, grad_res_ref = ins
        grad_ref, term_ref = outs
        buffer, sems, total = scratch
        copies = fetches(pieces, refs, buffer, sems)
        for copy in copies:
            copy.start()
        for copy in copies:
            copy.wait()
        queries, keys = gq_ref[...], gkv_ref[...]
        for k in range(0, size, 2):
            weights = buffer[k : k + 2].reshape(2 * rows, width + LANES)
            total[:, k * LANES : (k + 2) * LANES] = dot(
                queries, weights[:, :qsize], LAST
            ) + dot(keys, weights[:, qsize:width], LAST)
        factor = factor_ref[...]
        mean = jnp.zeros((rows, 1), F32)
        for k in range(size):
            normed = hidden_ref[:, block_at(table[ring.near + k])].astype(F32) * factor
            product = total[:, columns(k)] * normed
            term_ref[:, columns(k)] = jnp.broadcast_to(
                jnp.sum(product, 0, keepdims=True), (8, LANES)
            )
            mean += jnp.sum(product * gain_ref[:1, columns(k)], -1, keepdims=True)
        mean *= 1.0 / model
        for k in range(size):
            place = block_at(table[ring.near + k])
            normed = hidden_ref[:, place].astype(F32) * factor
            scaled = total[:, columns(k)] * gain_ref[:1, columns(k)]
            back = grad_res_ref[:, place] + factor * (scaled - normed * mean)
            grad_ref[:, place] = back.astype(BF16)

    return call(
        kernel,
        ring.table,
        [grad_queries, grad_kv, hidden, factor, gains, grad_residual],
        [shaped((rows, model), BF16), shaped((8, model), F32)],
        [piece for _, _, piece in pieces],
        [
            pltpu.VMEM((size, rows, width + LANES), BF16),
            pltpu.SemaphoreType.DMA((len(pieces),)),
            pltpu.VMEM((rows, model), F32),
        ],
        others,
    )


def cut_columns(ring, weight, wide):
    rows = weight.shape[0]
    half = rows // 2

    def kernel(table, ins, refs, outs, scratch):
        upper = table[ring.side_at] == 0
        for chip in range(ring.chips):
            for part in range(2):
                start = (part * ring.chips + chip) * wide
                block = ins[0][:, start : start + wide].astype(F32)
                outs[0][chip, part] = jnp.where(upper, block[:half], block[half:]).astype(BF16)

    return call(
        kernel, ring.table, [weight], [shaped((ring.chips, 2, half, wide), BF16)]
    )[0]


def join_columns(ring, mine, theirs):
    chips, parts, half, wide = mine.shape

    def kernel(table, ins, refs, outs, scratch):
        flip = table[ring.side_at] == 0
        for chip in range(chips):
            for part in range(parts):
                start = (part * chips + chip) * wide
                one, two = ins[0][chip, part].astype(F32), ins[1][chip, part].astype(F32)
                outs[0][:half, start : start + wide] = jnp.where(flip, one, two)
                outs[0][half:, start : start + wide] = jnp.where(flip, two, one)

    return call(
        kernel,
        ring.table,
        [mine, theirs],
        [shaped((2 * half, parts * chips * wide), F32)],
    )[0]


def give_terms(ring, inputs, grads, others=()):
    tokens, model = inputs.shape
    chips, count, extra = ring.chips, len(grads), len(others)
    rows = model // ring.size

    def body(input_ref, *refs):
        for grad_ref, out_ref in zip(refs[:count], refs[count + extra :]):
            out_ref[...] = dot(input_ref[...], grad_ref[...], FIRST).astype(BF16)

    return pl.pallas_call(
        body,
        grid=(chips,),
        in_specs=[pl.BlockSpec((tokens, rows), lambda i: (0, chips + i))]
        + [whole(g.shape) for g in grads]
        + [HELD] * extra,
        out_specs=[pl.BlockSpec((rows, g.shape[1]), lambda i: (i, 0)) for g in grads],
        out_shape=[shaped((chips * rows, g.shape[1]), BF16) for g in grads],
        compiler_params=ROOMY,
    )(inputs, *grads, *others)


def keep_terms(ring, inputs, grads, gots):
    tokens, model = inputs.shape
    chips, count = ring.chips, len(grads)
    rows = model // ring.size

    def body(input_ref, *refs):
        for part in range(count):
            term = dot(input_ref[...], refs[part][...], FIRST)
            refs[2 * count + part][...] = (term + refs[count + part][...].astype(F32)).astype(BF16)

    blocks = [pl.BlockSpec((rows, g.shape[1]), lambda i: (i, 0)) for g in grads]
    return pl.pallas_call(
        body,
        grid=(chips,),
        in_specs=[pl.BlockSpec((tokens, rows), lambda i: (0, i))]
        + [whole(g.shape) for g in grads]
        + blocks,
        out_specs=blocks,
        out_shape=[shaped((chips * rows, g.shape[1]), BF16) for g in grads],
        compiler_params=ROOMY,
    )(inputs, *grads, *gots)


def halve_terms(ring, inputs, grads, gots):
    tokens, model = inputs.shape
    chips, count = ring.chips, len(grads)
    rows, wide = model // ring.size, grads[0].shape[1]
    half = rows // 2

    def body(table, input_ref, *refs):
        upper = table[ring.side_at] == 0
        keep_ref, give_ref = refs[2 * count :]
        for part in range(count):
            total = dot(input_ref[...], refs[part][...], FIRST)
            total += refs[count + part][...].astype(F32)
            keep_ref[0, part] = jnp.where(upper, total[:half], total[half:])
            give_ref[0, part] = jnp.where(upper, total[half:], total[:half]).astype(BF16)

    return pl.pallas_call(
        body,
        grid_spec=pltpu.PrefetchScalarGridSpec(
            num_scalar_prefetch=1,
            grid=(chips,),
            in_specs=[pl.BlockSpec((tokens, rows), lambda i, _: (0, i))]
            + [whole(g.shape) for g in grads]
            + [pl.BlockSpec((rows, wide), lambda i, _: (i, 0))] * count,
            out_specs=[pl.BlockSpec((1, count, half, wide), lambda i, _: (i, 0, 0, 0))] * 2,
        ),
        out_shape=[shaped((chips, count, half, wide), kind) for kind in (F32, BF16)],
        compiler_params=ROOMY,
    )(ring.table, inputs, *grads, *gots)


def down_terms(ring, activation, cot, others):
    tokens, wide = activation.shape
    model = cot.shape[1]
    step, half = 2 * LANES, wide // 2

    def body(table, act_ref, cot_ref, *refs):
        keep_ref, give_ref = refs[len(others) :]
        total = dot(act_ref[...], cot_ref[...], FIRST)
        first = table[ring.core_at] == 0
        keep_ref[...] = jnp.where(first, total[:half], total[half:])
        give_ref[...] = jnp.where(first, total[half:], total[:half]).astype(BF16)

    return pl.pallas_call(
        body,
        grid_spec=pltpu.PrefetchScalarGridSpec(
            num_scalar_prefetch=1,
            grid=(model // step,),
            in_specs=[whole(activation.shape), pl.BlockSpec((tokens, step), lambda i, _: (0, i))]
            + [HELD] * len(others),
            out_specs=[pl.BlockSpec((half, step), lambda i, _: (0, i))] * 2,
        ),
        out_shape=[shaped((half, model), kind) for kind in (F32, BF16)],
        compiler_params=ROOMY,
    )(ring.table, activation, cot, *others)


def down_project(activation, down, others):
    tokens, wide = activation.shape
    model = down.shape[1]
    step = 2 * LANES

    def body(act_ref, down_ref, *refs):
        refs[-1][...] = dot(act_ref[...], down_ref[...]).astype(BF16)

    return pl.pallas_call(
        body,
        grid=(tokens // step,),
        in_specs=[pl.BlockSpec((step, wide), lambda i: (i, 0)), whole(down.shape)]
        + [HELD] * len(others),
        out_specs=pl.BlockSpec((step, model), lambda i: (i, 0)),
        out_shape=shaped((tokens, model), BF16),
        compiler_params=ROOMY,
    )(activation, down, *others)


def join_rows(ring, mine, theirs):
    rows, wide = mine.shape

    def body(table, mine_ref, theirs_ref, out_ref, sems):
        core = table[ring.core_at]
        copies = []
        for n, (place, ref) in enumerate(((core, mine_ref), (1 - core, theirs_ref))):
            target = out_ref.at[pl.ds(pl.multiple_of(place * rows, 16), rows)]
            copies.append(pltpu.make_async_copy(ref, target, sems.at[n]))
        for copy in copies:
            copy.start()
        for copy in copies:
            copy.wait()

    return pl.pallas_call(
        body,
        grid_spec=pltpu.PrefetchScalarGridSpec(
            num_scalar_prefetch=1,
            grid=(1,),
            in_specs=[HELD] * 2,
            out_specs=whole((2 * rows, wide)),
            scratch_shapes=[pltpu.SemaphoreType.DMA((2,))],
        ),
        out_shape=shaped((2 * rows, wide), mine.dtype),
        compiler_params=ROOMY,
    )(ring.table, mine, theirs)


def feed_forward(ring, twos, cots, weights, down, others):
    chips = ring.chips
    tok, model = twos[0][2].shape
    _, _, half, wide = weights[0].shape
    steps = chips // 2
    chunk = 2 * tok
    count = len(twos)

    def body(table, *refs):
        two_refs, cot_refs = refs[:count], refs[count : 2 * count]
        weight_refs = refs[2 * count : 2 * count + 4]
        down_ref = refs[2 * count + 4]
        outs = refs[2 * count + 5 + len(others) :]
        act_ref, gate_ref, up_ref, grad_ref, two_out, cot_out = outs[:6]
        two_buf, cot_buf, weight_buf, down_buf, two_sems, cot_sems, weight_sems = outs[6:]
        step = pl.program_id(0)
        side = table[ring.side_at]
        moves = [pltpu.make_async_copy(down_ref, down_buf, weight_sems.at[8])]
        for n, ref in enumerate(weight_refs):
            place = side if n % 2 == 0 else 1 - side
            for part in range(2):
                target = weight_buf.at[part, pl.ds(n // 2 * chips, chips), place]
                sem = weight_sems.at[2 * n + part]
                moves.append(pltpu.make_async_copy(ref.at[:, part], target, sem))
        blocks = fetches(twos, two_refs, two_buf, two_sems)
        blocks += fetches(cots, cot_refs, cot_buf, cot_sems)

        @pl.when(step == 0)
        def _():
            for move in moves + blocks:
                move.start()
            for move in moves:
                move.wait()

        for at in range(steps):

            @pl.when(step == at)
            def _():
                for (slot, _, _), block in zip(twos + cots, blocks):
                    if slot // 2 == at:
                        block.wait()

        two = two_buf[pl.ds(step * 2, 2)].reshape(chunk, model)
        cot = cot_buf[pl.ds(step * 2, 2)].reshape(chunk, model)
        two_out[...] = two
        cot_out[...] = cot
        gate_weight = weight_buf[0].reshape(model, wide)
        up_weight = weight_buf[1].reshape(model, wide)
        gate = dot(two, gate_weight)
        upward = dot(two, up_weight)
        grad = dot(cot, down_buf[...], LAST)
        sigma = jax.nn.sigmoid(gate)
        act_ref[...] = (gate * sigma * upward).astype(BF16)
        grad_gate = (grad * upward * (sigma * (1.0 + gate * (1.0 - sigma)))).astype(BF16)
        grad_up = (grad * gate * sigma).astype(BF16)
        gate_ref[...] = grad_gate
        up_ref[...] = grad_up
        grad_two = dot(grad_gate, gate_weight, LAST) + dot(grad_up, up_weight, LAST)
        grad_ref[...] = grad_two.astype(BF16)

    def out(width):
        return pl.BlockSpec((chunk, width), lambda i, _: (i, 0))

    widths = (wide, wide, wide, model, model, model)
    kinds = (BF16,) * 6
    return pl.pallas_call(
        body,
        grid_spec=pltpu.PrefetchScalarGridSpec(
            num_scalar_prefetch=1,
            grid=(steps,),
            in_specs=[HELD] * (2 * count + 5 + len(others)),
            out_specs=[out(w) for w in widths],
            scratch_shapes=[
                pltpu.VMEM((chips, tok, model), BF16),
                pltpu.VMEM((chips, tok, model), BF16),
                pltpu.VMEM((2, 2 * chips, 2, half, wide), BF16),
                pltpu.VMEM(down.shape, BF16),
                pltpu.SemaphoreType.DMA((count,)),
                pltpu.SemaphoreType.DMA((count,)),
                pltpu.SemaphoreType.DMA((9,)),
            ],
        ),
        out_shape=[shaped((chips * tok, w), kind) for w, kind in zip(widths, kinds)],
        compiler_params=ROOMY,
    )(
        ring.table,
        *[piece for _, _, piece in twos],
        *[piece for _, _, piece in cots],
        *weights,
        down,
        *others,
    )


def load_window(table, at, own_ref, other_ref, window, rows):
    chips = own_ref.shape[0]
    for b in range(window.shape[0] // rows):
        place = table[at + b]
        target = window.at[b * rows : (b + 1) * rows, :]

        @pl.when(place < chips)
        def _():
            target[...] = own_ref[place]

        @pl.when(place >= chips)
        def _():
            target[...] = other_ref[place - chips]


def allowed_pairs(first_ref, reach, keys, rows):
    key = lax.broadcasted_iota(jnp.int32, (keys, rows), 0)
    token = lax.broadcasted_iota(jnp.int32, (keys, rows), 1)
    allowed = (key >= first_ref[...]) & (key <= token + reach)
    return jnp.concatenate([allowed, allowed], 1)


def stacked(block, low_side):
    turned = pltpu.roll(block, HEAD_DIM, 1)
    low = lane_low(block.shape)
    if low_side:
        one, two = jnp.where(low, block, 0.0), jnp.where(low, turned, 0.0)
    else:
        one, two = jnp.where(low, 0.0, turned), jnp.where(low, 0.0, block)
    return jnp.concatenate([one, two], 0).astype(BF16)


def attend_kernel(
    ring, table, proj_ref, own_ref, other_ref, first_ref, cos_ref, sin_ref, q_ref, out_ref, log_ref, window
):
    rows = proj_ref.shape[0]
    keys = window.shape[0]

    @pl.when(pl.program_id(1) == 0)
    def _():
        load_window(table, ring.window, own_ref, other_ref, window, rows)

    block = proj_ref[...]
    block = block * cos_ref[...] + rotated(block) * sin_ref[...]
    q_ref[...] = block.astype(BF16)
    queries = stacked(block, True)
    score = dot(window[...], queries, LAST) * SCALE
    allowed = allowed_pairs(first_ref, keys - rows, keys, rows)
    score = jnp.where(allowed, score, -jnp.inf)
    top = jnp.max(score, 0, keepdims=True)
    expon = jnp.exp(score - top)
    total = jnp.sum(expon, 0, keepdims=True)
    log_ref[0] = top + jnp.log(total)
    probs = (expon * (1.0 / total)).astype(BF16)
    out = dot(probs, window[...], FIRST)
    one, two = out[:rows], out[rows:]
    out_ref[...] = jnp.where(lane_low(one.shape), pltpu.roll(one, HEAD_DIM, 1), two).astype(BF16)


def attend_back_kernel(
    ring,
    table,
    q_ref,
    grad_ref,
    att_ref,
    log_ref,
    own_ref,
    other_ref,
    first_ref,
    cos_ref,
    sin_ref,
    gq_ref,
    gown_ref,
    gother_ref,
    window,
    total,
):
    rows = q_ref.shape[0]
    keys = window.shape[0]
    chips = own_ref.shape[0]
    step = pl.program_id(1)

    @pl.when(step == 0)
    def _():
        load_window(table, ring.window, own_ref, other_ref, window, rows)
        total[...] = jnp.zeros_like(total)

    grad = grad_ref[...].astype(F32)
    queries = stacked(q_ref[...].astype(F32), True)
    grads = stacked(grad, False)
    product = jnp.transpose(grad * att_ref[...].astype(F32))
    delta = jnp.concatenate(
        [
            jnp.sum(product[:HEAD_DIM], 0, keepdims=True),
            jnp.sum(product[HEAD_DIM:], 0, keepdims=True),
        ],
        1,
    )
    score = dot(window[...], queries, LAST) * SCALE
    allowed = allowed_pairs(first_ref, keys - rows, keys, rows)
    probs = jnp.where(allowed, jnp.exp(score - log_ref[0]), 0.0)
    grad_probs = dot(window[...], grads, LAST)
    grad_scores = (probs * (grad_probs - delta) * SCALE).astype(BF16)
    total[...] += dot(grad_scores, queries) + dot(probs.astype(BF16), grads)
    grad_queries = dot(grad_scores, window[...], FIRST)
    one, two = grad_queries[:rows], grad_queries[rows:]
    block = jnp.where(lane_low(one.shape), one, pltpu.roll(two, HEAD_DIM, 1))
    gq_ref[...] = (block * cos_ref[...] - rotated(block) * sin_ref[...]).astype(BF16)

    @pl.when(step == pl.num_programs(1) - 1)
    def _():
        gown_ref[...] = jnp.zeros_like(gown_ref)
        gother_ref[...] = jnp.zeros_like(gother_ref)
        for b in range(keys // rows):
            place = table[ring.window + b]
            block = total[b * rows : (b + 1) * rows, :]

            @pl.when(place < chips)
            def _():
                gown_ref[place] = block

            @pl.when(place >= chips)
            def _():
                gother_ref[place - chips] = block.astype(BF16)


def attention_call(kernel, ring, groups, ins, outs, scratch, before, others):
    start, stop = groups
    inner = HEADS // KV_HEADS // 2
    given = len(ins)

    def body(table, *refs):
        kernel(ring, table, *refs[:given], *refs[given + len(before) + len(others) :])

    def spec(entry):
        shape, place = entry
        return pl.BlockSpec(
            shape, lambda g, i, table: place(g + start, (g + start) * inner + i, table)
        )

    return pl.pallas_call(
        body,
        grid_spec=pltpu.PrefetchScalarGridSpec(
            num_scalar_prefetch=1,
            grid=(stop - start, inner),
            in_specs=[spec(entry) for _, entry in ins] + [HELD] * (len(before) + len(others)),
            out_specs=[spec(entry) for _, entry in outs],
            scratch_shapes=scratch,
        ),
        out_shape=[shape for shape, _ in outs],
        input_output_aliases={1 + given + k: k for k in range(len(before))},
        compiler_params=ROOMY,
    )(ring.table, *[value for value, _ in ins], *before, *others)


def attention_specs(ring, rows):
    return (
        ((rows, LANES), lambda g, pair, table: (0, pair)),
        ((rows, LANES), lambda g, pair, table: (0, table[ring.place_near + pair])),
        ((1, 1, 2 * rows), lambda g, pair, table: (pair, 0, 0)),
        ((ring.chips, rows, LANES), lambda g, pair, table: (0, 0, g)),
        ((1, rows), lambda g, pair, table: (0, 0)),
        ((rows, LANES), lambda g, pair, table: (0, 0)),
    )


def attend(ring, groups, others, keys, proj, own, other, first, cosine, sine, before=()):
    rows = proj.shape[0]
    pairs = HEADS // 2
    block, near_block, log_block, kv_block, row, table = attention_specs(ring, rows)
    return attention_call(
        attend_kernel,
        ring,
        groups,
        [(proj, block), (own, kv_block), (other, kv_block)]
        + [(first, row), (cosine, table), (sine, table)],
        [
            (shaped((rows, pairs * LANES), BF16), block),
            (shaped((rows, pairs * LANES), BF16), near_block),
            (shaped((pairs, 1, 2 * rows), F32), log_block),
        ],
        [pltpu.VMEM((keys, LANES), BF16)],
        before,
        others,
    )


def attend_back(
    ring, groups, others, keys, queries, grad, attended, logs, own, other, first, cosine, sine, before=()
):
    rows = queries.shape[0]
    block, near_block, log_block, kv_block, row, table = attention_specs(ring, rows)
    return attention_call(
        attend_back_kernel,
        ring,
        groups,
        [
            (queries, block),
            (grad, near_block),
            (attended, near_block),
            (logs, log_block),
            (own, kv_block),
            (other, kv_block),
            (first, row),
            (cosine, table),
            (sine, table),
        ],
        [
            (shaped(queries.shape, BF16), block),
            (shaped(own.shape, F32), kv_block),
            (shaped(own.shape, BF16), kv_block),
        ],
        [pltpu.VMEM((keys, LANES), BF16), pltpu.VMEM((keys, LANES), F32)],
        before,
        others,
    )


def on_device(
    reps,
    shards,
    hidden_in,
    segments,
    cotangent,
    qkv_weight,
    out_weight,
    gate_up_weight,
    down_weight,
    attn_gain,
    ffn_gain,
):
    tok = hidden_in.shape[1]
    model = hidden_in.shape[2]
    rows, width = qkv_weight.shape
    blocks = min(REACH // tok, shards - 1) + 1
    ring = Ring(shards, blocks)
    chips = ring.chips
    middle = chips * rows
    ff = down_weight.shape[0] * shards
    wide = ff // chips
    half = rows // 2
    side = ring.side
    twin_map = [(i, i ^ 1) for i in range(reps)]
    side_groups = [list(range(s, reps, 2)) for s in range(2)]
    hidden, cot_local, seg_row = hidden_in[0], cotangent[0], segments[0]
    groups = ((0, KV_HEADS // 2), (KV_HEADS // 2, KV_HEADS))

    def twin(value):
        return lax.ppermute(value, "rep", twin_map)

    def rest_of_reps(value):
        if reps == 2:
            return value
        return lax.psum(value, "rep", axis_index_groups=side_groups)

    def over_reps(value):
        mine = rest_of_reps(value).astype(BF16)
        return mine.astype(F32) + twin(mine).astype(F32)

    def cut(value, size):
        return [value[k * size : (k + 1) * size] for k in range(chips)]

    mine = cut_columns(ring, gate_up_weight, wide)
    mine = lax.all_to_all(
        mine, "shard", 0, 0, axis_index_groups=ring.core_groups, tiled=True
    )

    packed = pack_weight(qkv_weight, attn_gain, ffn_gain, ring.table)
    qkv_pieces, qkv_marks = ring.gather_both(packed)

    offset = ring.index * tok
    local_seg = lax.dynamic_slice_in_dim(seg_row, offset, tok)
    starts = jnp.sum((seg_row[None, :] < local_seg[:, None]).astype(jnp.int32), 1)
    positions = offset + jnp.arange(tok, dtype=jnp.int32) - starts
    freqs = jnp.exp(
        (jnp.arange(LANES) % (HEAD_DIM // 2)).astype(F32) * (-2.0 * math.log(10000.0) / HEAD_DIM)
    )
    angles = positions.astype(F32)[:, None] * freqs[None, :]
    cosine, sine = jnp.cos(angles), jnp.sin(angles)
    first = (starts - offset + (blocks - 1) * tok)[None, :]

    proj, kv_local, input_one, factor_one, gains = project(
        ring, hidden, cosine, sine, qkv_pieces, width, (mine,)
    )
    out_pieces, out_marks = ring.gather_both(after(out_weight, *qkv_marks[-2:]))
    kv_own = stack_blocks(ring, ring.gather(kv_local, {2: out_marks[1:3]}), out_marks[3:5])
    kv_other = ring.swap(kv_own)
    theirs = twin(mine)
    cots = ring.gather(after(cot_local, *out_marks[-2:]))
    tables = (kv_own, kv_other, first, cosine, sine)
    keys = blocks * tok
    kept = attend(ring, groups[0], (), keys, proj, *tables)
    kept = attend(ring, groups[1], tuple(out_marks[5:7]), keys, proj, *tables, kept)
    queries, attended, logs = kept
    residual, factor_two, input_two = project_out(ring, attended, hidden, gains, out_pieces, ())

    twos = ring.gather(input_two)
    weights = (mine, theirs, ring.swap(mine), ring.swap(theirs))
    down = join_rows(ring, down_weight, ring.swap(down_weight))
    activation, grad_gate, grad_up, grad_two, two, cot = feed_forward(
        ring, twos, cots, weights, down, ()
    )
    grad_two, two_marks = ring.scatter(cut(grad_two, tok))

    ffn_term = down_project(activation, down, two_marks[0])
    gu_gots = [ring.swap(v) for v in give_terms(ring, two, (grad_gate, grad_up), (ffn_term,))]
    down_keep, down_give = down_terms(ring, activation, cot, two_marks[1])
    down_keep = rest_of_reps(down_keep + ring.swap(down_give).astype(F32)).astype(BF16)
    gu_keep, gu_give = halve_terms(ring, two, (grad_gate, grad_up), gu_gots)
    gu_recv = twin(gu_give)
    gu_sum = rest_of_reps(gu_keep + gu_recv.astype(F32)).astype(BF16)
    down_recv = twin(down_keep)
    grad_down = down_keep.astype(F32) + down_recv.astype(F32)

    grad_residual, residual_half, grad_attended, gain_two_term = back_out(
        ring,
        grad_two,
        residual,
        factor_two,
        gains,
        cot_local,
        out_pieces,
        (ffn_term, gu_give),
    )
    (out_give,) = give_terms(ring, attended, (residual_half,))
    out_got = ring.swap(out_give)
    tables = (logs, kv_own, kv_other, first, cosine, sine)

    done = []

    def ffn_ties(step, marks):
        if step == 1:
            return two_marks[-1]
        if step == 2:
            return ()
        others = {3: (*marks[0], out_give), 4: (*marks[1], gu_sum)}[step]
        before = done[-1] if done else ()
        done.append(
            attend_back(
                ring, groups[step - 3], others, keys, queries, grad_attended, attended, *tables, before
            )
        )
        return (done[-1][0],)

    ffn_out, ffn_marks = ring.scatter(cut(ffn_term, tok), ffn_ties)
    hidden_out = (residual + ffn_out).astype(BF16)
    grad_queries, kv_keep, kv_give = done[-1]
    out_keep, out_send = halve_terms(ring, attended, (residual_half,), (out_got,))
    out_recv = twin(out_send)
    gu_sum = lax.all_to_all(
        gu_sum, "shard", 0, 0, axis_index_groups=ring.core_groups, tiled=True
    )
    (query_give,) = give_terms(ring, input_one, (grad_queries,))
    kv_give = after(kv_give, query_give, out_send)
    kv_keep = kv_keep + ring.swap(kv_give).astype(F32)
    query_got = ring.swap(query_give)
    (query_term,) = keep_terms(ring, input_one, (grad_queries,), (query_got,))
    query_sum, query_marks = ring.scatter(cut(query_term, rows))

    def kv_ties(step, marks):
        return {3: (query_got,), 4: query_marks[0]}.get(step, ())

    grad_kv, kv_marks = ring.scatter([kv_keep[k] for k in range(chips)], kv_ties)
    out_term = (out_keep + out_recv.astype(F32)).astype(BF16).reshape(chips * half, model)
    out_sum, out_marks = ring.scatter(cut(after(out_term, *ffn_marks[3]), half))
    grad_kv = finish_kv(
        ring, grad_kv, cosine, sine, (*query_marks[1], *ffn_marks[3], *out_marks[0], gu_sum)
    )
    (kv_give,) = give_terms(ring, input_one, (grad_kv,))
    (kv_term,) = keep_terms(ring, input_one, (grad_kv,), (ring.swap(kv_give),))
    gu_other = twin(gu_sum)
    grad_hidden, gain_one_term = back_project(
        ring,
        grad_queries,
        grad_kv,
        hidden,
        factor_one,
        gains,
        grad_residual,
        qkv_pieces,
        width,
        (*out_marks[1], *query_marks[2]),
    )
    gain_terms = jnp.concatenate([gain_one_term[:1], gain_two_term[:1]], 0)
    gain_terms = gain_terms[:, :middle] + ring.swap(gain_terms[:, middle:])
    below = gain_terms.reshape(2, chips, rows).transpose(1, 0, 2).reshape(chips, 1, 2 * rows)
    below = jnp.pad(below, ((0, 0), (0, 15), (0, kv_term.shape[1] - 2 * rows)))
    below = below.astype(BF16)
    parts = [jnp.concatenate([part, below[k]], 0) for k, part in enumerate(cut(kv_term, rows))]
    kv_sum, _ = ring.scatter(parts)
    kv_sum = over_reps(kv_sum)
    grad_qkv = jnp.concatenate([over_reps(query_sum), kv_sum[:rows]], 1)
    out_sum = rest_of_reps(out_sum).astype(BF16)
    out_other = twin(out_sum)
    grad_out = jnp.concatenate([pick(side, out_sum, out_other), pick(side, out_other, out_sum)], 0)
    return (
        hidden_out[None],
        grad_hidden[None],
        grad_qkv,
        grad_out.astype(F32),
        join_columns(ring, gu_sum, gu_other),
        grad_down,
        kv_sum[rows, :rows],
        kv_sum[rows, rows : 2 * rows],
    )


def solution(mesh):
    reps, shards = mesh.shape["rep"], mesh.shape["shard"]

    def layer(*args):
        return on_device(reps, shards, *args)

    return jax.shard_map(
        layer,
        mesh=mesh,
        in_specs=(
            P("rep", "shard", None),
            P("rep", None),
            P("rep", "shard", None),
            P("shard", None),
            P("shard", None),
            P("shard", None),
            P("shard", None),
            P("shard"),
            P("shard"),
        ),
        out_specs=(
            P("rep", "shard", None),
            P("rep", "shard", None),
            P("shard", None),
            P("shard", None),
            P("shard", None),
            P("shard", None),
            P("shard"),
            P("shard"),
        ),
        check_vma=False,
    )
```

```python
import math

import jax
import jax.numpy as jnp
import numpy as np
from jax import lax
from jax.experimental import pallas as pl
from jax.experimental.pallas import tpu as pltpu
from jax.sharding import PartitionSpec as P

HEADS = 32
KV_HEADS = 4
HEAD_DIM = 64
REACH = 1024
EPS = 1e-05
F32 = jnp.float32
BF16 = jnp.bfloat16
LANES = 128
SCALE = HEAD_DIM**-0.5
LIMIT = 58 * 1024 * 1024
ROOMY = pltpu.CompilerParams(vmem_limit_bytes=LIMIT)
HELD = pl.BlockSpec(memory_space=pl.ANY)


def takes(micros):
    return pl.CostEstimate(
        flops=int(micros * 1.1e9), bytes_accessed=int(micros * 3.3e6), transcendentals=0
    )


def dot(a, b, dims=((1,), (0,))):
    return lax.dot_general(a, b, (dims, ((), ())), preferred_element_type=F32)


LAST = ((1,), (1,))
FIRST = ((0,), (0,))


def pick(flag, one, other):
    return jnp.where(flag == 0, one, other)


class Ring:
    def __init__(self, size, window):
        self.size = size
        self.chips = chips = size // 2
        rows = chips // 2
        self.order = [2 * i for i in range(rows)] + [2 * i + 1 for i in reversed(range(rows))]
        self.place = [self.order.index(chip) for chip in range(chips)]
        self.half = chips // 2

        def turned(step):
            return [
                (s, self.order[(self.place[s // 2] + step) % chips] * 2 + s % 2)
                for s in range(size)
            ]

        self.ahead = turned(1)
        self.back = turned(-1)
        self.sibling = [(s, s ^ 1) for s in range(size)]
        self.core_groups = [list(range(core, size, 2)) for core in range(2)]
        self.near, self.place_near, self.cores, self.place_cores, self.window = (
            k * size for k in range(5)
        )
        self.core_at = self.window + window
        self.side_at = self.core_at + 1
        table = []
        for side in range(2):
            for s in range(size):
                chip, core = s // 2, s % 2
                at = self.place[chip]
                near = [
                    self.order[(at + j) % chips] * 2 + (core ^ other)
                    for other in range(2)
                    for j in range(chips)
                ]
                cores = [j * 2 + (core ^ other) for other in range(2) for j in range(chips)]
                place_near = [near.index(d) for d in range(size)]
                place_cores = [cores.index(d) for d in range(size)]
                seen = [place_near[(s + 1 - window + b) % size] for b in range(window)]
                table.append(near + place_near + cores + place_cores + seen + [core, side])
        self.index = lax.axis_index("shard")
        self.side = lax.axis_index("rep") % 2
        self.table = lax.dynamic_index_in_dim(
            jnp.asarray(np.array(table, np.int32)), self.side * size + self.index, 0, False
        )

    def swap(self, value):
        return lax.ppermute(value, "shard", self.sibling)

    def gather(self, block, ties=None):
        n, h = self.chips, block.shape[0] // 2
        cw = ccw = block
        found = [(0, 0, block)]
        for k in range(1, self.half):
            if ties and k in ties:
                cw, ccw = after(cw, *ties[k]), after(ccw, *ties[k])
            cw = lax.ppermute(cw, "shard", self.ahead)
            ccw = lax.ppermute(ccw, "shard", self.back)
            found += [(n - k, 0, cw), (k, 0, ccw)]
        top = lax.ppermute(cw[:h], "shard", self.ahead)
        low = lax.ppermute(ccw[h:], "shard", self.back)
        return found + [(self.half, 0, top), (self.half, h, low)]

    def gather_both(self, block, ties=None):
        own = self.gather(block, ties)
        other = [(k + self.chips, row, self.swap(piece)) for k, row, piece in own]
        return own + other, [piece for _, _, piece in own]

    def scatter(self, parts, ties=None):
        n, m = self.chips, self.half
        rows = parts.shape[0] // n
        h = rows // 2
        cw, ccw = parts[m * rows : m * rows + h], parts[m * rows + h : (m + 1) * rows]
        marks = []
        for k in range(m - 1, -1, -1):
            if ties:
                others = ties(m - k, marks)
                if others:
                    cw, ccw = after(cw, *others), after(ccw, *others)
            cw = lax.ppermute(cw, "shard", self.ahead)
            ccw = lax.ppermute(ccw, "shard", self.back)
            marks.append((cw, ccw))
            if k > 0:
                cw, ccw = add_step(parts, rows, k, n - k, cw, ccw)
        return (parts, cw, ccw), marks


def add_step(parts, rows, ahead, back, cw, ccw):
    width = parts.shape[1]
    got = cw.shape[0]

    def body(ahead_ref, back_ref, cw_ref, ccw_ref, one_ref, two_ref):
        if got < rows:
            one_ref[got:] = ahead_ref[got:]
            two_ref[: rows - ccw.shape[0]] = back_ref[: rows - ccw.shape[0]]
        last = rows - ccw.shape[0]
        one_ref[:got] = (ahead_ref[:got].astype(F32) + cw_ref[...].astype(F32)).astype(BF16)
        two_ref[last:] = (back_ref[last:].astype(F32) + ccw_ref[...].astype(F32)).astype(BF16)

    return pl.pallas_call(
        body,
        grid=(1,),
        in_specs=[
            pl.BlockSpec((rows, width), lambda _: (ahead, 0)),
            pl.BlockSpec((rows, width), lambda _: (back, 0)),
            whole(cw.shape),
            whole(ccw.shape),
        ],
        out_specs=[whole((rows, width))] * 2,
        out_shape=[shaped((rows, width), BF16)] * 2,
        cost_estimate=takes(0.875), compiler_params=ROOMY,
    )(parts, parts, cw, ccw)


def summed(sums):
    parts, cw, ccw = sums
    return parts[: cw.shape[0]].astype(F32) + cw.astype(F32) + ccw.astype(F32)


def whole(shape):
    return pl.BlockSpec(shape, lambda *_: (0,) * len(shape))


def shaped(shape, kind):
    return jax.ShapeDtypeStruct(shape, kind)


def call(kernel, table, ins, outs, pieces=(), scratch=(), others=(), cost=3):
    count, more, extra = len(ins), len(pieces), len(others)

    def body(table_ref, *refs):
        behind = count + more + extra
        kernel(
            table_ref,
            refs[:count],
            refs[count : count + more],
            refs[behind : behind + len(outs)],
            refs[behind + len(outs) :],
        )

    return pl.pallas_call(
        body,
        grid_spec=pltpu.PrefetchScalarGridSpec(
            num_scalar_prefetch=1,
            grid=(1,),
            in_specs=[whole(v.shape) for v in ins] + [HELD] * (more + extra),
            out_specs=[whole(v.shape) for v in outs],
            scratch_shapes=list(scratch),
        ),
        out_shape=list(outs),
        compiler_params=ROOMY,
        cost_estimate=takes(cost),
    )(table, *ins, *pieces, *others)


def after(value, *others):
    return pl.pallas_call(
        lambda *refs: None,
        in_specs=[HELD] * (1 + len(others)),
        out_specs=HELD,
        out_shape=shaped(value.shape, value.dtype),
        input_output_aliases={0: 0},
    )(value, *others)


def fetches(pieces, refs, buffer, sems):
    return [
        pltpu.make_async_copy(
            ref, buffer.at[k, pl.ds(row, ref.shape[0])], sems.at[n]
        )
        for n, ((k, row, _), ref) in enumerate(zip(pieces, refs))
    ]


def block_at(place):
    return pl.ds(pl.multiple_of(place * LANES, LANES), LANES)


def columns(block):
    return slice(block * LANES, (block + 1) * LANES)


def lane_low(shape):
    return lax.broadcasted_iota(jnp.int32, shape, len(shape) - 1) % LANES < HEAD_DIM


def rotated(values):
    quarter = HEAD_DIM // 2
    first = lax.broadcasted_iota(jnp.int32, values.shape, 1) % HEAD_DIM < quarter
    return jnp.where(
        first, -pltpu.roll(values, LANES - quarter, 1), pltpu.roll(values, quarter, 1)
    )


def pack_weight(weight, gain_one, gain_two):
    rows, width = weight.shape

    def body(weight_ref, one_ref, two_ref, out_ref):
        out_ref[:, :width] = weight_ref[...]
        lane = lax.broadcasted_iota(jnp.int32, (rows, LANES), 1)
        block = jnp.where(lane == 0, one_ref[...], jnp.where(lane == 1, two_ref[...], 0.0))
        out_ref[:, width:] = block.astype(BF16)

    gains = [g.astype(F32)[:, None] for g in (gain_one, gain_two)]
    return pl.pallas_call(body, out_shape=shaped((rows, width + LANES), BF16), cost_estimate=takes(3), compiler_params=ROOMY)(
        weight, *gains
    )


def project(ring, hidden, cosine, sine, pieces, width, others):
    size = ring.size
    rows, model = hidden.shape
    qsize = HEADS * HEAD_DIM
    step = 2 * LANES

    def kernel(table, ins, refs, outs, scratch):
        hidden_ref, cos_ref, sin_ref = ins
        q_ref, kv_ref, input_ref, factor_ref, gain_ref = outs
        buffer, sems = scratch
        copies = fetches(pieces, refs, buffer, sems)
        for copy in copies:
            copy.start()
        values = hidden_ref[...].astype(F32)
        factor = lax.rsqrt(jnp.mean(values * values, -1, keepdims=True) + EPS)
        factor_ref[...] = jnp.broadcast_to(factor, factor_ref.shape)
        for copy in copies:
            copy.wait()
        for k in range(size):
            gains = jnp.transpose(buffer[k, :, width : width + LANES].astype(F32))
            gain_ref[:, columns(k)] = gains[:8]
            part = hidden_ref[:, block_at(table[ring.near + k])].astype(F32)
            input_ref[:, columns(k)] = (part * factor * gains[:1]).astype(BF16)
        inputs = input_ref[...]
        for start in range(0, qsize, step):
            weights = buffer[:, :, start : start + step].reshape(model, step)
            q_ref[:, start : start + step] = dot(inputs, weights)
        weights = buffer[:, :, qsize:width].reshape(model, width - qsize)
        proj = dot(inputs, weights)
        for pair in range(KV_HEADS // 2):
            keys = proj[:, columns(pair)]
            keys = keys * cos_ref[...] + rotated(keys) * sin_ref[...]
            heads = proj[:, columns(KV_HEADS // 2 + pair)]
            low = lane_low(keys.shape)
            one = jnp.where(low, keys, pltpu.roll(heads, HEAD_DIM, 1))
            two = jnp.where(low, pltpu.roll(keys, HEAD_DIM, 1), heads)
            kv_ref[:, columns(2 * pair)] = one.astype(BF16)
            kv_ref[:, columns(2 * pair + 1)] = two.astype(BF16)

    return call(
        kernel,
        ring.table,
        [hidden, cosine, sine],
        [
            shaped((rows, qsize), F32),
            shaped((rows, KV_HEADS * LANES), BF16),
            shaped((rows, model), BF16),
            shaped((rows, LANES), F32),
            shaped((8, model), F32),
        ],
        [piece for _, _, piece in pieces],
        [
            pltpu.VMEM((size, rows, width + LANES), BF16),
            pltpu.SemaphoreType.DMA((len(pieces),)),
        ],
        others,
        9,
    )


def stack_blocks(ring, pieces, others):
    rows, width = pieces[0][2].shape

    def body(*refs):
        copies = fetches(pieces, refs[: len(pieces)], refs[-2], refs[-1])
        for copy in copies:
            copy.start()
        for copy in copies:
            copy.wait()

    return pl.pallas_call(
        body,
        in_specs=[HELD] * (len(pieces) + len(others)),
        out_specs=pl.BlockSpec(memory_space=pltpu.VMEM),
        out_shape=shaped((ring.chips, rows, width), pieces[0][2].dtype),
        scratch_shapes=[pltpu.SemaphoreType.DMA((len(pieces),))],
        cost_estimate=takes(2.5), compiler_params=ROOMY,
    )(*[piece for _, _, piece in pieces], *others)


def project_out(ring, attended, hidden, gains, pieces, others):
    size = ring.size
    rows, model = hidden.shape
    step = 2 * LANES

    def kernel(table, ins, refs, outs, scratch):
        att_ref, hidden_ref, gain_ref = ins
        residual_ref, factor_ref, input_ref = outs
        buffer, sems = scratch
        copies = fetches(pieces, refs, buffer, sems)
        for copy in copies:
            copy.start()
        for copy in copies:
            copy.wait()
        inputs = att_ref[...]
        squares = jnp.zeros((rows, 1), F32)
        for start in range(0, model, step):
            weights = buffer[:, :, start : start + step].reshape(model, step)
            part = hidden_ref[:, start : start + step].astype(F32) + dot(inputs, weights)
            residual_ref[:, start : start + step] = part
            squares += jnp.sum(part * part, -1, keepdims=True)
        factor = lax.rsqrt(squares * (1.0 / model) + EPS)
        factor_ref[...] = jnp.broadcast_to(factor, factor_ref.shape)
        for k in range(size):
            device = table[ring.cores + k]
            gain = gain_ref[1:2, block_at(table[ring.place_near + device])]
            part = residual_ref[:, block_at(device)] * factor
            input_ref[:, columns(k)] = (part * gain).astype(BF16)

    return call(
        kernel,
        ring.table,
        [attended, hidden, gains],
        [shaped((rows, model), F32), shaped((rows, LANES), F32), shaped((rows, model), BF16)],
        [piece for _, _, piece in pieces],
        [
            pltpu.VMEM((size, rows, model), BF16),
            pltpu.SemaphoreType.DMA((len(pieces),)),
        ],
        others,
        8,
    )


def back_out(ring, sums, residual, factor, gains, cot, pieces, others):
    size = ring.size
    rows, model = residual.shape

    def kernel(table, ins, refs, outs, scratch):
        own_ref, cw_ref, ccw_ref, residual_ref, factor_ref, gain_ref, cot_ref = ins
        grad_res_ref, half_ref, att_ref, term_ref = outs
        buffer, sems, total = scratch
        copies = fetches(pieces, refs, buffer, sems)
        for copy in copies:
            copy.start()
        factor = factor_ref[...]
        mean = jnp.zeros((rows, 1), F32)
        for d in range(size):
            place, source = (
                block_at(table[order + d]) for order in (ring.place_near, ring.place_cores)
            )
            grad = sum(ref[:, source].astype(F32) for ref in (own_ref, cw_ref, ccw_ref))
            total[:, columns(d)] = grad
            normed = residual_ref[:, columns(d)] * factor
            product = grad * normed
            term_ref[:, place] = jnp.broadcast_to(
                jnp.sum(product, 0, keepdims=True), (8, LANES)
            )
            mean += jnp.sum(product * gain_ref[1:2, place], -1, keepdims=True)
        mean *= 1.0 / model
        for d in range(size):
            place = block_at(table[ring.place_near + d])
            grad = total[:, columns(d)] * gain_ref[1:2, place]
            normed = residual_ref[:, columns(d)] * factor
            back = cot_ref[:, columns(d)].astype(F32) + factor * (grad - normed * mean)
            grad_res_ref[:, columns(d)] = back
            half_ref[:, columns(d)] = back.astype(BF16)
        for copy in copies:
            copy.wait()
        halves = half_ref[...]
        for k in range(0, size, 2):
            weights = buffer[k : k + 2].reshape(2 * rows, model)
            att_ref[:, k * LANES : (k + 2) * LANES] = dot(halves, weights, LAST).astype(BF16)

    return call(
        kernel,
        ring.table,
        [sums[0][:rows], sums[1], sums[2], residual, factor, gains, cot],
        [
            shaped((rows, model), F32),
            shaped((rows, model), BF16),
            shaped((rows, model), BF16),
            shaped((8, model), F32),
        ],
        [piece for _, _, piece in pieces],
        [
            pltpu.VMEM((size, rows, model), BF16),
            pltpu.SemaphoreType.DMA((len(pieces),)),
            pltpu.VMEM((rows, model), F32),
        ],
        others,
        3.5,
    )


def finish_kv(ring, sums, cosine, sine, others):
    def kernel(table, ins, refs, outs, scratch):
        own_ref, cw_ref, ccw_ref, cos_ref, sin_ref = ins
        grad = sum(ref[...].astype(F32) for ref in (own_ref, cw_ref, ccw_ref))
        for pair in range(KV_HEADS // 2):
            one = grad[:, columns(2 * pair)]
            two = grad[:, columns(2 * pair + 1)]
            low = lane_low(one.shape)
            keys = jnp.where(low, one, pltpu.roll(two, HEAD_DIM, 1))
            values = jnp.where(low, pltpu.roll(one, HEAD_DIM, 1), two)
            keys = keys * cos_ref[...] - rotated(keys) * sin_ref[...]
            outs[0][:, columns(pair)] = keys.astype(BF16)
            outs[0][:, columns(KV_HEADS // 2 + pair)] = values.astype(BF16)

    rows = sums[1].shape[0]
    return call(
        kernel,
        ring.table,
        [sums[0][:rows], sums[1], sums[2], cosine, sine],
        [shaped((rows, 2 * KV_HEADS * HEAD_DIM), BF16)],
        others=others,
    )[0]


def back_project(
    ring, grad_queries, grad_kv, hidden, factor, gains, grad_residual, pieces, width, others
):
    size = ring.size
    rows, model = hidden.shape
    qsize = grad_queries.shape[1]

    def kernel(table, ins, refs, outs, scratch):
        gq_ref, gkv_ref, hidden_ref, factor_ref, gain_ref, grad_res_ref = ins
        grad_ref, term_ref = outs
        buffer, sems, total = scratch
        copies = fetches(pieces, refs, buffer, sems)
        for copy in copies:
            copy.start()
        for copy in copies:
            copy.wait()
        queries, keys = gq_ref[...], gkv_ref[...]
        for k in range(0, size, 2):
            weights = buffer[k : k + 2].reshape(2 * rows, width + LANES)
            total[:, k * LANES : (k + 2) * LANES] = dot(
                queries, weights[:, :qsize], LAST
            ) + dot(keys, weights[:, qsize:width], LAST)
        factor = factor_ref[...]
        mean = jnp.zeros((rows, 1), F32)
        for k in range(size):
            normed = hidden_ref[:, block_at(table[ring.near + k])].astype(F32) * factor
            product = total[:, columns(k)] * normed
            term_ref[:, columns(k)] = jnp.broadcast_to(
                jnp.sum(product, 0, keepdims=True), (8, LANES)
            )
            mean += jnp.sum(product * gain_ref[:1, columns(k)], -1, keepdims=True)
        mean *= 1.0 / model
        for k in range(size):
            place = block_at(table[ring.near + k])
            normed = hidden_ref[:, place].astype(F32) * factor
            scaled = total[:, columns(k)] * gain_ref[:1, columns(k)]
            back = grad_res_ref[:, place] + factor * (scaled - normed * mean)
            grad_ref[:, place] = back.astype(BF16)

    return call(
        kernel,
        ring.table,
        [grad_queries, grad_kv, hidden, factor, gains, grad_residual],
        [shaped((rows, model), BF16), shaped((8, model), F32)],
        [piece for _, _, piece in pieces],
        [
            pltpu.VMEM((size, rows, width + LANES), BF16),
            pltpu.SemaphoreType.DMA((len(pieces),)),
            pltpu.VMEM((rows, model), F32),
        ],
        others,
        4.025,
    )


def cut_columns(ring, weight, wide):
    rows = weight.shape[0]
    half = rows // 2

    def kernel(table, ins, refs, outs, scratch):
        upper = table[ring.side_at] == 0
        for chip in range(ring.chips):
            for part in range(2):
                start = (part * ring.chips + chip) * wide
                block = ins[0][:, start : start + wide].astype(F32)
                outs[0][chip, part] = jnp.where(upper, block[:half], block[half:]).astype(BF16)

    return call(
        kernel, ring.table, [weight], [shaped((ring.chips, 2, half, wide), BF16)]
    )[0]


def join_columns(ring, mine, theirs, others):
    chips, parts, half, wide = mine.shape

    def kernel(table, ins, refs, outs, scratch):
        flip = table[ring.side_at] == 0
        for chip in range(chips):
            for part in range(parts):
                start = (part * chips + chip) * wide
                one, two = ins[0][chip, part].astype(F32), ins[1][chip, part].astype(F32)
                outs[0][:half, start : start + wide] = jnp.where(flip, one, two)
                outs[0][half:, start : start + wide] = jnp.where(flip, two, one)

    return call(
        kernel,
        ring.table,
        [mine, theirs],
        [shaped((2 * half, parts * chips * wide), F32)],
        others=others,
    )[0]


def step_columns(tokens):
    return (4 if tokens <= LANES else 2) * LANES


def give_terms(ring, inputs, grads, others=()):
    tokens, model = inputs.shape
    count, extra = len(grads), len(others)
    step = step_columns(tokens)
    steps = model // 2 // step

    def body(input_ref, *refs):
        for grad_ref, out_ref in zip(refs[:count], refs[count + extra :]):
            out_ref[...] = dot(input_ref[...], grad_ref[...], FIRST).astype(BF16)

    return pl.pallas_call(
        body,
        grid=(steps,),
        in_specs=[pl.BlockSpec((tokens, step), lambda i: (0, steps + i))]
        + [whole(g.shape) for g in grads]
        + [HELD] * extra,
        out_specs=[pl.BlockSpec((step, g.shape[1]), lambda i: (i, 0)) for g in grads],
        out_shape=[shaped((model // 2, g.shape[1]), BF16) for g in grads],
        cost_estimate=takes(2.1), compiler_params=ROOMY,
    )(inputs, *grads, *others)


def keep_terms(ring, inputs, grads, gots):
    tokens, model = inputs.shape
    count = len(grads)
    step = step_columns(tokens)

    def body(input_ref, *refs):
        for part in range(count):
            term = dot(input_ref[...], refs[part][...], FIRST)
            refs[2 * count + part][...] = (term + refs[count + part][...].astype(F32)).astype(BF16)

    blocks = [pl.BlockSpec((step, g.shape[1]), lambda i: (i, 0)) for g in grads]
    return pl.pallas_call(
        body,
        grid=(model // 2 // step,),
        in_specs=[pl.BlockSpec((tokens, step), lambda i: (0, i))]
        + [whole(g.shape) for g in grads]
        + blocks,
        out_specs=blocks,
        out_shape=[shaped((model // 2, g.shape[1]), BF16) for g in grads],
        cost_estimate=takes(1.75), compiler_params=ROOMY,
    )(inputs, *grads, *gots)


def merge_terms(ring, inputs, grads, got, halves, halves_got):
    tokens, model = inputs.shape
    chips, _, half, wide = halves.shape
    rows = model // ring.size
    step = step_columns(tokens)
    each = step // rows
    high = rows + half

    def body(input_ref, grad_ref, got_ref, half_ref, half_got_ref, out_ref):
        term = dot(input_ref[...], grad_ref[...], FIRST)
        for n in range(each):
            at = slice(n * rows, (n + 1) * rows)
            total = term[at] + got_ref[at].astype(F32)
            out_ref[n * high : n * high + rows] = total.astype(BF16)
            total = half_ref[n, 0] + half_got_ref[n, 0].astype(F32)
            out_ref[n * high + rows : (n + 1) * high] = total.astype(BF16)

    block = pl.BlockSpec((each, 1, half, wide), lambda i: (i, 0, 0, 0))
    return pl.pallas_call(
        body,
        grid=(chips // each,),
        in_specs=[
            pl.BlockSpec((tokens, step), lambda i: (0, i)),
            whole(grads.shape),
            pl.BlockSpec((step, wide), lambda i: (i, 0)),
            block,
            block,
        ],
        out_specs=pl.BlockSpec((each * high, wide), lambda i: (i, 0)),
        out_shape=shaped((chips * high, wide), BF16),
        cost_estimate=takes(2), compiler_params=ROOMY,
    )(inputs, grads, got, halves, halves_got)


def halve_terms(ring, inputs, grads, gots):
    tokens, model = inputs.shape
    chips, count = ring.chips, len(grads)
    rows, wide = model // ring.size, grads[0].shape[1]
    half = rows // 2
    step = step_columns(tokens)
    each = step // rows

    def body(table, input_ref, *refs):
        upper = table[ring.side_at] == 0
        keep_ref, give_ref = refs[2 * count :]
        for part in range(count):
            term = dot(input_ref[...], refs[part][...], FIRST)
            for n in range(each):
                at = slice(n * rows, (n + 1) * rows)
                total = term[at] + refs[count + part][at].astype(F32)
                keep_ref[n, part] = jnp.where(upper, total[:half], total[half:])
                give_ref[n, part] = jnp.where(upper, total[half:], total[:half]).astype(BF16)

    return pl.pallas_call(
        body,
        grid_spec=pltpu.PrefetchScalarGridSpec(
            num_scalar_prefetch=1,
            grid=(chips // each,),
            in_specs=[pl.BlockSpec((tokens, step), lambda i, _: (0, i))]
            + [whole(g.shape) for g in grads]
            + [pl.BlockSpec((step, wide), lambda i, _: (i, 0))] * count,
            out_specs=[pl.BlockSpec((each, count, half, wide), lambda i, _: (i, 0, 0, 0))] * 2,
        ),
        out_shape=[shaped((chips, count, half, wide), kind) for kind in (F32, BF16)],
        cost_estimate=takes(3.15), compiler_params=ROOMY,
    )(ring.table, inputs, *grads, *gots)


def down_terms(ring, activation, cot, others):
    tokens, wide = activation.shape
    model = cot.shape[1]
    step, half = 2 * LANES, wide // 2

    def body(table, act_ref, cot_ref, *refs):
        keep_ref, give_ref = refs[len(others) :]
        total = dot(act_ref[...], cot_ref[...], FIRST)
        first = table[ring.core_at] == 0
        keep_ref[...] = jnp.where(first, total[:half], total[half:])
        give_ref[...] = jnp.where(first, total[half:], total[:half]).astype(BF16)

    return pl.pallas_call(
        body,
        grid_spec=pltpu.PrefetchScalarGridSpec(
            num_scalar_prefetch=1,
            grid=(model // step,),
            in_specs=[whole(activation.shape), pl.BlockSpec((tokens, step), lambda i, _: (0, i))]
            + [HELD] * len(others),
            out_specs=[pl.BlockSpec((half, step), lambda i, _: (0, i))] * 2,
        ),
        out_shape=[shaped((half, model), kind) for kind in (F32, BF16)],
        cost_estimate=takes(3.5), compiler_params=ROOMY,
    )(ring.table, activation, cot, *others)


def down_project(activation, down, others):
    tokens, wide = activation.shape
    model = down.shape[1]
    step = 2 * LANES

    def body(act_ref, down_ref, *refs):
        refs[-1][...] = dot(act_ref[...], down_ref[...]).astype(BF16)

    return pl.pallas_call(
        body,
        grid=(tokens // step,),
        in_specs=[pl.BlockSpec((step, wide), lambda i: (i, 0)), whole(down.shape)]
        + [HELD] * len(others),
        out_specs=pl.BlockSpec((step, model), lambda i: (i, 0)),
        out_shape=shaped((tokens, model), BF16),
        cost_estimate=takes(2.45), compiler_params=ROOMY,
    )(activation, down, *others)


def join_rows(ring, mine, theirs):
    rows, wide = mine.shape

    def body(table, mine_ref, theirs_ref, out_ref, sems):
        core = table[ring.core_at]
        copies = []
        for n, (place, ref) in enumerate(((core, mine_ref), (1 - core, theirs_ref))):
            target = out_ref.at[pl.ds(pl.multiple_of(place * rows, 16), rows)]
            copies.append(pltpu.make_async_copy(ref, target, sems.at[n]))
        for copy in copies:
            copy.start()
        for copy in copies:
            copy.wait()

    return pl.pallas_call(
        body,
        grid_spec=pltpu.PrefetchScalarGridSpec(
            num_scalar_prefetch=1,
            grid=(1,),
            in_specs=[HELD] * 2,
            out_specs=whole((2 * rows, wide)),
            scratch_shapes=[pltpu.SemaphoreType.DMA((2,))],
        ),
        out_shape=shaped((2 * rows, wide), mine.dtype),
        cost_estimate=takes(4), compiler_params=ROOMY,
    )(ring.table, mine, theirs)


def feed_forward(ring, twos, cots, weights, down, others):
    chips = ring.chips
    tok, model = twos[0][2].shape
    _, _, half, wide = weights[0].shape
    steps = chips // 2
    chunk = 2 * tok
    count = len(twos)

    def body(table, *refs):
        two_refs, cot_refs = refs[:count], refs[count : 2 * count]
        weight_refs = refs[2 * count : 2 * count + 4]
        down_ref = refs[2 * count + 4]
        outs = refs[2 * count + 5 + len(others) :]
        act_ref, gate_ref, up_ref, grad_ref, two_out, cot_out = outs[:6]
        two_buf, cot_buf, weight_buf, down_buf, two_sems, cot_sems, weight_sems = outs[6:]
        step = pl.program_id(0)
        side = table[ring.side_at]
        moves = [pltpu.make_async_copy(down_ref, down_buf, weight_sems.at[8])]
        for n, ref in enumerate(weight_refs):
            place = side if n % 2 == 0 else 1 - side
            for part in range(2):
                target = weight_buf.at[part, pl.ds(n // 2 * chips, chips), place]
                sem = weight_sems.at[2 * n + part]
                moves.append(pltpu.make_async_copy(ref.at[:, part], target, sem))
        blocks = fetches(twos, two_refs, two_buf, two_sems)
        blocks += fetches(cots, cot_refs, cot_buf, cot_sems)

        @pl.when(step == 0)
        def _():
            for move in moves + blocks:
                move.start()
            for move in moves:
                move.wait()

        for at in range(steps):

            @pl.when(step == at)
            def _():
                for (slot, _, _), block in zip(twos + cots, blocks):
                    if slot // 2 == at:
                        block.wait()

        two = two_buf[pl.ds(step * 2, 2)].reshape(chunk, model)
        cot = cot_buf[pl.ds(step * 2, 2)].reshape(chunk, model)
        two_out[...] = two
        cot_out[...] = cot
        gate_weight = weight_buf[0].reshape(model, wide)
        up_weight = weight_buf[1].reshape(model, wide)
        gate = dot(two, gate_weight)
        upward = dot(two, up_weight)
        grad = dot(cot, down_buf[...], LAST)
        sigma = jax.nn.sigmoid(gate)
        act_ref[...] = (gate * sigma * upward).astype(BF16)
        grad_gate = (grad * upward * (sigma * (1.0 + gate * (1.0 - sigma)))).astype(BF16)
        grad_up = (grad * gate * sigma).astype(BF16)
        gate_ref[...] = grad_gate
        up_ref[...] = grad_up
        grad_two = dot(grad_gate, gate_weight, LAST) + dot(grad_up, up_weight, LAST)
        grad_ref[...] = grad_two.astype(BF16)

    def out(width):
        return pl.BlockSpec((chunk, width), lambda i, _: (i, 0))

    widths = (wide, wide, wide, model, model, model)
    kinds = (BF16,) * 6
    return pl.pallas_call(
        body,
        grid_spec=pltpu.PrefetchScalarGridSpec(
            num_scalar_prefetch=1,
            grid=(steps,),
            in_specs=[HELD] * (2 * count + 5 + len(others)),
            out_specs=[out(w) for w in widths],
            scratch_shapes=[
                pltpu.VMEM((chips, tok, model), BF16),
                pltpu.VMEM((chips, tok, model), BF16),
                pltpu.VMEM((2, 2 * chips, 2, half, wide), BF16),
                pltpu.VMEM(down.shape, BF16),
                pltpu.SemaphoreType.DMA((count,)),
                pltpu.SemaphoreType.DMA((count,)),
                pltpu.SemaphoreType.DMA((9,)),
            ],
        ),
        out_shape=[shaped((chips * tok, w), kind) for w, kind in zip(widths, kinds)],
        cost_estimate=takes(28), compiler_params=ROOMY,
    )(
        ring.table,
        *[piece for _, _, piece in twos],
        *[piece for _, _, piece in cots],
        *weights,
        down,
        *others,
    )


def load_window(table, at, own_ref, other_ref, window, rows):
    chips = own_ref.shape[0]
    for b in range(window.shape[0] // rows):
        place = table[at + b]
        target = window.at[b * rows : (b + 1) * rows, :]

        @pl.when(place < chips)
        def _():
            target[...] = own_ref[place]

        @pl.when(place >= chips)
        def _():
            target[...] = other_ref[place - chips]


def allowed_pairs(first_ref, reach, keys, rows):
    key = lax.broadcasted_iota(jnp.int32, (keys, rows), 0)
    token = lax.broadcasted_iota(jnp.int32, (keys, rows), 1)
    allowed = (key >= first_ref[...]) & (key <= token + reach)
    return jnp.concatenate([allowed, allowed], 1)


def stacked(block, low_side):
    turned = pltpu.roll(block, HEAD_DIM, 1)
    low = lane_low(block.shape)
    if low_side:
        one, two = jnp.where(low, block, 0.0), jnp.where(low, turned, 0.0)
    else:
        one, two = jnp.where(low, 0.0, turned), jnp.where(low, 0.0, block)
    return jnp.concatenate([one, two], 0).astype(BF16)


def attend_kernel(
    ring, table, proj_ref, own_ref, other_ref, first_ref, cos_ref, sin_ref, q_ref, out_ref, log_ref, window
):
    rows = proj_ref.shape[0]
    keys = window.shape[0]

    @pl.when(pl.program_id(1) == 0)
    def _():
        load_window(table, ring.window, own_ref, other_ref, window, rows)

    block = proj_ref[...]
    block = block * cos_ref[...] + rotated(block) * sin_ref[...]
    q_ref[...] = block.astype(BF16)
    queries = stacked(block, True)
    score = dot(window[...], queries, LAST) * SCALE
    allowed = allowed_pairs(first_ref, keys - rows, keys, rows)
    score = jnp.where(allowed, score, -jnp.inf)
    top = jnp.max(score, 0, keepdims=True)
    expon = jnp.exp(score - top)
    total = jnp.sum(expon, 0, keepdims=True)
    log_ref[0] = top + jnp.log(total)
    probs = (expon * (1.0 / total)).astype(BF16)
    out = dot(probs, window[...], FIRST)
    one, two = out[:rows], out[rows:]
    out_ref[...] = jnp.where(lane_low(one.shape), pltpu.roll(one, HEAD_DIM, 1), two).astype(BF16)


def attend_back_kernel(
    ring,
    table,
    q_ref,
    grad_ref,
    att_ref,
    log_ref,
    own_ref,
    other_ref,
    first_ref,
    cos_ref,
    sin_ref,
    gq_ref,
    gown_ref,
    gother_ref,
    window,
    total,
):
    rows = q_ref.shape[0]
    keys = window.shape[0]
    chips = own_ref.shape[0]
    step = pl.program_id(1)

    @pl.when(step == 0)
    def _():
        load_window(table, ring.window, own_ref, other_ref, window, rows)
        total[...] = jnp.zeros_like(total)

    grad = grad_ref[...].astype(F32)
    queries = stacked(q_ref[...].astype(F32), True)
    grads = stacked(grad, False)
    product = jnp.transpose(grad * att_ref[...].astype(F32))
    delta = jnp.concatenate(
        [
            jnp.sum(product[:HEAD_DIM], 0, keepdims=True),
            jnp.sum(product[HEAD_DIM:], 0, keepdims=True),
        ],
        1,
    )
    score = dot(window[...], queries, LAST) * SCALE
    allowed = allowed_pairs(first_ref, keys - rows, keys, rows)
    probs = jnp.where(allowed, jnp.exp(score - log_ref[0]), 0.0)
    grad_probs = dot(window[...], grads, LAST)
    grad_scores = (probs * (grad_probs - delta) * SCALE).astype(BF16)
    total[...] += dot(grad_scores, queries) + dot(probs.astype(BF16), grads)
    grad_queries = dot(grad_scores, window[...], FIRST)
    one, two = grad_queries[:rows], grad_queries[rows:]
    block = jnp.where(lane_low(one.shape), one, pltpu.roll(two, HEAD_DIM, 1))
    gq_ref[...] = (block * cos_ref[...] - rotated(block) * sin_ref[...]).astype(BF16)

    @pl.when(step == pl.num_programs(1) - 1)
    def _():
        gown_ref[...] = jnp.zeros_like(gown_ref)
        gother_ref[...] = jnp.zeros_like(gother_ref)
        for b in range(keys // rows):
            place = table[ring.window + b]
            block = total[b * rows : (b + 1) * rows, :]

            @pl.when(place < chips)
            def _():
                gown_ref[place] = block.astype(BF16)

            @pl.when(place >= chips)
            def _():
                gother_ref[place - chips] = block.astype(BF16)


def attention_call(kernel, ring, groups, ins, outs, scratch, before, others, cost):
    start, stop = groups
    inner = HEADS // KV_HEADS // 2
    given = len(ins)

    def body(table, *refs):
        kernel(ring, table, *refs[:given], *refs[given + len(before) + len(others) :])

    def spec(entry):
        shape, place = entry
        return pl.BlockSpec(
            shape, lambda g, i, table: place(g + start, (g + start) * inner + i, table)
        )

    return pl.pallas_call(
        body,
        grid_spec=pltpu.PrefetchScalarGridSpec(
            num_scalar_prefetch=1,
            grid=(stop - start, inner),
            in_specs=[spec(entry) for _, entry in ins] + [HELD] * (len(before) + len(others)),
            out_specs=[spec(entry) for _, entry in outs],
            scratch_shapes=scratch,
        ),
        out_shape=[shape for shape, _ in outs],
        input_output_aliases={1 + given + k: k for k in range(len(before))},
        cost_estimate=takes(cost), compiler_params=ROOMY,
    )(ring.table, *[value for value, _ in ins], *before, *others)


def attention_specs(ring, rows):
    return (
        ((rows, LANES), lambda g, pair, table: (0, pair)),
        ((rows, LANES), lambda g, pair, table: (0, table[ring.place_near + pair])),
        ((1, 1, 2 * rows), lambda g, pair, table: (pair, 0, 0)),
        ((ring.chips, rows, LANES), lambda g, pair, table: (0, 0, g)),
        ((1, rows), lambda g, pair, table: (0, 0)),
        ((rows, LANES), lambda g, pair, table: (0, 0)),
    )


def attend(ring, groups, others, keys, proj, own, other, first, cosine, sine, before=()):
    rows = proj.shape[0]
    pairs = HEADS // 2
    block, near_block, log_block, kv_block, row, table = attention_specs(ring, rows)
    return attention_call(
        attend_kernel,
        ring,
        groups,
        [(proj, block), (own, kv_block), (other, kv_block)]
        + [(first, row), (cosine, table), (sine, table)],
        [
            (shaped((rows, pairs * LANES), BF16), block),
            (shaped((rows, pairs * LANES), BF16), near_block),
            (shaped((pairs, 1, 2 * rows), F32), log_block),
        ],
        [pltpu.VMEM((keys, LANES), BF16)],
        before,
        others,
        14,
    )


def attend_back(
    ring, groups, others, keys, queries, grad, attended, logs, own, other, first, cosine, sine, before=()
):
    rows = queries.shape[0]
    block, near_block, log_block, kv_block, row, table = attention_specs(ring, rows)
    return attention_call(
        attend_back_kernel,
        ring,
        groups,
        [
            (queries, block),
            (grad, near_block),
            (attended, near_block),
            (logs, log_block),
            (own, kv_block),
            (other, kv_block),
            (first, row),
            (cosine, table),
            (sine, table),
        ],
        [
            (shaped(queries.shape, BF16), block),
            (shaped(own.shape, BF16), kv_block),
            (shaped(own.shape, BF16), kv_block),
        ],
        [pltpu.VMEM((keys, LANES), BF16), pltpu.VMEM((keys, LANES), F32)],
        before,
        others,
        5,
    )


def on_device(
    reps,
    shards,
    hidden_in,
    segments,
    cotangent,
    qkv_weight,
    out_weight,
    gate_up_weight,
    down_weight,
    attn_gain,
    ffn_gain,
):
    tok = hidden_in.shape[1]
    model = hidden_in.shape[2]
    rows, width = qkv_weight.shape
    blocks = min(REACH // tok, shards - 1) + 1
    ring = Ring(shards, blocks)
    chips = ring.chips
    middle = chips * rows
    ff = down_weight.shape[0] * shards
    wide = ff // chips
    half = rows // 2
    side = ring.side
    twin_map = [(i, i ^ 1) for i in range(reps)]
    side_groups = [list(range(s, reps, 2)) for s in range(2)]
    hidden, cot_local, seg_row = hidden_in[0], cotangent[0], segments[0]
    groups = ((0, KV_HEADS // 2), (KV_HEADS // 2, KV_HEADS))

    def twin(value):
        return lax.ppermute(value, "rep", twin_map)

    def rest_of_reps(value):
        if reps == 2:
            return value
        return lax.psum(value, "rep", axis_index_groups=side_groups)

    def over_reps(value):
        mine = rest_of_reps(value).astype(BF16)
        return mine.astype(F32) + twin(mine).astype(F32)

    mine = cut_columns(ring, gate_up_weight, wide)
    mine = lax.all_to_all(
        mine, "shard", 0, 0, axis_index_groups=ring.core_groups, tiled=True
    )

    packed = pack_weight(qkv_weight, attn_gain, ffn_gain)
    qkv_pieces, qkv_marks = ring.gather_both(packed)

    offset = ring.index * tok
    local_seg = lax.dynamic_slice_in_dim(seg_row, offset, tok)
    starts = jnp.sum((seg_row[None, :] < local_seg[:, None]).astype(jnp.int32), 1)
    positions = offset + jnp.arange(tok, dtype=jnp.int32) - starts
    freqs = jnp.exp(
        (jnp.arange(LANES) % (HEAD_DIM // 2)).astype(F32) * (-2.0 * math.log(10000.0) / HEAD_DIM)
    )
    angles = positions.astype(F32)[:, None] * freqs[None, :]
    cosine, sine = jnp.cos(angles), jnp.sin(angles)
    first = (starts - offset + (blocks - 1) * tok)[None, :]

    proj, kv_local, input_one, factor_one, gains = project(
        ring, hidden, cosine, sine, qkv_pieces, width, (mine,)
    )
    kv_own = stack_blocks(ring, ring.gather(kv_local), ())
    kv_other = ring.swap(kv_own)
    out_pieces, out_marks = ring.gather_both(
        after(out_weight, *qkv_marks[-2:]), {2: (kv_local,), 3: (kv_own,)}
    )
    theirs = twin(mine)
    cots = ring.gather(after(cot_local, *out_marks[-2:]))
    tables = (kv_own, kv_other, first, cosine, sine)
    keys = blocks * tok
    kept = attend(ring, groups[0], (), keys, proj, *tables)
    kept = attend(ring, groups[1], tuple(out_marks[5:7]), keys, proj, *tables, kept)
    queries, attended, logs = kept
    residual, factor_two, input_two = project_out(ring, attended, hidden, gains, out_pieces, ())

    twos = ring.gather(input_two)
    weights = (mine, theirs, ring.swap(mine), ring.swap(theirs))
    down = join_rows(ring, down_weight, ring.swap(down_weight))
    activation, grad_gate, grad_up, grad_two, two, cot = feed_forward(
        ring, twos, cots, weights, down, ()
    )
    gu_gives = give_terms(ring, two, (grad_gate, grad_up))
    gu_gots = [ring.swap(v) for v in gu_gives]
    gu_keep, gu_give = halve_terms(ring, two, (grad_gate, grad_up), gu_gots)
    ffn_term = down_project(activation, down, (gu_give,))
    gu_recv = twin(gu_give)
    gu_sum = rest_of_reps(gu_keep + gu_recv.astype(F32)).astype(BF16)
    gu_sum = lax.all_to_all(
        gu_sum, "shard", 0, 0, axis_index_groups=ring.core_groups, tiled=True
    )
    grad_two, two_marks = ring.scatter(
        grad_two, lambda step, _: {3: (gu_give,), 4: (ffn_term,)}.get(step)
    )
    down_keep, down_give = down_terms(ring, activation, cot, two_marks[3])
    down_keep = rest_of_reps(down_keep + ring.swap(down_give).astype(F32)).astype(BF16)
    down_recv = twin(down_keep)

    grad_residual, residual_half, grad_attended, gain_two_term = back_out(
        ring, grad_two, residual, factor_two, gains, cot_local, out_pieces, (gu_recv,)
    )
    (out_give,) = give_terms(ring, attended, (residual_half,))
    out_got = ring.swap(out_give)
    out_keep, out_send = halve_terms(ring, attended, (residual_half,), (out_got,))
    out_recv = twin(out_send)
    tables = (logs, kv_own, kv_other, first, cosine, sine)
    ffn_out, ffn_marks = ring.scatter(ffn_term, lambda step, _: two_marks[-1] if step == 1 else ())
    back = attend_back(
        ring, groups[0], (), keys, queries, grad_attended, attended, *tables
    )
    back = attend_back(
        ring,
        groups[1],
        (*ffn_marks[0], gu_sum, out_send),
        keys,
        queries,
        grad_attended,
        attended,
        *tables,
        back,
    )
    grad_queries, kv_keep, kv_give = back
    gu_other = twin(gu_sum)
    (query_give,) = give_terms(ring, input_one, (grad_queries,))
    query_got = ring.swap(query_give)
    kv_got = ring.swap(after(kv_give, query_give))
    kv_term = (kv_keep.astype(F32) + kv_got.astype(F32)).astype(BF16)
    merged = merge_terms(ring, input_one, grad_queries, query_got, out_keep, out_recv)
    merged_sum, merged_marks = ring.scatter(merged)

    def kv_ties(step, marks):
        return {3: (merged, *ffn_marks[2])}.get(step)

    grad_kv, kv_marks = ring.scatter(kv_term.reshape(chips * tok, -1), kv_ties)
    grad_kv = finish_kv(ring, grad_kv, cosine, sine, merged_marks[0])
    (kv_give,) = give_terms(ring, input_one, (grad_kv,))
    (kv_term,) = keep_terms(ring, input_one, (grad_kv,), (ring.swap(kv_give),))
    grad_hidden, gain_one_term = back_project(
        ring,
        grad_queries,
        grad_kv,
        hidden,
        factor_one,
        gains,
        grad_residual,
        qkv_pieces,
        width,
        (*merged_marks[1], *ffn_marks[3]),
    )
    gain_terms = jnp.concatenate([gain_one_term[:1], gain_two_term[:1]], 0)
    gain_terms = gain_terms[:, :middle] + ring.swap(gain_terms[:, middle:])
    below = gain_terms.reshape(2, chips, rows).transpose(1, 0, 2).reshape(chips, 1, 2 * rows)
    below = jnp.pad(below, ((0, 0), (0, 15), (0, kv_term.shape[1] - 2 * rows))).astype(BF16)
    parts = jnp.concatenate([kv_term.reshape(chips, rows, -1), below], 1)
    kv_sum, last_marks = ring.scatter(
        parts.reshape(chips * (rows + 16), -1),
        lambda step, _: {3: merged_marks[2]}.get(step),
    )
    kv_sum = over_reps(summed(kv_sum))
    merged_sum = rest_of_reps(summed(merged_sum)).astype(BF16)
    other = twin(merged_sum)
    grad_queries = merged_sum[:rows].astype(F32) + other[:rows].astype(F32)
    grad_qkv = jnp.concatenate([grad_queries, kv_sum[:rows]], 1)
    mine, theirs = merged_sum[rows:], other[rows:]
    grad_out = jnp.concatenate([pick(side, mine, theirs), pick(side, theirs, mine)], 0)
    hidden_out = (residual + summed((ffn_out[0], ffn_out[1], after(ffn_out[2], grad_kv)))).astype(BF16)
    grad_down = down_keep.astype(F32) + after(down_recv, *last_marks[1]).astype(F32)
    return (
        hidden_out[None],
        grad_hidden[None],
        grad_qkv,
        grad_out.astype(F32),
        join_columns(ring, gu_sum, gu_other, (grad_kv,)),
        grad_down,
        kv_sum[rows, :rows],
        kv_sum[rows, rows : 2 * rows],
    )


def solution(mesh):
    reps, shards = mesh.shape["rep"], mesh.shape["shard"]

    def layer(*args):
        return on_device(reps, shards, *args)

    return jax.shard_map(
        layer,
        mesh=mesh,
        in_specs=(
            P("rep", "shard", None),
            P("rep", None),
            P("rep", "shard", None),
            P("shard", None),
            P("shard", None),
            P("shard", None),
            P("shard", None),
            P("shard"),
            P("shard"),
        ),
        out_specs=(
            P("rep", "shard", None),
            P("rep", "shard", None),
            P("shard", None),
            P("shard", None),
            P("shard", None),
            P("shard", None),
            P("shard"),
            P("shard"),
        ),
        check_vma=False,
    )
```

```python
import math

import jax
import jax.numpy as jnp
import numpy as np
from jax import lax
from jax.experimental import pallas as pl
from jax.experimental.pallas import tpu as pltpu
from jax.sharding import PartitionSpec as P

HEADS = 32
KV_HEADS = 4
HEAD_DIM = 64
REACH = 1024
EPS = 1e-05
F32 = jnp.float32
BF16 = jnp.bfloat16
LANES = 128
SCALE = HEAD_DIM**-0.5
LIMIT = 58 * 1024 * 1024
ROOMY = pltpu.CompilerParams(vmem_limit_bytes=LIMIT)
HELD = pl.BlockSpec(memory_space=pl.ANY)


def takes(micros):
    return pl.CostEstimate(
        flops=int(micros * 1.1e9), bytes_accessed=int(micros * 3.3e6), transcendentals=0
    )


def dot(a, b, dims=((1,), (0,))):
    return lax.dot_general(a, b, (dims, ((), ())), preferred_element_type=F32)


LAST = ((1,), (1,))
FIRST = ((0,), (0,))


def pick(flag, one, other):
    return jnp.where(flag == 0, one, other)


class Ring:
    def __init__(self, size, window):
        self.size = size
        self.chips = chips = size // 2
        rows = chips // 2
        self.order = [2 * i for i in range(rows)] + [2 * i + 1 for i in reversed(range(rows))]
        self.place = [self.order.index(chip) for chip in range(chips)]
        self.half = chips // 2

        def turned(step):
            return [
                (s, self.order[(self.place[s // 2] + step) % chips] * 2 + s % 2)
                for s in range(size)
            ]

        self.ahead = turned(1)
        self.back = turned(-1)
        self.sibling = [(s, s ^ 1) for s in range(size)]
        self.core_groups = [list(range(core, size, 2)) for core in range(2)]
        self.near, self.place_near, self.cores, self.place_cores, self.window = (
            k * size for k in range(5)
        )
        self.core_at = self.window + window
        self.side_at = self.core_at + 1
        table = []
        for side in range(2):
            for s in range(size):
                chip, core = s // 2, s % 2
                at = self.place[chip]
                near = [
                    self.order[(at + j) % chips] * 2 + (core ^ other)
                    for other in range(2)
                    for j in range(chips)
                ]
                cores = [j * 2 + (core ^ other) for other in range(2) for j in range(chips)]
                place_near = [near.index(d) for d in range(size)]
                place_cores = [cores.index(d) for d in range(size)]
                seen = [place_near[(s + 1 - window + b) % size] for b in range(window)]
                table.append(near + place_near + cores + place_cores + seen + [core, side])
        self.index = lax.axis_index("shard")
        self.side = lax.axis_index("rep") % 2
        self.table = lax.dynamic_index_in_dim(
            jnp.asarray(np.array(table, np.int32)), self.side * size + self.index, 0, False
        )

    def swap(self, value):
        return lax.ppermute(value, "shard", self.sibling)

    def gather(self, block, ties=None):
        n, h = self.chips, block.shape[0] // 2
        cw = ccw = block
        found = [(0, 0, block)]
        for k in range(1, self.half):
            if ties and k in ties:
                cw, ccw = after(cw, *ties[k]), after(ccw, *ties[k])
            cw = lax.ppermute(cw, "shard", self.ahead)
            ccw = lax.ppermute(ccw, "shard", self.back)
            found += [(n - k, 0, cw), (k, 0, ccw)]
        top = lax.ppermute(cw[:h], "shard", self.ahead)
        low = lax.ppermute(ccw[h:], "shard", self.back)
        return found + [(self.half, 0, top), (self.half, h, low)]

    def gather_shared(self, mine, other, twin, ties=None):
        own = self.gather(mine, ties)
        found = [(k, row, 0, piece) for k, row, piece in own]
        found += [(k, row, 1, twin(piece) if k else other) for k, row, piece in own]
        found += [(k + self.chips, row, part, self.swap(piece)) for k, row, part, piece in found]
        return found, [piece for _, _, piece in own]

    def scatter(self, parts, ties=None):
        n, m = self.chips, self.half
        rows = parts.shape[0] // n
        h = rows // 2
        cw, ccw = parts[m * rows : m * rows + h], parts[m * rows + h : (m + 1) * rows]
        marks = []
        for k in range(m - 1, -1, -1):
            if ties:
                others = ties(m - k, marks)
                if others:
                    cw, ccw = after(cw, *others), after(ccw, *others)
            cw = lax.ppermute(cw, "shard", self.ahead)
            ccw = lax.ppermute(ccw, "shard", self.back)
            marks.append((cw, ccw))
            if k > 0:
                cw, ccw = add_step(parts, rows, k, n - k, cw, ccw)
        return (parts, cw, ccw), marks


def add_step(parts, rows, ahead, back, cw, ccw):
    width = parts.shape[1]
    got = cw.shape[0]

    def body(ahead_ref, back_ref, cw_ref, ccw_ref, one_ref, two_ref):
        if got < rows:
            one_ref[got:] = ahead_ref[got:]
            two_ref[: rows - ccw.shape[0]] = back_ref[: rows - ccw.shape[0]]
        last = rows - ccw.shape[0]
        one_ref[:got] = (ahead_ref[:got].astype(F32) + cw_ref[...].astype(F32)).astype(BF16)
        two_ref[last:] = (back_ref[last:].astype(F32) + ccw_ref[...].astype(F32)).astype(BF16)

    return pl.pallas_call(
        body,
        grid=(1,),
        in_specs=[
            pl.BlockSpec((rows, width), lambda _: (ahead, 0)),
            pl.BlockSpec((rows, width), lambda _: (back, 0)),
            whole(cw.shape),
            whole(ccw.shape),
        ],
        out_specs=[whole((rows, width))] * 2,
        out_shape=[shaped((rows, width), BF16)] * 2,
        cost_estimate=takes(0.875), compiler_params=ROOMY,
    )(parts, parts, cw, ccw)


def summed(sums):
    parts, cw, ccw = sums
    return parts[: cw.shape[0]].astype(F32) + cw.astype(F32) + ccw.astype(F32)


def whole(shape):
    return pl.BlockSpec(shape, lambda *_: (0,) * len(shape))


def shaped(shape, kind):
    return jax.ShapeDtypeStruct(shape, kind)


def call(kernel, table, ins, outs, pieces=(), scratch=(), others=(), cost=3):
    count, more, extra = len(ins), len(pieces), len(others)

    def body(table_ref, *refs):
        behind = count + more + extra
        kernel(
            table_ref,
            refs[:count],
            refs[count : count + more],
            refs[behind : behind + len(outs)],
            refs[behind + len(outs) :],
        )

    return pl.pallas_call(
        body,
        grid_spec=pltpu.PrefetchScalarGridSpec(
            num_scalar_prefetch=1,
            grid=(1,),
            in_specs=[whole(v.shape) for v in ins] + [HELD] * (more + extra),
            out_specs=[whole(v.shape) for v in outs],
            scratch_shapes=list(scratch),
        ),
        out_shape=list(outs),
        compiler_params=ROOMY,
        cost_estimate=takes(cost),
    )(table, *ins, *pieces, *others)


def after(value, *others):
    return pl.pallas_call(
        lambda *refs: None,
        in_specs=[HELD] * (1 + len(others)),
        out_specs=HELD,
        out_shape=shaped(value.shape, value.dtype),
        input_output_aliases={0: 0},
    )(value, *others)


def fetches(pieces, refs, buffer, sems):
    return [
        pltpu.make_async_copy(
            ref, buffer.at[k, pl.ds(row, ref.shape[0])], sems.at[n]
        )
        for n, ((k, row, _), ref) in enumerate(zip(pieces, refs))
    ]


def shared_fetches(side, pieces, refs, buffer, sems):
    copies = []
    for n, ((k, row, part, _), ref) in enumerate(zip(pieces, refs)):
        rows, width = ref.shape
        start = pl.multiple_of((side if part == 0 else 1 - side) * width, LANES)
        target = buffer.at[k, pl.ds(row, rows), pl.ds(start, width)]
        copies.append(pltpu.make_async_copy(ref, target, sems.at[n]))
    return copies


def block_at(place):
    return pl.ds(pl.multiple_of(place * LANES, LANES), LANES)


def columns(block):
    return slice(block * LANES, (block + 1) * LANES)


def lane_low(shape):
    return lax.broadcasted_iota(jnp.int32, shape, len(shape) - 1) % LANES < HEAD_DIM


def rotated(values):
    quarter = HEAD_DIM // 2
    first = lax.broadcasted_iota(jnp.int32, values.shape, 1) % HEAD_DIM < quarter
    return jnp.where(
        first, -pltpu.roll(values, LANES - quarter, 1), pltpu.roll(values, quarter, 1)
    )


def pack_weight(weight, gain_one, gain_two, side):
    rows, width = weight.shape
    half = packed_width(width) // 2

    def body(side_ref, weight_ref, one_ref, two_ref, mine_ref, other_ref):
        lane = lax.broadcasted_iota(jnp.int32, (rows, LANES), 1)
        block = jnp.where(lane == 0, one_ref[...], jnp.where(lane == 1, two_ref[...], 0.0))
        first = side_ref[0] == 0
        tail = width - half

        def put(start, stop, left, right):
            mine_ref[:, start:stop] = jnp.where(first, left, right)
            other_ref[:, start:stop] = jnp.where(first, right, left)

        put(0, tail, weight_ref[:, :tail], weight_ref[:, half:])
        put(tail, tail + LANES, weight_ref[:, tail : tail + LANES], block.astype(BF16))
        if tail + LANES < half:
            left = weight_ref[:, tail + LANES : half]
            put(tail + LANES, half, left, jnp.zeros_like(left))

    gains = [g.astype(F32)[:, None] for g in (gain_one, gain_two)]
    return pl.pallas_call(
        body,
        grid_spec=pltpu.PrefetchScalarGridSpec(
            num_scalar_prefetch=1,
            grid=(1,),
            in_specs=[whole(weight.shape)] + [whole((rows, 1))] * 2,
            out_specs=[whole((rows, half))] * 2,
        ),
        out_shape=[shaped((rows, half), BF16)] * 2,
        cost_estimate=takes(3), compiler_params=ROOMY,
    )(side.astype(jnp.int32)[None], weight, *gains)


def packed_width(width):
    return -(-(width + LANES) // (2 * LANES)) * 2 * LANES


def project(ring, hidden, cosine, sine, pieces, width, others):
    size = ring.size
    rows, model = hidden.shape
    qsize = HEADS * HEAD_DIM
    step = 2 * LANES

    def kernel(table, ins, refs, outs, scratch):
        hidden_ref, cos_ref, sin_ref = ins
        q_ref, kv_ref, input_ref, factor_ref, gain_ref = outs
        buffer, sems = scratch
        copies = shared_fetches(table[ring.side_at], pieces, refs, buffer, sems)
        for copy in copies:
            copy.start()
        values = hidden_ref[...].astype(F32)
        factor = lax.rsqrt(jnp.mean(values * values, -1, keepdims=True) + EPS)
        factor_ref[...] = jnp.broadcast_to(factor, factor_ref.shape)
        for copy in copies:
            copy.wait()
        for k in range(size):
            gains = jnp.transpose(buffer[k, :, width : width + LANES].astype(F32))
            gain_ref[:, columns(k)] = gains[:8]
            part = hidden_ref[:, block_at(table[ring.near + k])].astype(F32)
            input_ref[:, columns(k)] = (part * factor * gains[:1]).astype(BF16)
        inputs = input_ref[...]
        for start in range(0, qsize, step):
            weights = buffer[:, :, start : start + step].reshape(model, step)
            q_ref[:, start : start + step] = dot(inputs, weights)
        weights = buffer[:, :, qsize:width].reshape(model, width - qsize)
        proj = dot(inputs, weights)
        for pair in range(KV_HEADS // 2):
            keys = proj[:, columns(pair)]
            keys = keys * cos_ref[...] + rotated(keys) * sin_ref[...]
            heads = proj[:, columns(KV_HEADS // 2 + pair)]
            low = lane_low(keys.shape)
            one = jnp.where(low, keys, pltpu.roll(heads, HEAD_DIM, 1))
            two = jnp.where(low, pltpu.roll(keys, HEAD_DIM, 1), heads)
            kv_ref[:, columns(2 * pair)] = one.astype(BF16)
            kv_ref[:, columns(2 * pair + 1)] = two.astype(BF16)

    return call(
        kernel,
        ring.table,
        [hidden, cosine, sine],
        [
            shaped((rows, qsize), F32),
            shaped((rows, KV_HEADS * LANES), BF16),
            shaped((rows, model), BF16),
            shaped((rows, LANES), F32),
            shaped((8, model), F32),
        ],
        [piece for *_, piece in pieces],
        [
            pltpu.VMEM((size, rows, packed_width(width)), BF16),
            pltpu.SemaphoreType.DMA((len(pieces),)),
        ],
        others,
        9,
    )


def stack_blocks(ring, pieces, others):
    rows, width = pieces[0][2].shape

    def body(*refs):
        copies = fetches(pieces, refs[: len(pieces)], refs[-2], refs[-1])
        for copy in copies:
            copy.start()
        for copy in copies:
            copy.wait()

    return pl.pallas_call(
        body,
        in_specs=[HELD] * (len(pieces) + len(others)),
        out_specs=pl.BlockSpec(memory_space=pltpu.VMEM),
        out_shape=shaped((ring.chips, rows, width), pieces[0][2].dtype),
        scratch_shapes=[pltpu.SemaphoreType.DMA((len(pieces),))],
        cost_estimate=takes(2.5), compiler_params=ROOMY,
    )(*[piece for _, _, piece in pieces], *others)


def project_out(ring, attended, hidden, gains, pieces, others):
    size = ring.size
    rows, model = hidden.shape
    step = 2 * LANES

    def kernel(table, ins, refs, outs, scratch):
        att_ref, hidden_ref, gain_ref = ins
        residual_ref, factor_ref, input_ref = outs
        buffer, sems = scratch
        copies = shared_fetches(table[ring.side_at], pieces, refs, buffer, sems)
        for copy in copies:
            copy.start()
        for copy in copies:
            copy.wait()
        inputs = att_ref[...]
        squares = jnp.zeros((rows, 1), F32)
        for start in range(0, model, step):
            weights = buffer[:, :, start : start + step].reshape(model, step)
            part = hidden_ref[:, start : start + step].astype(F32) + dot(inputs, weights)
            residual_ref[:, start : start + step] = part
            squares += jnp.sum(part * part, -1, keepdims=True)
        factor = lax.rsqrt(squares * (1.0 / model) + EPS)
        factor_ref[...] = jnp.broadcast_to(factor, factor_ref.shape)
        for k in range(size):
            device = table[ring.cores + k]
            gain = gain_ref[1:2, block_at(table[ring.place_near + device])]
            part = residual_ref[:, block_at(device)] * factor
            input_ref[:, columns(k)] = (part * gain).astype(BF16)

    return call(
        kernel,
        ring.table,
        [attended, hidden, gains],
        [shaped((rows, model), F32), shaped((rows, LANES), F32), shaped((rows, model), BF16)],
        [piece for *_, piece in pieces],
        [
            pltpu.VMEM((size, rows, model), BF16),
            pltpu.SemaphoreType.DMA((len(pieces),)),
        ],
        others,
        8,
    )


def back_out(ring, sums, residual, factor, gains, cot, pieces, others):
    size = ring.size
    rows, model = residual.shape

    def kernel(table, ins, refs, outs, scratch):
        own_ref, cw_ref, ccw_ref, residual_ref, factor_ref, gain_ref, cot_ref = ins
        grad_res_ref, half_ref, att_ref, term_ref = outs
        buffer, sems, total = scratch
        copies = shared_fetches(table[ring.side_at], pieces, refs, buffer, sems)
        for copy in copies:
            copy.start()
        factor = factor_ref[...]
        mean = jnp.zeros((rows, 1), F32)
        for d in range(size):
            place, source = (
                block_at(table[order + d]) for order in (ring.place_near, ring.place_cores)
            )
            grad = sum(ref[:, source].astype(F32) for ref in (own_ref, cw_ref, ccw_ref))
            total[:, columns(d)] = grad
            normed = residual_ref[:, columns(d)] * factor
            product = grad * normed
            term_ref[:, place] = jnp.broadcast_to(
                jnp.sum(product, 0, keepdims=True), (8, LANES)
            )
            mean += jnp.sum(product * gain_ref[1:2, place], -1, keepdims=True)
        mean *= 1.0 / model
        for d in range(size):
            place = block_at(table[ring.place_near + d])
            grad = total[:, columns(d)] * gain_ref[1:2, place]
            normed = residual_ref[:, columns(d)] * factor
            back = cot_ref[:, columns(d)].astype(F32) + factor * (grad - normed * mean)
            grad_res_ref[:, columns(d)] = back
            half_ref[:, columns(d)] = back.astype(BF16)
        for copy in copies:
            copy.wait()
        halves = half_ref[...]
        for k in range(0, size, 2):
            weights = buffer[k : k + 2].reshape(2 * rows, model)
            att_ref[:, k * LANES : (k + 2) * LANES] = dot(halves, weights, LAST).astype(BF16)

    return call(
        kernel,
        ring.table,
        [sums[0][:rows], sums[1], sums[2], residual, factor, gains, cot],
        [
            shaped((rows, model), F32),
            shaped((rows, model), BF16),
            shaped((rows, model), BF16),
            shaped((8, model), F32),
        ],
        [piece for *_, piece in pieces],
        [
            pltpu.VMEM((size, rows, model), BF16),
            pltpu.SemaphoreType.DMA((len(pieces),)),
            pltpu.VMEM((rows, model), F32),
        ],
        others,
        3.5,
    )


def finish_kv(ring, sums, cosine, sine, others):
    def kernel(table, ins, refs, outs, scratch):
        own_ref, cw_ref, ccw_ref, cos_ref, sin_ref = ins
        grad = sum(ref[...].astype(F32) for ref in (own_ref, cw_ref, ccw_ref))
        for pair in range(KV_HEADS // 2):
            one = grad[:, columns(2 * pair)]
            two = grad[:, columns(2 * pair + 1)]
            low = lane_low(one.shape)
            keys = jnp.where(low, one, pltpu.roll(two, HEAD_DIM, 1))
            values = jnp.where(low, pltpu.roll(one, HEAD_DIM, 1), two)
            keys = keys * cos_ref[...] - rotated(keys) * sin_ref[...]
            outs[0][:, columns(pair)] = keys.astype(BF16)
            outs[0][:, columns(KV_HEADS // 2 + pair)] = values.astype(BF16)

    rows = sums[1].shape[0]
    return call(
        kernel,
        ring.table,
        [sums[0][:rows], sums[1], sums[2], cosine, sine],
        [shaped((rows, 2 * KV_HEADS * HEAD_DIM), BF16)],
        others=others,
    )[0]


def back_project(
    ring, grad_queries, grad_kv, hidden, factor, gains, grad_residual, pieces, width, others
):
    size = ring.size
    rows, model = hidden.shape
    qsize = grad_queries.shape[1]

    def kernel(table, ins, refs, outs, scratch):
        gq_ref, gkv_ref, hidden_ref, factor_ref, gain_ref, grad_res_ref = ins
        grad_ref, term_ref = outs
        buffer, sems, total = scratch
        copies = shared_fetches(table[ring.side_at], pieces, refs, buffer, sems)
        for copy in copies:
            copy.start()
        for copy in copies:
            copy.wait()
        queries, keys = gq_ref[...], gkv_ref[...]
        for k in range(0, size, 2):
            weights = buffer[k : k + 2].reshape(2 * rows, packed_width(width))
            total[:, k * LANES : (k + 2) * LANES] = dot(
                queries, weights[:, :qsize], LAST
            ) + dot(keys, weights[:, qsize:width], LAST)
        factor = factor_ref[...]
        mean = jnp.zeros((rows, 1), F32)
        for k in range(size):
            normed = hidden_ref[:, block_at(table[ring.near + k])].astype(F32) * factor
            product = total[:, columns(k)] * normed
            term_ref[:, columns(k)] = jnp.broadcast_to(
                jnp.sum(product, 0, keepdims=True), (8, LANES)
            )
            mean += jnp.sum(product * gain_ref[:1, columns(k)], -1, keepdims=True)
        mean *= 1.0 / model
        for k in range(size):
            place = block_at(table[ring.near + k])
            normed = hidden_ref[:, place].astype(F32) * factor
            scaled = total[:, columns(k)] * gain_ref[:1, columns(k)]
            back = grad_res_ref[:, place] + factor * (scaled - normed * mean)
            grad_ref[:, place] = back.astype(BF16)

    return call(
        kernel,
        ring.table,
        [grad_queries, grad_kv, hidden, factor, gains, grad_residual],
        [shaped((rows, model), BF16), shaped((8, model), F32)],
        [piece for *_, piece in pieces],
        [
            pltpu.VMEM((size, rows, packed_width(width)), BF16),
            pltpu.SemaphoreType.DMA((len(pieces),)),
            pltpu.VMEM((rows, model), F32),
        ],
        others,
        4.025,
    )


def cut_columns(ring, weight, wide):
    rows = weight.shape[0]
    half = rows // 2

    def kernel(table, ins, refs, outs, scratch):
        upper = table[ring.side_at] == 0
        for chip in range(ring.chips):
            for part in range(2):
                start = (part * ring.chips + chip) * wide
                block = ins[0][:, start : start + wide].astype(F32)
                outs[0][chip, part] = jnp.where(upper, block[:half], block[half:]).astype(BF16)

    return call(
        kernel, ring.table, [weight], [shaped((ring.chips, 2, half, wide), BF16)]
    )[0]


def join_columns(ring, mine, theirs, others):
    chips, parts, half, wide = mine.shape

    def kernel(table, ins, refs, outs, scratch):
        flip = table[ring.side_at] == 0
        for chip in range(chips):
            for part in range(parts):
                start = (part * chips + chip) * wide
                one, two = ins[0][chip, part].astype(F32), ins[1][chip, part].astype(F32)
                outs[0][:half, start : start + wide] = jnp.where(flip, one, two)
                outs[0][half:, start : start + wide] = jnp.where(flip, two, one)

    return call(
        kernel,
        ring.table,
        [mine, theirs],
        [shaped((2 * half, parts * chips * wide), F32)],
        others=others,
    )[0]


def step_columns(tokens):
    return (4 if tokens <= LANES else 2) * LANES


def give_terms(ring, inputs, grads, others=()):
    tokens, model = inputs.shape
    count, extra = len(grads), len(others)
    step = step_columns(tokens)
    steps = model // 2 // step

    def body(input_ref, *refs):
        for grad_ref, out_ref in zip(refs[:count], refs[count + extra :]):
            out_ref[...] = dot(input_ref[...], grad_ref[...], FIRST).astype(BF16)

    return pl.pallas_call(
        body,
        grid=(steps,),
        in_specs=[pl.BlockSpec((tokens, step), lambda i: (0, steps + i))]
        + [whole(g.shape) for g in grads]
        + [HELD] * extra,
        out_specs=[pl.BlockSpec((step, g.shape[1]), lambda i: (i, 0)) for g in grads],
        out_shape=[shaped((model // 2, g.shape[1]), BF16) for g in grads],
        cost_estimate=takes(2.1), compiler_params=ROOMY,
    )(inputs, *grads, *others)


def keep_terms(ring, inputs, grads, gots):
    tokens, model = inputs.shape
    count = len(grads)
    step = step_columns(tokens)

    def body(input_ref, *refs):
        for part in range(count):
            term = dot(input_ref[...], refs[part][...], FIRST)
            refs[2 * count + part][...] = (term + refs[count + part][...].astype(F32)).astype(BF16)

    blocks = [pl.BlockSpec((step, g.shape[1]), lambda i: (i, 0)) for g in grads]
    return pl.pallas_call(
        body,
        grid=(model // 2 // step,),
        in_specs=[pl.BlockSpec((tokens, step), lambda i: (0, i))]
        + [whole(g.shape) for g in grads]
        + blocks,
        out_specs=blocks,
        out_shape=[shaped((model // 2, g.shape[1]), BF16) for g in grads],
        cost_estimate=takes(1.75), compiler_params=ROOMY,
    )(inputs, *grads, *gots)


def merge_terms(ring, inputs, grads, got, halves, halves_got):
    tokens, model = inputs.shape
    chips, _, half, wide = halves.shape
    rows = model // ring.size
    step = step_columns(tokens)
    each = step // rows
    high = rows + half

    def body(input_ref, grad_ref, got_ref, half_ref, half_got_ref, out_ref):
        term = dot(input_ref[...], grad_ref[...], FIRST)
        for n in range(each):
            at = slice(n * rows, (n + 1) * rows)
            total = term[at] + got_ref[at].astype(F32)
            out_ref[n * high : n * high + rows] = total.astype(BF16)
            total = half_ref[n, 0] + half_got_ref[n, 0].astype(F32)
            out_ref[n * high + rows : (n + 1) * high] = total.astype(BF16)

    block = pl.BlockSpec((each, 1, half, wide), lambda i: (i, 0, 0, 0))
    return pl.pallas_call(
        body,
        grid=(chips // each,),
        in_specs=[
            pl.BlockSpec((tokens, step), lambda i: (0, i)),
            whole(grads.shape),
            pl.BlockSpec((step, wide), lambda i: (i, 0)),
            block,
            block,
        ],
        out_specs=pl.BlockSpec((each * high, wide), lambda i: (i, 0)),
        out_shape=shaped((chips * high, wide), BF16),
        cost_estimate=takes(2), compiler_params=ROOMY,
    )(inputs, grads, got, halves, halves_got)


def halve_terms(ring, inputs, grads, gots):
    tokens, model = inputs.shape
    chips, count = ring.chips, len(grads)
    rows, wide = model // ring.size, grads[0].shape[1]
    half = rows // 2
    step = step_columns(tokens)
    each = step // rows

    def body(table, input_ref, *refs):
        upper = table[ring.side_at] == 0
        keep_ref, give_ref = refs[2 * count :]
        for part in range(count):
            term = dot(input_ref[...], refs[part][...], FIRST)
            for n in range(each):
                at = slice(n * rows, (n + 1) * rows)
                total = term[at] + refs[count + part][at].astype(F32)
                keep_ref[n, part] = jnp.where(upper, total[:half], total[half:])
                give_ref[n, part] = jnp.where(upper, total[half:], total[:half]).astype(BF16)

    return pl.pallas_call(
        body,
        grid_spec=pltpu.PrefetchScalarGridSpec(
            num_scalar_prefetch=1,
            grid=(chips // each,),
            in_specs=[pl.BlockSpec((tokens, step), lambda i, _: (0, i))]
            + [whole(g.shape) for g in grads]
            + [pl.BlockSpec((step, wide), lambda i, _: (i, 0))] * count,
            out_specs=[pl.BlockSpec((each, count, half, wide), lambda i, _: (i, 0, 0, 0))] * 2,
        ),
        out_shape=[shaped((chips, count, half, wide), kind) for kind in (F32, BF16)],
        cost_estimate=takes(3.15), compiler_params=ROOMY,
    )(ring.table, inputs, *grads, *gots)


def down_terms(ring, activation, cot, others):
    tokens, wide = activation.shape
    model = cot.shape[1]
    step, half = 2 * LANES, wide // 2

    def body(table, act_ref, cot_ref, *refs):
        keep_ref, give_ref = refs[len(others) :]
        total = dot(act_ref[...], cot_ref[...], FIRST)
        first = table[ring.core_at] == 0
        keep_ref[...] = jnp.where(first, total[:half], total[half:])
        give_ref[...] = jnp.where(first, total[half:], total[:half]).astype(BF16)

    return pl.pallas_call(
        body,
        grid_spec=pltpu.PrefetchScalarGridSpec(
            num_scalar_prefetch=1,
            grid=(model // step,),
            in_specs=[whole(activation.shape), pl.BlockSpec((tokens, step), lambda i, _: (0, i))]
            + [HELD] * len(others),
            out_specs=[pl.BlockSpec((half, step), lambda i, _: (0, i))] * 2,
        ),
        out_shape=[shaped((half, model), kind) for kind in (F32, BF16)],
        cost_estimate=takes(3.5), compiler_params=ROOMY,
    )(ring.table, activation, cot, *others)


def down_project(activation, down, others):
    tokens, wide = activation.shape
    model = down.shape[1]
    step = 2 * LANES

    def body(act_ref, down_ref, *refs):
        refs[-1][...] = dot(act_ref[...], down_ref[...]).astype(BF16)

    return pl.pallas_call(
        body,
        grid=(tokens // step,),
        in_specs=[pl.BlockSpec((step, wide), lambda i: (i, 0)), whole(down.shape)]
        + [HELD] * len(others),
        out_specs=pl.BlockSpec((step, model), lambda i: (i, 0)),
        out_shape=shaped((tokens, model), BF16),
        cost_estimate=takes(2.45), compiler_params=ROOMY,
    )(activation, down, *others)


def join_rows(ring, mine, theirs):
    rows, wide = mine.shape

    def body(table, mine_ref, theirs_ref, out_ref, sems):
        core = table[ring.core_at]
        copies = []
        for n, (place, ref) in enumerate(((core, mine_ref), (1 - core, theirs_ref))):
            target = out_ref.at[pl.ds(pl.multiple_of(place * rows, 16), rows)]
            copies.append(pltpu.make_async_copy(ref, target, sems.at[n]))
        for copy in copies:
            copy.start()
        for copy in copies:
            copy.wait()

    return pl.pallas_call(
        body,
        grid_spec=pltpu.PrefetchScalarGridSpec(
            num_scalar_prefetch=1,
            grid=(1,),
            in_specs=[HELD] * 2,
            out_specs=whole((2 * rows, wide)),
            scratch_shapes=[pltpu.SemaphoreType.DMA((2,))],
        ),
        out_shape=shaped((2 * rows, wide), mine.dtype),
        cost_estimate=takes(4), compiler_params=ROOMY,
    )(ring.table, mine, theirs)


def feed_forward(ring, twos, cots, weights, down, others):
    chips = ring.chips
    tok, model = twos[0][2].shape
    _, _, half, wide = weights[0].shape
    steps = chips // 2
    chunk = 2 * tok
    count = len(twos)

    def body(table, *refs):
        two_refs, cot_refs = refs[:count], refs[count : 2 * count]
        weight_refs = refs[2 * count : 2 * count + 4]
        down_ref = refs[2 * count + 4]
        outs = refs[2 * count + 5 + len(others) :]
        act_ref, gate_ref, up_ref, grad_ref, two_out, cot_out = outs[:6]
        two_buf, cot_buf, weight_buf, down_buf, two_sems, cot_sems, weight_sems = outs[6:]
        step = pl.program_id(0)
        side = table[ring.side_at]
        moves = [pltpu.make_async_copy(down_ref, down_buf, weight_sems.at[8])]
        for n, ref in enumerate(weight_refs):
            place = side if n % 2 == 0 else 1 - side
            for part in range(2):
                target = weight_buf.at[part, pl.ds(n // 2 * chips, chips), place]
                sem = weight_sems.at[2 * n + part]
                moves.append(pltpu.make_async_copy(ref.at[:, part], target, sem))
        blocks = fetches(twos, two_refs, two_buf, two_sems)
        blocks += fetches(cots, cot_refs, cot_buf, cot_sems)

        @pl.when(step == 0)
        def _():
            for move in moves + blocks:
                move.start()
            for move in moves:
                move.wait()

        for at in range(steps):

            @pl.when(step == at)
            def _():
                for (slot, _, _), block in zip(twos + cots, blocks):
                    if slot // 2 == at:
                        block.wait()

        two = two_buf[pl.ds(step * 2, 2)].reshape(chunk, model)
        cot = cot_buf[pl.ds(step * 2, 2)].reshape(chunk, model)
        two_out[...] = two
        cot_out[...] = cot
        gate_weight = weight_buf[0].reshape(model, wide)
        up_weight = weight_buf[1].reshape(model, wide)
        gate = dot(two, gate_weight)
        upward = dot(two, up_weight)
        grad = dot(cot, down_buf[...], LAST)
        sigma = jax.nn.sigmoid(gate)
        act_ref[...] = (gate * sigma * upward).astype(BF16)
        grad_gate = (grad * upward * (sigma * (1.0 + gate * (1.0 - sigma)))).astype(BF16)
        grad_up = (grad * gate * sigma).astype(BF16)
        gate_ref[...] = grad_gate
        up_ref[...] = grad_up
        grad_two = dot(grad_gate, gate_weight, LAST) + dot(grad_up, up_weight, LAST)
        grad_ref[...] = grad_two.astype(BF16)

    def out(width):
        return pl.BlockSpec((chunk, width), lambda i, _: (i, 0))

    widths = (wide, wide, wide, model, model, model)
    kinds = (BF16,) * 6
    return pl.pallas_call(
        body,
        grid_spec=pltpu.PrefetchScalarGridSpec(
            num_scalar_prefetch=1,
            grid=(steps,),
            in_specs=[HELD] * (2 * count + 5 + len(others)),
            out_specs=[out(w) for w in widths],
            scratch_shapes=[
                pltpu.VMEM((chips, tok, model), BF16),
                pltpu.VMEM((chips, tok, model), BF16),
                pltpu.VMEM((2, 2 * chips, 2, half, wide), BF16),
                pltpu.VMEM(down.shape, BF16),
                pltpu.SemaphoreType.DMA((count,)),
                pltpu.SemaphoreType.DMA((count,)),
                pltpu.SemaphoreType.DMA((9,)),
            ],
        ),
        out_shape=[shaped((chips * tok, w), kind) for w, kind in zip(widths, kinds)],
        cost_estimate=takes(28), compiler_params=ROOMY,
    )(
        ring.table,
        *[piece for _, _, piece in twos],
        *[piece for _, _, piece in cots],
        *weights,
        down,
        *others,
    )


def load_window(table, at, own_ref, other_ref, window, rows):
    chips = own_ref.shape[0]
    for b in range(window.shape[0] // rows):
        place = table[at + b]
        target = window.at[b * rows : (b + 1) * rows, :]

        @pl.when(place < chips)
        def _():
            target[...] = own_ref[place]

        @pl.when(place >= chips)
        def _():
            target[...] = other_ref[place - chips]


def write_bias(first_ref, bias, rows):
    keys = bias.shape[0]
    key = lax.broadcasted_iota(jnp.int32, (keys, rows), 0)
    token = lax.broadcasted_iota(jnp.int32, (keys, rows), 1)
    allowed = (key >= first_ref[...]) & (key <= token + (keys - rows))
    values = jnp.where(allowed, 0.0, -jnp.inf)
    bias[:, :rows] = values
    bias[:, rows:] = values


def stacked(block, low_side):
    turned = pltpu.roll(block, HEAD_DIM, 1)
    low = lane_low(block.shape)
    if low_side:
        one, two = jnp.where(low, block, 0.0), jnp.where(low, turned, 0.0)
    else:
        one, two = jnp.where(low, 0.0, turned), jnp.where(low, 0.0, block)
    return jnp.concatenate([one, two], 0).astype(BF16)


def attend_kernel(
    ring, table, proj_ref, own_ref, other_ref, first_ref, cos_ref, sin_ref, q_ref, out_ref, log_ref, window, turned, bias
):
    rows = proj_ref.shape[0]

    @pl.when(pl.program_id(1) == 0)
    def _():
        load_window(table, ring.window, own_ref, other_ref, window, rows)
        turned[...] = jnp.transpose(window[...].astype(F32)).astype(BF16)

    @pl.when((pl.program_id(0) == 0) & (pl.program_id(1) == 0))
    def _():
        write_bias(first_ref, bias, rows)

    block = proj_ref[...]
    block = block * cos_ref[...] + rotated(block) * sin_ref[...]
    q_ref[...] = block.astype(BF16)
    queries = stacked(block * SCALE, True)
    score = dot(window[...], queries, LAST) + bias[...]
    top = jnp.max(score, 0, keepdims=True)
    expon = jnp.exp(score - top)
    total = jnp.sum(expon, 0, keepdims=True)
    log_ref[0] = top + jnp.log(total)
    out = jnp.transpose(dot(turned[...], expon.astype(BF16)) * (1.0 / total))
    one, two = out[:rows], out[rows:]
    out_ref[...] = jnp.where(lane_low(one.shape), pltpu.roll(one, HEAD_DIM, 1), two).astype(BF16)


def attend_back_kernel(
    ring,
    table,
    q_ref,
    grad_ref,
    att_ref,
    log_ref,
    own_ref,
    other_ref,
    first_ref,
    cos_ref,
    sin_ref,
    gq_ref,
    gown_ref,
    gother_ref,
    window,
    turned,
    total,
    bias,
):
    rows = q_ref.shape[0]
    keys = window.shape[0]
    chips = own_ref.shape[0]
    step = pl.program_id(1)

    @pl.when(step == 0)
    def _():
        load_window(table, ring.window, own_ref, other_ref, window, rows)
        turned[...] = jnp.transpose(window[...].astype(F32)).astype(BF16)
        total[...] = jnp.zeros_like(total)

    @pl.when((pl.program_id(0) == 0) & (step == 0))
    def _():
        write_bias(first_ref, bias, rows)

    grad = grad_ref[...].astype(F32)
    queries = stacked(q_ref[...].astype(F32) * SCALE, True)
    grads = stacked(grad, False)
    product = jnp.transpose(grad * att_ref[...].astype(F32))
    delta = jnp.concatenate(
        [
            jnp.sum(product[:HEAD_DIM], 0, keepdims=True),
            jnp.sum(product[HEAD_DIM:], 0, keepdims=True),
        ],
        1,
    )
    score = dot(window[...], queries, LAST) + bias[...]
    probs = jnp.exp(score - log_ref[0])
    grad_probs = dot(window[...], grads, LAST)
    grad_scores = (probs * (grad_probs - delta)).astype(BF16)
    total[...] += dot(grad_scores, queries) + dot(probs.astype(BF16), grads)
    grad_queries = jnp.transpose(dot(turned[...], grad_scores) * SCALE)
    one, two = grad_queries[:rows], grad_queries[rows:]
    block = jnp.where(lane_low(one.shape), one, pltpu.roll(two, HEAD_DIM, 1))
    gq_ref[...] = (block * cos_ref[...] - rotated(block) * sin_ref[...]).astype(BF16)

    @pl.when(step == pl.num_programs(1) - 1)
    def _():
        gown_ref[...] = jnp.zeros_like(gown_ref)
        gother_ref[...] = jnp.zeros_like(gother_ref)
        for b in range(keys // rows):
            place = table[ring.window + b]
            block = total[b * rows : (b + 1) * rows, :]

            @pl.when(place < chips)
            def _():
                gown_ref[place] = block.astype(BF16)

            @pl.when(place >= chips)
            def _():
                gother_ref[place - chips] = block.astype(BF16)


def attention_call(kernel, ring, groups, ins, outs, scratch, before, others, cost):
    start, stop = groups
    inner = HEADS // KV_HEADS // 2
    given = len(ins)

    def body(table, *refs):
        kernel(ring, table, *refs[:given], *refs[given + len(before) + len(others) :])

    def spec(entry):
        shape, place = entry
        return pl.BlockSpec(
            shape, lambda g, i, table: place(g + start, (g + start) * inner + i, table)
        )

    return pl.pallas_call(
        body,
        grid_spec=pltpu.PrefetchScalarGridSpec(
            num_scalar_prefetch=1,
            grid=(stop - start, inner),
            in_specs=[spec(entry) for _, entry in ins] + [HELD] * (len(before) + len(others)),
            out_specs=[spec(entry) for _, entry in outs],
            scratch_shapes=scratch,
        ),
        out_shape=[shape for shape, _ in outs],
        input_output_aliases={1 + given + k: k for k in range(len(before))},
        cost_estimate=takes(cost), compiler_params=ROOMY,
    )(ring.table, *[value for value, _ in ins], *before, *others)


def attention_specs(ring, rows):
    return (
        ((rows, LANES), lambda g, pair, table: (0, pair)),
        ((rows, LANES), lambda g, pair, table: (0, table[ring.place_near + pair])),
        ((1, 1, 2 * rows), lambda g, pair, table: (pair, 0, 0)),
        ((ring.chips, rows, LANES), lambda g, pair, table: (0, 0, g)),
        ((1, rows), lambda g, pair, table: (0, 0)),
        ((rows, LANES), lambda g, pair, table: (0, 0)),
    )


def attend(ring, groups, others, keys, proj, own, other, first, cosine, sine, before=()):
    rows = proj.shape[0]
    pairs = HEADS // 2
    block, near_block, log_block, kv_block, row, table = attention_specs(ring, rows)
    return attention_call(
        attend_kernel,
        ring,
        groups,
        [(proj, block), (own, kv_block), (other, kv_block)]
        + [(first, row), (cosine, table), (sine, table)],
        [
            (shaped((rows, pairs * LANES), BF16), block),
            (shaped((rows, pairs * LANES), BF16), near_block),
            (shaped((pairs, 1, 2 * rows), F32), log_block),
        ],
        [
            pltpu.VMEM((keys, LANES), BF16),
            pltpu.VMEM((LANES, keys), BF16),
            pltpu.VMEM((keys, 2 * rows), F32),
        ],
        before,
        others,
        14,
    )


def attend_back(
    ring, groups, others, keys, queries, grad, attended, logs, own, other, first, cosine, sine, before=()
):
    rows = queries.shape[0]
    block, near_block, log_block, kv_block, row, table = attention_specs(ring, rows)
    return attention_call(
        attend_back_kernel,
        ring,
        groups,
        [
            (queries, block),
            (grad, near_block),
            (attended, near_block),
            (logs, log_block),
            (own, kv_block),
            (other, kv_block),
            (first, row),
            (cosine, table),
            (sine, table),
        ],
        [
            (shaped(queries.shape, BF16), block),
            (shaped(own.shape, BF16), kv_block),
            (shaped(own.shape, BF16), kv_block),
        ],
        [
            pltpu.VMEM((keys, LANES), BF16),
            pltpu.VMEM((LANES, keys), BF16),
            pltpu.VMEM((keys, LANES), F32),
            pltpu.VMEM((keys, 2 * rows), F32),
        ],
        before,
        others,
        5,
    )


def on_device(
    reps,
    shards,
    hidden_in,
    segments,
    cotangent,
    qkv_weight,
    out_weight,
    gate_up_weight,
    down_weight,
    attn_gain,
    ffn_gain,
):
    tok = hidden_in.shape[1]
    model = hidden_in.shape[2]
    rows, width = qkv_weight.shape
    blocks = min(REACH // tok, shards - 1) + 1
    ring = Ring(shards, blocks)
    chips = ring.chips
    middle = chips * rows
    ff = down_weight.shape[0] * shards
    wide = ff // chips
    half = rows // 2
    side = ring.side
    twin_map = [(i, i ^ 1) for i in range(reps)]
    side_groups = [list(range(s, reps, 2)) for s in range(2)]
    hidden, cot_local, seg_row = hidden_in[0], cotangent[0], segments[0]
    groups = ((0, KV_HEADS // 2), (KV_HEADS // 2, KV_HEADS))

    def twin(value):
        return lax.ppermute(value, "rep", twin_map)

    def rest_of_reps(value):
        if reps == 2:
            return value
        return lax.psum(value, "rep", axis_index_groups=side_groups)

    def over_reps(value):
        mine = rest_of_reps(value).astype(BF16)
        return mine.astype(F32) + twin(mine).astype(F32)

    mine = cut_columns(ring, gate_up_weight, wide)

    packed = pack_weight(qkv_weight, attn_gain, ffn_gain, side)
    qkv_pieces, qkv_marks = ring.gather_shared(*packed, twin)
    mine = lax.all_to_all(
        after(mine, *qkv_marks[-2:]), "shard", 0, 0, axis_index_groups=ring.core_groups, tiled=True
    )

    offset = ring.index * tok
    local_seg = lax.dynamic_slice_in_dim(seg_row, offset, tok)
    starts = jnp.sum((seg_row[None, :] < local_seg[:, None]).astype(jnp.int32), 1)
    positions = offset + jnp.arange(tok, dtype=jnp.int32) - starts
    freqs = jnp.exp(
        (jnp.arange(LANES) % (HEAD_DIM // 2)).astype(F32) * (-2.0 * math.log(10000.0) / HEAD_DIM)
    )
    angles = positions.astype(F32)[:, None] * freqs[None, :]
    cosine, sine = jnp.cos(angles), jnp.sin(angles)
    first = (starts - offset + (blocks - 1) * tok)[None, :]

    proj, kv_local, input_one, factor_one, gains = project(
        ring, hidden, cosine, sine, qkv_pieces, width, ()
    )
    kv_own = stack_blocks(ring, ring.gather(kv_local), (mine,))
    kv_other = ring.swap(kv_own)
    tables = (kv_own, kv_other, first, cosine, sine)
    keys = blocks * tok
    kept = attend(ring, groups[0], (), keys, proj, *tables)
    out_halves = [
        lax.dynamic_slice_in_dim(out_weight, place * (model // 2), model // 2, 1)
        for place in (side, 1 - side)
    ]
    out_pieces, out_marks = ring.gather_shared(
        after(out_halves[0], *qkv_marks[-2:]),
        out_halves[1],
        twin,
        {2: (kv_local,), 3: (kv_own,), 4: (kept[0],)},
    )
    theirs = twin(mine)
    cots = ring.gather(after(cot_local, *out_marks[-2:]))
    kept = attend(ring, groups[1], (), keys, proj, *tables, kept)
    queries, attended, logs = kept
    residual, factor_two, input_two = project_out(ring, attended, hidden, gains, out_pieces, ())

    twos = ring.gather(input_two)
    weights = (mine, theirs, ring.swap(mine), ring.swap(theirs))
    down = join_rows(ring, down_weight, ring.swap(down_weight))
    activation, grad_gate, grad_up, grad_two, two, cot = feed_forward(
        ring, twos, cots, weights, down, ()
    )
    gu_gives = give_terms(ring, two, (grad_gate, grad_up))
    gu_gots = [ring.swap(v) for v in gu_gives]
    gu_keep, gu_give = halve_terms(ring, two, (grad_gate, grad_up), gu_gots)
    ffn_term = down_project(activation, down, (gu_give,))
    gu_recv = twin(gu_give)
    gu_sum = rest_of_reps(gu_keep + gu_recv.astype(F32)).astype(BF16)
    gu_sum = lax.all_to_all(
        gu_sum, "shard", 0, 0, axis_index_groups=ring.core_groups, tiled=True
    )
    grad_two, two_marks = ring.scatter(
        grad_two, lambda step, _: {3: (gu_give,), 4: (ffn_term,)}.get(step)
    )
    down_keep, down_give = down_terms(ring, activation, cot, two_marks[3])
    down_keep = rest_of_reps(down_keep + ring.swap(down_give).astype(F32)).astype(BF16)
    down_recv = twin(down_keep)

    grad_residual, residual_half, grad_attended, gain_two_term = back_out(
        ring, grad_two, residual, factor_two, gains, cot_local, out_pieces, (gu_recv,)
    )
    (out_give,) = give_terms(ring, attended, (residual_half,))
    out_got = ring.swap(out_give)
    out_keep, out_send = halve_terms(ring, attended, (residual_half,), (out_got,))
    out_recv = twin(out_send)
    tables = (logs, kv_own, kv_other, first, cosine, sine)
    ffn_out, ffn_marks = ring.scatter(ffn_term, lambda step, _: two_marks[-1] if step == 1 else ())
    back = attend_back(
        ring, groups[0], (), keys, queries, grad_attended, attended, *tables
    )
    back = attend_back(
        ring,
        groups[1],
        (*ffn_marks[0], gu_sum, out_send),
        keys,
        queries,
        grad_attended,
        attended,
        *tables,
        back,
    )
    grad_queries, kv_keep, kv_give = back
    gu_other = twin(gu_sum)
    (query_give,) = give_terms(ring, input_one, (grad_queries,))
    query_got = ring.swap(query_give)
    kv_got = ring.swap(after(kv_give, query_give))
    kv_term = (kv_keep.astype(F32) + kv_got.astype(F32)).astype(BF16)
    merged = merge_terms(ring, input_one, grad_queries, query_got, out_keep, out_recv)
    merged_sum, merged_marks = ring.scatter(merged)

    def kv_ties(step, marks):
        return {3: (merged, *ffn_marks[2])}.get(step)

    grad_kv, kv_marks = ring.scatter(kv_term.reshape(chips * tok, -1), kv_ties)
    grad_kv = finish_kv(ring, grad_kv, cosine, sine, merged_marks[0])
    (kv_give,) = give_terms(ring, input_one, (grad_kv,))
    (kv_term,) = keep_terms(ring, input_one, (grad_kv,), (ring.swap(kv_give),))
    grad_hidden, gain_one_term = back_project(
        ring,
        grad_queries,
        grad_kv,
        hidden,
        factor_one,
        gains,
        grad_residual,
        qkv_pieces,
        width,
        (*merged_marks[1], *ffn_marks[3]),
    )
    gain_terms = jnp.concatenate([gain_one_term[:1], gain_two_term[:1]], 0)
    gain_terms = gain_terms[:, :middle] + ring.swap(gain_terms[:, middle:])
    below = gain_terms.reshape(2, chips, rows).transpose(1, 0, 2).reshape(chips, 1, 2 * rows)
    below = jnp.pad(below, ((0, 0), (0, 15), (0, kv_term.shape[1] - 2 * rows))).astype(BF16)
    parts = jnp.concatenate([kv_term.reshape(chips, rows, -1), below], 1)
    kv_sum, last_marks = ring.scatter(
        parts.reshape(chips * (rows + 16), -1),
        lambda step, _: {3: merged_marks[2]}.get(step),
    )
    kv_sum = over_reps(summed(kv_sum))
    merged_sum = rest_of_reps(summed(merged_sum)).astype(BF16)
    other = twin(merged_sum)
    grad_queries = merged_sum[:rows].astype(F32) + other[:rows].astype(F32)
    grad_qkv = jnp.concatenate([grad_queries, kv_sum[:rows]], 1)
    mine, theirs = merged_sum[rows:], other[rows:]
    grad_out = jnp.concatenate([pick(side, mine, theirs), pick(side, theirs, mine)], 0)
    hidden_out = (residual + summed((ffn_out[0], ffn_out[1], after(ffn_out[2], grad_kv)))).astype(BF16)
    grad_down = down_keep.astype(F32) + after(down_recv, *last_marks[1]).astype(F32)
    return (
        hidden_out[None],
        grad_hidden[None],
        grad_qkv,
        grad_out.astype(F32),
        join_columns(ring, gu_sum, gu_other, (grad_kv,)),
        grad_down,
        kv_sum[rows, :rows],
        kv_sum[rows, rows : 2 * rows],
    )


def solution(mesh):
    reps, shards = mesh.shape["rep"], mesh.shape["shard"]

    def layer(*args):
        return on_device(reps, shards, *args)

    return jax.shard_map(
        layer,
        mesh=mesh,
        in_specs=(
            P("rep", "shard", None),
            P("rep", None),
            P("rep", "shard", None),
            P("shard", None),
            P("shard", None),
            P("shard", None),
            P("shard", None),
            P("shard"),
            P("shard"),
        ),
        out_specs=(
            P("rep", "shard", None),
            P("rep", "shard", None),
            P("shard", None),
            P("shard", None),
            P("shard", None),
            P("shard", None),
            P("shard"),
            P("shard"),
        ),
        check_vma=False,
    )
```

```python
import math

import jax
import jax.numpy as jnp
import numpy as np
from jax import lax
from jax.experimental import pallas as pl
from jax.experimental.pallas import tpu as pltpu
from jax.sharding import PartitionSpec as P

HEADS = 32
KV_HEADS = 4
HEAD_DIM = 64
REACH = 1024
EPS = 1e-05
F32 = jnp.float32
BF16 = jnp.bfloat16
LANES = 128
SCALE = HEAD_DIM**-0.5
LIMIT = 58 * 1024 * 1024
ROOMY = pltpu.CompilerParams(vmem_limit_bytes=LIMIT)
HELD = pl.BlockSpec(memory_space=pl.ANY)


def takes(micros):
    return pl.CostEstimate(
        flops=int(micros * 1.1e9), bytes_accessed=int(micros * 3.3e6), transcendentals=0
    )


def dot(a, b, dims=((1,), (0,))):
    return lax.dot_general(a, b, (dims, ((), ())), preferred_element_type=F32)


LAST = ((1,), (1,))
FIRST = ((0,), (0,))


def pick(flag, one, other):
    return jnp.where(flag == 0, one, other)


class Ring:
    def __init__(self, size, window):
        self.size = size
        self.chips = chips = size // 2
        rows = chips // 2
        self.order = [2 * i for i in range(rows)] + [2 * i + 1 for i in reversed(range(rows))]
        self.place = [self.order.index(chip) for chip in range(chips)]
        self.half = chips // 2

        def turned(step):
            return [
                (s, self.order[(self.place[s // 2] + step) % chips] * 2 + s % 2)
                for s in range(size)
            ]

        self.ahead = turned(1)
        self.back = turned(-1)
        self.sibling = [(s, s ^ 1) for s in range(size)]
        self.core_groups = [list(range(core, size, 2)) for core in range(2)]
        self.near, self.place_near, self.cores, self.place_cores, self.window = (
            k * size for k in range(5)
        )
        self.core_at = self.window + window
        self.side_at = self.core_at + 1
        table = []
        for side in range(2):
            for s in range(size):
                chip, core = s // 2, s % 2
                at = self.place[chip]
                near = [
                    self.order[(at + j) % chips] * 2 + (core ^ other)
                    for other in range(2)
                    for j in range(chips)
                ]
                cores = [j * 2 + (core ^ other) for other in range(2) for j in range(chips)]
                place_near = [near.index(d) for d in range(size)]
                place_cores = [cores.index(d) for d in range(size)]
                seen = [place_near[(s + 1 - window + b) % size] for b in range(window)]
                table.append(near + place_near + cores + place_cores + seen + [core, side])
        self.index = lax.axis_index("shard")
        self.side = lax.axis_index("rep") % 2
        self.table = lax.dynamic_index_in_dim(
            jnp.asarray(np.array(table, np.int32)), self.side * size + self.index, 0, False
        )

    def swap(self, value):
        return lax.ppermute(value, "shard", self.sibling)

    def gather(self, block, ties=None):
        n, h = self.chips, block.shape[0] // 2
        cw = ccw = block
        found = [(0, 0, block)]
        for k in range(1, self.half):
            if ties and k in ties:
                cw, ccw = after(cw, *ties[k]), after(ccw, *ties[k])
            cw = lax.ppermute(cw, "shard", self.ahead)
            ccw = lax.ppermute(ccw, "shard", self.back)
            found += [(n - k, 0, cw), (k, 0, ccw)]
        top = lax.ppermute(cw[:h], "shard", self.ahead)
        low = lax.ppermute(ccw[h:], "shard", self.back)
        return found + [(self.half, 0, top), (self.half, h, low)]

    def gather_shared(self, mine, other, twin, ties=None):
        own = self.gather(mine, ties)
        found = [(k, row, 0, piece) for k, row, piece in own]
        found += [(k, row, 1, twin(piece) if k else other) for k, row, piece in own]
        found += [(k + self.chips, row, part, self.swap(piece)) for k, row, part, piece in found]
        return found, [piece for _, _, piece in own]

    def scatter(self, parts, ties=None):
        n, m = self.chips, self.half
        rows = parts.shape[0] // n
        h = rows // 2
        cw, ccw = parts[m * rows : m * rows + h], parts[m * rows + h : (m + 1) * rows]
        marks = []
        for k in range(m - 1, -1, -1):
            if ties:
                others = ties(m - k, marks)
                if others:
                    cw, ccw = after(cw, *others), after(ccw, *others)
            cw = lax.ppermute(cw, "shard", self.ahead)
            ccw = lax.ppermute(ccw, "shard", self.back)
            marks.append((cw, ccw))
            if k > 0:
                cw, ccw = add_step(parts, rows, k, n - k, cw, ccw)
        return (parts, cw, ccw), marks


def add_step(parts, rows, ahead, back, cw, ccw):
    width = parts.shape[1]
    got = cw.shape[0]

    def body(ahead_ref, back_ref, cw_ref, ccw_ref, one_ref, two_ref):
        if got < rows:
            one_ref[got:] = ahead_ref[got:]
            two_ref[: rows - ccw.shape[0]] = back_ref[: rows - ccw.shape[0]]
        last = rows - ccw.shape[0]
        one_ref[:got] = (ahead_ref[:got].astype(F32) + cw_ref[...].astype(F32)).astype(BF16)
        two_ref[last:] = (back_ref[last:].astype(F32) + ccw_ref[...].astype(F32)).astype(BF16)

    return pl.pallas_call(
        body,
        grid=(1,),
        in_specs=[
            pl.BlockSpec((rows, width), lambda _: (ahead, 0)),
            pl.BlockSpec((rows, width), lambda _: (back, 0)),
            whole(cw.shape),
            whole(ccw.shape),
        ],
        out_specs=[whole((rows, width))] * 2,
        out_shape=[shaped((rows, width), BF16)] * 2,
        cost_estimate=takes(2.5), compiler_params=ROOMY,
    )(parts, parts, cw, ccw)


def summed(sums):
    parts, cw, ccw = sums
    return parts[: cw.shape[0]].astype(F32) + cw.astype(F32) + ccw.astype(F32)


def whole(shape):
    return pl.BlockSpec(shape, lambda *_: (0,) * len(shape))


def shaped(shape, kind):
    return jax.ShapeDtypeStruct(shape, kind)


def call(kernel, table, ins, outs, pieces=(), scratch=(), others=(), cost=3):
    count, more, extra = len(ins), len(pieces), len(others)

    def body(table_ref, *refs):
        behind = count + more + extra
        kernel(
            table_ref,
            refs[:count],
            refs[count : count + more],
            refs[behind : behind + len(outs)],
            refs[behind + len(outs) :],
        )

    return pl.pallas_call(
        body,
        grid_spec=pltpu.PrefetchScalarGridSpec(
            num_scalar_prefetch=1,
            grid=(1,),
            in_specs=[whole(v.shape) for v in ins] + [HELD] * (more + extra),
            out_specs=[whole(v.shape) for v in outs],
            scratch_shapes=list(scratch),
        ),
        out_shape=list(outs),
        compiler_params=ROOMY,
        cost_estimate=takes(cost),
    )(table, *ins, *pieces, *others)


def after(value, *others):
    return pl.pallas_call(
        lambda *refs: None,
        in_specs=[HELD] * (1 + len(others)),
        out_specs=HELD,
        out_shape=shaped(value.shape, value.dtype),
        input_output_aliases={0: 0},
    )(value, *others)


def fetches(pieces, refs, buffer, sems):
    return [
        pltpu.make_async_copy(
            ref, buffer.at[k, pl.ds(row, ref.shape[0])], sems.at[n]
        )
        for n, ((k, row, _), ref) in enumerate(zip(pieces, refs))
    ]


def shared_fetches(side, pieces, refs, buffer, sems):
    copies = []
    for n, ((k, row, part, _), ref) in enumerate(zip(pieces, refs)):
        rows, width = ref.shape
        start = pl.multiple_of((side if part == 0 else 1 - side) * width, LANES)
        target = buffer.at[k, pl.ds(row, rows), pl.ds(start, width)]
        copies.append(pltpu.make_async_copy(ref, target, sems.at[n]))
    return copies


def block_at(place):
    return pl.ds(pl.multiple_of(place * LANES, LANES), LANES)


def columns(block):
    return slice(block * LANES, (block + 1) * LANES)


def lane_low(shape):
    return lax.broadcasted_iota(jnp.int32, shape, len(shape) - 1) % LANES < HEAD_DIM


def rotated(values):
    quarter = HEAD_DIM // 2
    first = lax.broadcasted_iota(jnp.int32, values.shape, 1) % HEAD_DIM < quarter
    return jnp.where(
        first, -pltpu.roll(values, LANES - quarter, 1), pltpu.roll(values, quarter, 1)
    )


def pack_weight(weight, gain_one, gain_two, side):
    rows, width = weight.shape
    half = packed_width(width) // 2

    def body(side_ref, weight_ref, one_ref, two_ref, mine_ref, other_ref):
        lane = lax.broadcasted_iota(jnp.int32, (rows, LANES), 1)
        block = jnp.where(lane == 0, one_ref[...], jnp.where(lane == 1, two_ref[...], 0.0))
        first = side_ref[0] == 0
        tail = width - half

        def put(start, stop, left, right):
            mine_ref[:, start:stop] = jnp.where(first, left, right)
            other_ref[:, start:stop] = jnp.where(first, right, left)

        put(0, tail, weight_ref[:, :tail], weight_ref[:, half:])
        put(tail, tail + LANES, weight_ref[:, tail : tail + LANES], block.astype(BF16))
        if tail + LANES < half:
            left = weight_ref[:, tail + LANES : half]
            put(tail + LANES, half, left, jnp.zeros_like(left))

    gains = [g.astype(F32)[:, None] for g in (gain_one, gain_two)]
    return pl.pallas_call(
        body,
        grid_spec=pltpu.PrefetchScalarGridSpec(
            num_scalar_prefetch=1,
            grid=(1,),
            in_specs=[whole(weight.shape)] + [whole((rows, 1))] * 2,
            out_specs=[whole((rows, half))] * 2,
        ),
        out_shape=[shaped((rows, half), BF16)] * 2,
        cost_estimate=takes(3), compiler_params=ROOMY,
    )(side.astype(jnp.int32)[None], weight, *gains)


def packed_width(width):
    return -(-(width + LANES) // (2 * LANES)) * 2 * LANES


def project(ring, hidden, cosine, sine, pieces, width, others):
    size = ring.size
    rows, model = hidden.shape
    qsize = HEADS * HEAD_DIM
    step = 2 * LANES

    def kernel(table, ins, refs, outs, scratch):
        hidden_ref, cos_ref, sin_ref = ins
        q_ref, kv_ref, input_ref, factor_ref, gain_ref = outs
        buffer, sems = scratch
        copies = shared_fetches(table[ring.side_at], pieces, refs, buffer, sems)
        for copy in copies:
            copy.start()
        values = hidden_ref[...].astype(F32)
        factor = lax.rsqrt(jnp.mean(values * values, -1, keepdims=True) + EPS)
        factor_ref[...] = jnp.broadcast_to(factor, factor_ref.shape)
        for copy in copies:
            copy.wait()
        for k in range(size):
            gains = jnp.transpose(buffer[k, :, width : width + LANES].astype(F32))
            gain_ref[:, columns(k)] = gains[:8]
            part = hidden_ref[:, block_at(table[ring.near + k])].astype(F32)
            input_ref[:, columns(k)] = (part * factor * gains[:1]).astype(BF16)
        inputs = input_ref[...]
        for start in range(0, qsize, step):
            weights = buffer[:, :, start : start + step].reshape(model, step)
            q_ref[:, start : start + step] = dot(inputs, weights)
        weights = buffer[:, :, qsize:width].reshape(model, width - qsize)
        proj = dot(inputs, weights)
        for pair in range(KV_HEADS // 2):
            keys = proj[:, columns(pair)]
            keys = keys * cos_ref[...] + rotated(keys) * sin_ref[...]
            heads = proj[:, columns(KV_HEADS // 2 + pair)]
            low = lane_low(keys.shape)
            one = jnp.where(low, keys, pltpu.roll(heads, HEAD_DIM, 1))
            two = jnp.where(low, pltpu.roll(keys, HEAD_DIM, 1), heads)
            kv_ref[:, columns(2 * pair)] = one.astype(BF16)
            kv_ref[:, columns(2 * pair + 1)] = two.astype(BF16)

    return call(
        kernel,
        ring.table,
        [hidden, cosine, sine],
        [
            shaped((rows, qsize), F32),
            shaped((rows, KV_HEADS * LANES), BF16),
            shaped((rows, model), BF16),
            shaped((rows, LANES), F32),
            shaped((8, model), F32),
        ],
        [piece for *_, piece in pieces],
        [
            pltpu.VMEM((size, rows, packed_width(width)), BF16),
            pltpu.SemaphoreType.DMA((len(pieces),)),
        ],
        others,
        9,
    )


def stack_blocks(ring, pieces, others):
    rows, width = pieces[0][2].shape

    def body(*refs):
        copies = fetches(pieces, refs[: len(pieces)], refs[-2], refs[-1])
        for copy in copies:
            copy.start()
        for copy in copies:
            copy.wait()

    return pl.pallas_call(
        body,
        in_specs=[HELD] * (len(pieces) + len(others)),
        out_specs=pl.BlockSpec(memory_space=pltpu.VMEM),
        out_shape=shaped((ring.chips, rows, width), pieces[0][2].dtype),
        scratch_shapes=[pltpu.SemaphoreType.DMA((len(pieces),))],
        cost_estimate=takes(2.5), compiler_params=ROOMY,
    )(*[piece for _, _, piece in pieces], *others)


def project_out(ring, attended, hidden, gains, pieces, others):
    size = ring.size
    rows, model = hidden.shape
    step = 2 * LANES

    def kernel(table, ins, refs, outs, scratch):
        att_ref, hidden_ref, gain_ref = ins
        residual_ref, factor_ref, input_ref = outs
        buffer, sems = scratch
        copies = shared_fetches(table[ring.side_at], pieces, refs, buffer, sems)
        for copy in copies:
            copy.start()
        for copy in copies:
            copy.wait()
        inputs = att_ref[...]
        squares = jnp.zeros((rows, 1), F32)
        for start in range(0, model, step):
            weights = buffer[:, :, start : start + step].reshape(model, step)
            part = hidden_ref[:, start : start + step].astype(F32) + dot(inputs, weights)
            residual_ref[:, start : start + step] = part
            squares += jnp.sum(part * part, -1, keepdims=True)
        factor = lax.rsqrt(squares * (1.0 / model) + EPS)
        factor_ref[...] = jnp.broadcast_to(factor, factor_ref.shape)
        for k in range(size):
            device = table[ring.cores + k]
            gain = gain_ref[1:2, block_at(table[ring.place_near + device])]
            part = residual_ref[:, block_at(device)] * factor
            input_ref[:, columns(k)] = (part * gain).astype(BF16)

    return call(
        kernel,
        ring.table,
        [attended, hidden, gains],
        [shaped((rows, model), F32), shaped((rows, LANES), F32), shaped((rows, model), BF16)],
        [piece for *_, piece in pieces],
        [
            pltpu.VMEM((size, rows, model), BF16),
            pltpu.SemaphoreType.DMA((len(pieces),)),
        ],
        others,
        8,
    )


def back_out(ring, sums, residual, factor, gains, cot, pieces, others):
    size = ring.size
    rows, model = residual.shape

    def kernel(table, ins, refs, outs, scratch):
        own_ref, cw_ref, ccw_ref, residual_ref, factor_ref, gain_ref, cot_ref = ins
        grad_res_ref, half_ref, att_ref, term_ref = outs
        buffer, sems, total = scratch
        copies = shared_fetches(table[ring.side_at], pieces, refs, buffer, sems)
        for copy in copies:
            copy.start()
        factor = factor_ref[...]
        mean = jnp.zeros((rows, 1), F32)
        for d in range(size):
            place, source = (
                block_at(table[order + d]) for order in (ring.place_near, ring.place_cores)
            )
            grad = sum(ref[:, source].astype(F32) for ref in (own_ref, cw_ref, ccw_ref))
            total[:, columns(d)] = grad
            normed = residual_ref[:, columns(d)] * factor
            product = grad * normed
            term_ref[:, place] = jnp.broadcast_to(
                jnp.sum(product, 0, keepdims=True), (8, LANES)
            )
            mean += jnp.sum(product * gain_ref[1:2, place], -1, keepdims=True)
        mean *= 1.0 / model
        for d in range(size):
            place = block_at(table[ring.place_near + d])
            grad = total[:, columns(d)] * gain_ref[1:2, place]
            normed = residual_ref[:, columns(d)] * factor
            back = cot_ref[:, columns(d)].astype(F32) + factor * (grad - normed * mean)
            grad_res_ref[:, columns(d)] = back
            half_ref[:, columns(d)] = back.astype(BF16)
        for copy in copies:
            copy.wait()
        halves = half_ref[...]
        for k in range(0, size, 2):
            weights = buffer[k : k + 2].reshape(2 * rows, model)
            att_ref[:, k * LANES : (k + 2) * LANES] = dot(halves, weights, LAST).astype(BF16)

    return call(
        kernel,
        ring.table,
        [sums[0][:rows], sums[1], sums[2], residual, factor, gains, cot],
        [
            shaped((rows, model), F32),
            shaped((rows, model), BF16),
            shaped((rows, model), BF16),
            shaped((8, model), F32),
        ],
        [piece for *_, piece in pieces],
        [
            pltpu.VMEM((size, rows, model), BF16),
            pltpu.SemaphoreType.DMA((len(pieces),)),
            pltpu.VMEM((rows, model), F32),
        ],
        others,
        3.5,
    )


def finish_kv(ring, sums, cosine, sine, others):
    def kernel(table, ins, refs, outs, scratch):
        own_ref, cw_ref, ccw_ref, cos_ref, sin_ref = ins
        grad = sum(ref[...].astype(F32) for ref in (own_ref, cw_ref, ccw_ref))
        for pair in range(KV_HEADS // 2):
            one = grad[:, columns(2 * pair)]
            two = grad[:, columns(2 * pair + 1)]
            low = lane_low(one.shape)
            keys = jnp.where(low, one, pltpu.roll(two, HEAD_DIM, 1))
            values = jnp.where(low, pltpu.roll(one, HEAD_DIM, 1), two)
            keys = keys * cos_ref[...] - rotated(keys) * sin_ref[...]
            outs[0][:, columns(pair)] = keys.astype(BF16)
            outs[0][:, columns(KV_HEADS // 2 + pair)] = values.astype(BF16)

    rows = sums[1].shape[0]
    return call(
        kernel,
        ring.table,
        [sums[0][:rows], sums[1], sums[2], cosine, sine],
        [shaped((rows, 2 * KV_HEADS * HEAD_DIM), BF16)],
        others=others,
    )[0]


def back_project(
    ring, grad_queries, grad_kv, hidden, factor, gains, grad_residual, pieces, width, others
):
    size = ring.size
    rows, model = hidden.shape
    qsize = grad_queries.shape[1]

    def kernel(table, ins, refs, outs, scratch):
        gq_ref, gkv_ref, hidden_ref, factor_ref, gain_ref, grad_res_ref = ins
        grad_ref, term_ref = outs
        buffer, sems, total = scratch
        copies = shared_fetches(table[ring.side_at], pieces, refs, buffer, sems)
        for copy in copies:
            copy.start()
        for copy in copies:
            copy.wait()
        queries, keys = gq_ref[...], gkv_ref[...]
        for k in range(0, size, 2):
            weights = buffer[k : k + 2].reshape(2 * rows, packed_width(width))
            total[:, k * LANES : (k + 2) * LANES] = dot(
                queries, weights[:, :qsize], LAST
            ) + dot(keys, weights[:, qsize:width], LAST)
        factor = factor_ref[...]
        mean = jnp.zeros((rows, 1), F32)
        for k in range(size):
            normed = hidden_ref[:, block_at(table[ring.near + k])].astype(F32) * factor
            product = total[:, columns(k)] * normed
            term_ref[:, columns(k)] = jnp.broadcast_to(
                jnp.sum(product, 0, keepdims=True), (8, LANES)
            )
            mean += jnp.sum(product * gain_ref[:1, columns(k)], -1, keepdims=True)
        mean *= 1.0 / model
        for k in range(size):
            place = block_at(table[ring.near + k])
            normed = hidden_ref[:, place].astype(F32) * factor
            scaled = total[:, columns(k)] * gain_ref[:1, columns(k)]
            back = grad_res_ref[:, place] + factor * (scaled - normed * mean)
            grad_ref[:, place] = back.astype(BF16)

    return call(
        kernel,
        ring.table,
        [grad_queries, grad_kv, hidden, factor, gains, grad_residual],
        [shaped((rows, model), BF16), shaped((8, model), F32)],
        [piece for *_, piece in pieces],
        [
            pltpu.VMEM((size, rows, packed_width(width)), BF16),
            pltpu.SemaphoreType.DMA((len(pieces),)),
            pltpu.VMEM((rows, model), F32),
        ],
        others,
        4.025,
    )


def cut_columns(ring, weight, wide):
    rows = weight.shape[0]
    half = rows // 2

    def kernel(table, ins, refs, outs, scratch):
        upper = table[ring.side_at] == 0
        for chip in range(ring.chips):
            for part in range(2):
                start = (part * ring.chips + chip) * wide
                block = ins[0][:, start : start + wide].astype(F32)
                outs[0][chip, part] = jnp.where(upper, block[:half], block[half:]).astype(BF16)

    return call(
        kernel, ring.table, [weight], [shaped((ring.chips, 2, half, wide), BF16)]
    )[0]


def join_columns(ring, mine, theirs, others):
    chips, parts, half, wide = mine.shape

    def kernel(table, ins, refs, outs, scratch):
        flip = table[ring.side_at] == 0
        for chip in range(chips):
            for part in range(parts):
                start = (part * chips + chip) * wide
                one, two = ins[0][chip, part].astype(F32), ins[1][chip, part].astype(F32)
                outs[0][:half, start : start + wide] = jnp.where(flip, one, two)
                outs[0][half:, start : start + wide] = jnp.where(flip, two, one)

    return call(
        kernel,
        ring.table,
        [mine, theirs],
        [shaped((2 * half, parts * chips * wide), F32)],
        others=others,
    )[0]


def step_columns(tokens):
    return (4 if tokens <= LANES else 2) * LANES


def give_terms(ring, inputs, grads, others=()):
    tokens, model = inputs.shape
    count, extra = len(grads), len(others)
    step = step_columns(tokens)
    steps = model // 2 // step

    def body(input_ref, *refs):
        for grad_ref, out_ref in zip(refs[:count], refs[count + extra :]):
            out_ref[...] = dot(input_ref[...], grad_ref[...], FIRST).astype(BF16)

    return pl.pallas_call(
        body,
        grid=(steps,),
        in_specs=[pl.BlockSpec((tokens, step), lambda i: (0, steps + i))]
        + [whole(g.shape) for g in grads]
        + [HELD] * extra,
        out_specs=[pl.BlockSpec((step, g.shape[1]), lambda i: (i, 0)) for g in grads],
        out_shape=[shaped((model // 2, g.shape[1]), BF16) for g in grads],
        cost_estimate=takes(2.1), compiler_params=ROOMY,
    )(inputs, *grads, *others)


def keep_terms(ring, inputs, grads, gots):
    tokens, model = inputs.shape
    count = len(grads)
    step = step_columns(tokens)

    def body(input_ref, *refs):
        for part in range(count):
            term = dot(input_ref[...], refs[part][...], FIRST)
            refs[2 * count + part][...] = (term + refs[count + part][...].astype(F32)).astype(BF16)

    blocks = [pl.BlockSpec((step, g.shape[1]), lambda i: (i, 0)) for g in grads]
    return pl.pallas_call(
        body,
        grid=(model // 2 // step,),
        in_specs=[pl.BlockSpec((tokens, step), lambda i: (0, i))]
        + [whole(g.shape) for g in grads]
        + blocks,
        out_specs=blocks,
        out_shape=[shaped((model // 2, g.shape[1]), BF16) for g in grads],
        cost_estimate=takes(1.75), compiler_params=ROOMY,
    )(inputs, *grads, *gots)


def merge_terms(ring, inputs, grads, got, halves, halves_got):
    tokens, model = inputs.shape
    chips, _, half, wide = halves.shape
    rows = model // ring.size
    step = step_columns(tokens)
    each = step // rows
    high = rows + half

    def body(input_ref, grad_ref, got_ref, half_ref, half_got_ref, out_ref):
        term = dot(input_ref[...], grad_ref[...], FIRST)
        for n in range(each):
            at = slice(n * rows, (n + 1) * rows)
            total = term[at] + got_ref[at].astype(F32)
            out_ref[n * high : n * high + rows] = total.astype(BF16)
            total = half_ref[n, 0] + half_got_ref[n, 0].astype(F32)
            out_ref[n * high + rows : (n + 1) * high] = total.astype(BF16)

    block = pl.BlockSpec((each, 1, half, wide), lambda i: (i, 0, 0, 0))
    return pl.pallas_call(
        body,
        grid=(chips // each,),
        in_specs=[
            pl.BlockSpec((tokens, step), lambda i: (0, i)),
            whole(grads.shape),
            pl.BlockSpec((step, wide), lambda i: (i, 0)),
            block,
            block,
        ],
        out_specs=pl.BlockSpec((each * high, wide), lambda i: (i, 0)),
        out_shape=shaped((chips * high, wide), BF16),
        cost_estimate=takes(2), compiler_params=ROOMY,
    )(inputs, grads, got, halves, halves_got)


def halve_terms(ring, inputs, grads, gots):
    tokens, model = inputs.shape
    chips, count = ring.chips, len(grads)
    rows, wide = model // ring.size, grads[0].shape[1]
    half = rows // 2
    step = step_columns(tokens)
    each = step // rows

    def body(table, input_ref, *refs):
        upper = table[ring.side_at] == 0
        keep_ref, give_ref = refs[2 * count :]
        for part in range(count):
            term = dot(input_ref[...], refs[part][...], FIRST)
            for n in range(each):
                at = slice(n * rows, (n + 1) * rows)
                total = term[at] + refs[count + part][at].astype(F32)
                keep_ref[n, part] = jnp.where(upper, total[:half], total[half:])
                give_ref[n, part] = jnp.where(upper, total[half:], total[:half]).astype(BF16)

    return pl.pallas_call(
        body,
        grid_spec=pltpu.PrefetchScalarGridSpec(
            num_scalar_prefetch=1,
            grid=(chips // each,),
            in_specs=[pl.BlockSpec((tokens, step), lambda i, _: (0, i))]
            + [whole(g.shape) for g in grads]
            + [pl.BlockSpec((step, wide), lambda i, _: (i, 0))] * count,
            out_specs=[pl.BlockSpec((each, count, half, wide), lambda i, _: (i, 0, 0, 0))] * 2,
        ),
        out_shape=[shaped((chips, count, half, wide), kind) for kind in (F32, BF16)],
        cost_estimate=takes(3.15), compiler_params=ROOMY,
    )(ring.table, inputs, *grads, *gots)


def down_terms(ring, activation, cot, others):
    tokens, wide = activation.shape
    model = cot.shape[1]
    step, half = 2 * LANES, wide // 2

    def body(table, act_ref, cot_ref, *refs):
        keep_ref, give_ref = refs[len(others) :]
        total = dot(act_ref[...], cot_ref[...], FIRST)
        first = table[ring.core_at] == 0
        keep_ref[...] = jnp.where(first, total[:half], total[half:])
        give_ref[...] = jnp.where(first, total[half:], total[:half]).astype(BF16)

    return pl.pallas_call(
        body,
        grid_spec=pltpu.PrefetchScalarGridSpec(
            num_scalar_prefetch=1,
            grid=(model // step,),
            in_specs=[whole(activation.shape), pl.BlockSpec((tokens, step), lambda i, _: (0, i))]
            + [HELD] * len(others),
            out_specs=[pl.BlockSpec((half, step), lambda i, _: (0, i))] * 2,
        ),
        out_shape=[shaped((half, model), kind) for kind in (F32, BF16)],
        cost_estimate=takes(3.5), compiler_params=ROOMY,
    )(ring.table, activation, cot, *others)


def down_project(activation, down, others):
    tokens, wide = activation.shape
    model = down.shape[1]
    step = 2 * LANES

    def body(act_ref, down_ref, *refs):
        refs[-1][...] = dot(act_ref[...], down_ref[...]).astype(BF16)

    return pl.pallas_call(
        body,
        grid=(tokens // step,),
        in_specs=[pl.BlockSpec((step, wide), lambda i: (i, 0)), whole(down.shape)]
        + [HELD] * len(others),
        out_specs=pl.BlockSpec((step, model), lambda i: (i, 0)),
        out_shape=shaped((tokens, model), BF16),
        cost_estimate=takes(2.45), compiler_params=ROOMY,
    )(activation, down, *others)


def join_rows(ring, mine, theirs):
    rows, wide = mine.shape

    def body(table, mine_ref, theirs_ref, out_ref, sems):
        core = table[ring.core_at]
        copies = []
        for n, (place, ref) in enumerate(((core, mine_ref), (1 - core, theirs_ref))):
            target = out_ref.at[pl.ds(pl.multiple_of(place * rows, 16), rows)]
            copies.append(pltpu.make_async_copy(ref, target, sems.at[n]))
        for copy in copies:
            copy.start()
        for copy in copies:
            copy.wait()

    return pl.pallas_call(
        body,
        grid_spec=pltpu.PrefetchScalarGridSpec(
            num_scalar_prefetch=1,
            grid=(1,),
            in_specs=[HELD] * 2,
            out_specs=whole((2 * rows, wide)),
            scratch_shapes=[pltpu.SemaphoreType.DMA((2,))],
        ),
        out_shape=shaped((2 * rows, wide), mine.dtype),
        cost_estimate=takes(4), compiler_params=ROOMY,
    )(ring.table, mine, theirs)


def feed_forward(ring, twos, cots, weights, down, others):
    chips = ring.chips
    tok, model = twos[0][2].shape
    _, _, half, wide = weights[0].shape
    each = chips // 2
    steps = chips // each
    chunk = each * tok
    count = len(twos)

    def body(table, *refs):
        two_refs, cot_refs = refs[:count], refs[count : 2 * count]
        weight_refs = refs[2 * count : 2 * count + 4]
        down_ref = refs[2 * count + 4]
        outs = refs[2 * count + 5 + len(others) :]
        act_ref, gate_ref, up_ref, grad_ref, two_out, cot_out = outs[:6]
        two_buf, cot_buf, weight_buf, down_buf, two_sems, cot_sems, weight_sems = outs[6:]
        step = pl.program_id(0)
        side = table[ring.side_at]
        moves = [pltpu.make_async_copy(down_ref, down_buf, weight_sems.at[8])]
        for n, ref in enumerate(weight_refs):
            place = side if n % 2 == 0 else 1 - side
            for part in range(2):
                target = weight_buf.at[part, pl.ds(n // 2 * chips, chips), place]
                sem = weight_sems.at[2 * n + part]
                moves.append(pltpu.make_async_copy(ref.at[:, part], target, sem))
        blocks = fetches(twos, two_refs, two_buf, two_sems)
        blocks += fetches(cots, cot_refs, cot_buf, cot_sems)

        @pl.when(step == 0)
        def _():
            for move in moves + blocks:
                move.start()
            for move in moves:
                move.wait()

        for at in range(steps):

            @pl.when(step == at)
            def _():
                for (slot, _, _), block in zip(twos + cots, blocks):
                    if slot // each == at:
                        block.wait()

        two = two_buf[pl.ds(step * each, each)].reshape(chunk, model)
        cot = cot_buf[pl.ds(step * each, each)].reshape(chunk, model)
        two_out[...] = two
        cot_out[...] = cot
        gate_weight = weight_buf[0].reshape(model, wide)
        up_weight = weight_buf[1].reshape(model, wide)
        gate = dot(two, gate_weight)
        upward = dot(two, up_weight)
        grad = dot(cot, down_buf[...], LAST)
        sigma = jax.nn.sigmoid(gate)
        act_ref[...] = (gate * sigma * upward).astype(BF16)
        grad_gate = (grad * upward * (sigma * (1.0 + gate * (1.0 - sigma)))).astype(BF16)
        grad_up = (grad * gate * sigma).astype(BF16)
        gate_ref[...] = grad_gate
        up_ref[...] = grad_up
        grad_two = dot(grad_gate, gate_weight, LAST) + dot(grad_up, up_weight, LAST)
        grad_ref[...] = grad_two.astype(BF16)

    def out(width):
        return pl.BlockSpec((chunk, width), lambda i, _: (i, 0))

    widths = (wide, wide, wide, model, model, model)
    kinds = (BF16,) * 6
    return pl.pallas_call(
        body,
        grid_spec=pltpu.PrefetchScalarGridSpec(
            num_scalar_prefetch=1,
            grid=(steps,),
            in_specs=[HELD] * (2 * count + 5 + len(others)),
            out_specs=[out(w) for w in widths],
            scratch_shapes=[
                pltpu.VMEM((chips, tok, model), BF16),
                pltpu.VMEM((chips, tok, model), BF16),
                pltpu.VMEM((2, 2 * chips, 2, half, wide), BF16),
                pltpu.VMEM(down.shape, BF16),
                pltpu.SemaphoreType.DMA((count,)),
                pltpu.SemaphoreType.DMA((count,)),
                pltpu.SemaphoreType.DMA((9,)),
            ],
        ),
        out_shape=[shaped((chips * tok, w), kind) for w, kind in zip(widths, kinds)],
        cost_estimate=takes(28), compiler_params=ROOMY,
    )(
        ring.table,
        *[piece for _, _, piece in twos],
        *[piece for _, _, piece in cots],
        *weights,
        down,
        *others,
    )


def load_window(table, at, own_ref, other_ref, window, rows):
    chips = own_ref.shape[0]
    for b in range(window.shape[0] // rows):
        place = table[at + b]
        target = window.at[b * rows : (b + 1) * rows, :]

        @pl.when(place < chips)
        def _():
            target[...] = own_ref[place]

        @pl.when(place >= chips)
        def _():
            target[...] = other_ref[place - chips]


def write_bias(first_ref, bias, rows):
    keys = bias.shape[0]
    key = lax.broadcasted_iota(jnp.int32, (keys, rows), 0)
    token = lax.broadcasted_iota(jnp.int32, (keys, rows), 1)
    allowed = (key >= first_ref[...]) & (key <= token + (keys - rows))
    values = jnp.where(allowed, 0.0, -jnp.inf)
    bias[:, :rows] = values
    bias[:, rows:] = values


def stacked(block, low_side):
    turned = pltpu.roll(block, HEAD_DIM, 1)
    low = lane_low(block.shape)
    if low_side:
        one, two = jnp.where(low, block, 0.0), jnp.where(low, turned, 0.0)
    else:
        one, two = jnp.where(low, 0.0, turned), jnp.where(low, 0.0, block)
    return jnp.concatenate([one, two], 0).astype(BF16)


def attend_kernel(
    ring, table, proj_ref, own_ref, other_ref, first_ref, cos_ref, sin_ref, q_ref, out_ref, log_ref, window, turned, bias
):
    rows = proj_ref.shape[0]

    @pl.when(pl.program_id(1) == 0)
    def _():
        load_window(table, ring.window, own_ref, other_ref, window, rows)
        turned[...] = jnp.transpose(window[...].astype(F32)).astype(BF16)

    @pl.when((pl.program_id(0) == 0) & (pl.program_id(1) == 0))
    def _():
        write_bias(first_ref, bias, rows)

    block = proj_ref[...]
    block = block * cos_ref[...] + rotated(block) * sin_ref[...]
    q_ref[...] = block.astype(BF16)
    queries = stacked(block * SCALE, True)
    score = dot(window[...], queries, LAST) + bias[...]
    top = jnp.max(score, 0, keepdims=True)
    expon = jnp.exp(score - top)
    total = jnp.sum(expon, 0, keepdims=True)
    log_ref[0] = top + jnp.log(total)
    out = jnp.transpose(dot(turned[...], expon.astype(BF16)) * (1.0 / total))
    one, two = out[:rows], out[rows:]
    out_ref[...] = jnp.where(lane_low(one.shape), pltpu.roll(one, HEAD_DIM, 1), two).astype(BF16)


def attend_back_kernel(
    ring,
    table,
    q_ref,
    grad_ref,
    att_ref,
    log_ref,
    own_ref,
    other_ref,
    first_ref,
    cos_ref,
    sin_ref,
    gq_ref,
    gown_ref,
    gother_ref,
    window,
    turned,
    total,
    bias,
):
    rows = q_ref.shape[0]
    keys = window.shape[0]
    chips = own_ref.shape[0]
    step = pl.program_id(1)

    @pl.when(step == 0)
    def _():
        load_window(table, ring.window, own_ref, other_ref, window, rows)
        turned[...] = jnp.transpose(window[...].astype(F32)).astype(BF16)
        total[...] = jnp.zeros_like(total)

    @pl.when((pl.program_id(0) == 0) & (step == 0))
    def _():
        write_bias(first_ref, bias, rows)

    grad = grad_ref[...].astype(F32)
    queries = stacked(q_ref[...].astype(F32) * SCALE, True)
    grads = stacked(grad, False)
    product = jnp.transpose(grad * att_ref[...].astype(F32))
    delta = jnp.concatenate(
        [
            jnp.sum(product[:HEAD_DIM], 0, keepdims=True),
            jnp.sum(product[HEAD_DIM:], 0, keepdims=True),
        ],
        1,
    )
    score = dot(window[...], queries, LAST) + bias[...]
    probs = jnp.exp(score - log_ref[0])
    grad_probs = dot(window[...], grads, LAST)
    grad_scores = (probs * (grad_probs - delta)).astype(BF16)
    total[...] += dot(grad_scores, queries) + dot(probs.astype(BF16), grads)
    grad_queries = jnp.transpose(dot(turned[...], grad_scores) * SCALE)
    one, two = grad_queries[:rows], grad_queries[rows:]
    block = jnp.where(lane_low(one.shape), one, pltpu.roll(two, HEAD_DIM, 1))
    gq_ref[...] = (block * cos_ref[...] - rotated(block) * sin_ref[...]).astype(BF16)

    @pl.when(step == pl.num_programs(1) - 1)
    def _():
        gown_ref[...] = jnp.zeros_like(gown_ref)
        gother_ref[...] = jnp.zeros_like(gother_ref)
        for b in range(keys // rows):
            place = table[ring.window + b]
            block = total[b * rows : (b + 1) * rows, :]

            @pl.when(place < chips)
            def _():
                gown_ref[place] = block.astype(BF16)

            @pl.when(place >= chips)
            def _():
                gother_ref[place - chips] = block.astype(BF16)


def attention_call(kernel, ring, groups, ins, outs, scratch, before, others, cost):
    start, stop = groups
    inner = HEADS // KV_HEADS // 2
    given = len(ins)

    def body(table, *refs):
        kernel(ring, table, *refs[:given], *refs[given + len(before) + len(others) :])

    def spec(entry):
        shape, place = entry
        return pl.BlockSpec(
            shape, lambda g, i, table: place(g + start, (g + start) * inner + i, table)
        )

    return pl.pallas_call(
        body,
        grid_spec=pltpu.PrefetchScalarGridSpec(
            num_scalar_prefetch=1,
            grid=(stop - start, inner),
            in_specs=[spec(entry) for _, entry in ins] + [HELD] * (len(before) + len(others)),
            out_specs=[spec(entry) for _, entry in outs],
            scratch_shapes=scratch,
        ),
        out_shape=[shape for shape, _ in outs],
        input_output_aliases={1 + given + k: k for k in range(len(before))},
        cost_estimate=takes(cost), compiler_params=ROOMY,
    )(ring.table, *[value for value, _ in ins], *before, *others)


def attention_specs(ring, rows):
    return (
        ((rows, LANES), lambda g, pair, table: (0, pair)),
        ((rows, LANES), lambda g, pair, table: (0, table[ring.place_near + pair])),
        ((1, 1, 2 * rows), lambda g, pair, table: (pair, 0, 0)),
        ((ring.chips, rows, LANES), lambda g, pair, table: (0, 0, g)),
        ((1, rows), lambda g, pair, table: (0, 0)),
        ((rows, LANES), lambda g, pair, table: (0, 0)),
    )


def attend(ring, groups, others, keys, proj, own, other, first, cosine, sine, before=()):
    rows = proj.shape[0]
    pairs = HEADS // 2
    block, near_block, log_block, kv_block, row, table = attention_specs(ring, rows)
    return attention_call(
        attend_kernel,
        ring,
        groups,
        [(proj, block), (own, kv_block), (other, kv_block)]
        + [(first, row), (cosine, table), (sine, table)],
        [
            (shaped((rows, pairs * LANES), BF16), block),
            (shaped((rows, pairs * LANES), BF16), near_block),
            (shaped((pairs, 1, 2 * rows), F32), log_block),
        ],
        [
            pltpu.VMEM((keys, LANES), BF16),
            pltpu.VMEM((LANES, keys), BF16),
            pltpu.VMEM((keys, 2 * rows), F32),
        ],
        before,
        others,
        14,
    )


def attend_back(
    ring, groups, others, keys, queries, grad, attended, logs, own, other, first, cosine, sine, before=()
):
    rows = queries.shape[0]
    block, near_block, log_block, kv_block, row, table = attention_specs(ring, rows)
    return attention_call(
        attend_back_kernel,
        ring,
        groups,
        [
            (queries, block),
            (grad, near_block),
            (attended, near_block),
            (logs, log_block),
            (own, kv_block),
            (other, kv_block),
            (first, row),
            (cosine, table),
            (sine, table),
        ],
        [
            (shaped(queries.shape, BF16), block),
            (shaped(own.shape, BF16), kv_block),
            (shaped(own.shape, BF16), kv_block),
        ],
        [
            pltpu.VMEM((keys, LANES), BF16),
            pltpu.VMEM((LANES, keys), BF16),
            pltpu.VMEM((keys, LANES), F32),
            pltpu.VMEM((keys, 2 * rows), F32),
        ],
        before,
        others,
        5,
    )


def on_device(
    reps,
    shards,
    hidden_in,
    segments,
    cotangent,
    qkv_weight,
    out_weight,
    gate_up_weight,
    down_weight,
    attn_gain,
    ffn_gain,
):
    tok = hidden_in.shape[1]
    model = hidden_in.shape[2]
    rows, width = qkv_weight.shape
    blocks = min(REACH // tok, shards - 1) + 1
    ring = Ring(shards, blocks)
    chips = ring.chips
    middle = chips * rows
    ff = down_weight.shape[0] * shards
    wide = ff // chips
    half = rows // 2
    side = ring.side
    twin_map = [(i, i ^ 1) for i in range(reps)]
    side_groups = [list(range(s, reps, 2)) for s in range(2)]
    hidden, cot_local, seg_row = hidden_in[0], cotangent[0], segments[0]
    groups = ((0, KV_HEADS // 2), (KV_HEADS // 2, KV_HEADS))

    def twin(value):
        return lax.ppermute(value, "rep", twin_map)

    def rest_of_reps(value):
        if reps == 2:
            return value
        return lax.psum(value, "rep", axis_index_groups=side_groups)

    def over_reps(value):
        mine = rest_of_reps(value).astype(BF16)
        return mine.astype(F32) + twin(mine).astype(F32)

    mine = cut_columns(ring, gate_up_weight, wide)

    packed = pack_weight(qkv_weight, attn_gain, ffn_gain, side)
    qkv_pieces, qkv_marks = ring.gather_shared(*packed, twin)
    out_halves = [
        lax.dynamic_slice_in_dim(out_weight, place * (model // 2), model // 2, 1)
        for place in (side, 1 - side)
    ]
    out_pieces, out_marks = ring.gather_shared(
        after(out_halves[0], *qkv_marks[-2:]), out_halves[1], twin
    )
    mine = lax.all_to_all(
        after(mine, *out_marks[-2:]), "shard", 0, 0, axis_index_groups=ring.core_groups, tiled=True
    )

    offset = ring.index * tok
    local_seg = lax.dynamic_slice_in_dim(seg_row, offset, tok)
    starts = jnp.sum((seg_row[None, :] < local_seg[:, None]).astype(jnp.int32), 1)
    positions = offset + jnp.arange(tok, dtype=jnp.int32) - starts
    freqs = jnp.exp(
        (jnp.arange(LANES) % (HEAD_DIM // 2)).astype(F32) * (-2.0 * math.log(10000.0) / HEAD_DIM)
    )
    angles = positions.astype(F32)[:, None] * freqs[None, :]
    cosine, sine = jnp.cos(angles), jnp.sin(angles)
    first = (starts - offset + (blocks - 1) * tok)[None, :]

    proj, kv_local, input_one, factor_one, gains = project(
        ring, hidden, cosine, sine, qkv_pieces, width, tuple(out_marks[5:7])
    )
    kv_own = stack_blocks(ring, ring.gather(kv_local), ())
    kv_other = ring.swap(kv_own)
    tables = (kv_own, kv_other, first, cosine, sine)
    keys = blocks * tok
    kept = attend(ring, groups[0], (), keys, proj, *tables)
    theirs = twin(mine)
    cots = ring.gather(after(cot_local, mine))
    kept = attend(ring, groups[1], (), keys, proj, *tables, kept)
    queries, attended, logs = kept
    residual, factor_two, input_two = project_out(ring, attended, hidden, gains, out_pieces, tuple(p for *_, p in cots[1:3]))

    twos = ring.gather(input_two)
    weights = (mine, theirs, ring.swap(mine), ring.swap(theirs))
    down = join_rows(ring, down_weight, ring.swap(down_weight))
    activation, grad_gate, grad_up, grad_two, two, cot = feed_forward(
        ring, twos, cots, weights, down, ()
    )
    gu_gives = give_terms(ring, two, (grad_gate, grad_up))
    gu_gots = [ring.swap(v) for v in gu_gives]
    gu_keep, gu_give = halve_terms(ring, two, (grad_gate, grad_up), gu_gots)
    ffn_term = down_project(activation, down, (gu_give,))
    gu_recv = twin(gu_give)
    gu_sum = rest_of_reps(gu_keep + gu_recv.astype(F32)).astype(BF16)
    gu_sum = lax.all_to_all(
        gu_sum, "shard", 0, 0, axis_index_groups=ring.core_groups, tiled=True
    )
    grad_two, two_marks = ring.scatter(
        grad_two, lambda step, _: {3: (gu_give,), 4: (ffn_term,)}.get(step)
    )
    down_keep, down_give = down_terms(ring, activation, cot, two_marks[3])
    down_keep = rest_of_reps(down_keep + ring.swap(down_give).astype(F32)).astype(BF16)
    down_recv = twin(down_keep)

    grad_residual, residual_half, grad_attended, gain_two_term = back_out(
        ring, grad_two, residual, factor_two, gains, cot_local, out_pieces, (gu_recv,)
    )
    (out_give,) = give_terms(ring, attended, (residual_half,))
    out_got = ring.swap(out_give)
    out_keep, out_send = halve_terms(ring, attended, (residual_half,), (out_got,))
    out_recv = twin(out_send)
    tables = (logs, kv_own, kv_other, first, cosine, sine)
    ffn_out, ffn_marks = ring.scatter(ffn_term, lambda step, _: two_marks[-1] if step == 1 else ())
    back = attend_back(
        ring, groups[0], (), keys, queries, grad_attended, attended, *tables
    )
    back = attend_back(
        ring,
        groups[1],
        (*ffn_marks[0], gu_sum, out_send),
        keys,
        queries,
        grad_attended,
        attended,
        *tables,
        back,
    )
    grad_queries, kv_keep, kv_give = back
    gu_other = twin(gu_sum)
    (query_give,) = give_terms(ring, input_one, (grad_queries,))
    query_got = ring.swap(query_give)
    kv_got = ring.swap(after(kv_give, query_give))
    kv_term = (kv_keep.astype(F32) + kv_got.astype(F32)).astype(BF16)
    merged = merge_terms(ring, input_one, grad_queries, query_got, out_keep, out_recv)
    merged_sum, merged_marks = ring.scatter(merged)

    def kv_ties(step, marks):
        return {3: (merged, *ffn_marks[2])}.get(step)

    grad_kv, kv_marks = ring.scatter(kv_term.reshape(chips * tok, -1), kv_ties)
    grad_kv = finish_kv(ring, grad_kv, cosine, sine, merged_marks[0])
    (kv_give,) = give_terms(ring, input_one, (grad_kv,))
    (kv_term,) = keep_terms(ring, input_one, (grad_kv,), (ring.swap(kv_give),))
    grad_hidden, gain_one_term = back_project(
        ring,
        grad_queries,
        grad_kv,
        hidden,
        factor_one,
        gains,
        grad_residual,
        qkv_pieces,
        width,
        (*merged_marks[1], *ffn_marks[3]),
    )
    gain_terms = jnp.concatenate([gain_one_term[:1], gain_two_term[:1]], 0)
    gain_terms = gain_terms[:, :middle] + ring.swap(gain_terms[:, middle:])
    below = gain_terms.reshape(2, chips, rows).transpose(1, 0, 2).reshape(chips, 1, 2 * rows)
    below = jnp.pad(below, ((0, 0), (0, 15), (0, kv_term.shape[1] - 2 * rows))).astype(BF16)
    parts = jnp.concatenate([kv_term.reshape(chips, rows, -1), below], 1)
    kv_sum, last_marks = ring.scatter(
        parts.reshape(chips * (rows + 16), -1),
        lambda step, _: {3: merged_marks[2]}.get(step),
    )
    kv_sum = over_reps(summed(kv_sum))
    merged_sum = rest_of_reps(summed(merged_sum)).astype(BF16)
    other = twin(merged_sum)
    grad_queries = merged_sum[:rows].astype(F32) + other[:rows].astype(F32)
    grad_qkv = jnp.concatenate([grad_queries, kv_sum[:rows]], 1)
    mine, theirs = merged_sum[rows:], other[rows:]
    grad_out = jnp.concatenate([pick(side, mine, theirs), pick(side, theirs, mine)], 0)
    hidden_out = (residual + summed((ffn_out[0], ffn_out[1], after(ffn_out[2], grad_kv)))).astype(BF16)
    grad_down = down_keep.astype(F32) + after(down_recv, *last_marks[1]).astype(F32)
    return (
        hidden_out[None],
        grad_hidden[None],
        grad_qkv,
        grad_out.astype(F32),
        join_columns(ring, gu_sum, gu_other, (grad_kv,)),
        grad_down,
        kv_sum[rows, :rows],
        kv_sum[rows, rows : 2 * rows],
    )


def solution(mesh):
    reps, shards = mesh.shape["rep"], mesh.shape["shard"]

    def layer(*args):
        return on_device(reps, shards, *args)

    return jax.shard_map(
        layer,
        mesh=mesh,
        in_specs=(
            P("rep", "shard", None),
            P("rep", None),
            P("rep", "shard", None),
            P("shard", None),
            P("shard", None),
            P("shard", None),
            P("shard", None),
            P("shard"),
            P("shard"),
        ),
        out_specs=(
            P("rep", "shard", None),
            P("rep", "shard", None),
            P("shard", None),
            P("shard", None),
            P("shard", None),
            P("shard", None),
            P("shard"),
            P("shard"),
        ),
        check_vma=False,
    )
```

```python
import math

import jax
import jax.numpy as jnp
import numpy as np
from jax import lax
from jax.experimental import pallas as pl
from jax.experimental.pallas import tpu as pltpu
from jax.sharding import PartitionSpec as P

HEADS = 32
KV_HEADS = 4
HEAD_DIM = 64
REACH = 1024
EPS = 1e-05
F32 = jnp.float32
BF16 = jnp.bfloat16
LANES = 128
SCALE = HEAD_DIM**-0.5
LIMIT = 58 * 1024 * 1024
ROOMY = pltpu.CompilerParams(vmem_limit_bytes=LIMIT)
HELD = pl.BlockSpec(memory_space=pl.ANY)


def takes(micros):
    return pl.CostEstimate(
        flops=int(micros * 1.1e9), bytes_accessed=int(micros * 3.3e6), transcendentals=0
    )


def dot(a, b, dims=((1,), (0,))):
    return lax.dot_general(a, b, (dims, ((), ())), preferred_element_type=F32)


LAST = ((1,), (1,))
FIRST = ((0,), (0,))


def pick(flag, one, other):
    return jnp.where(flag == 0, one, other)


class Ring:
    def __init__(self, size, window):
        self.size = size
        self.chips = chips = size // 2
        rows = chips // 2
        self.order = [2 * i for i in range(rows)] + [2 * i + 1 for i in reversed(range(rows))]
        self.place = [self.order.index(chip) for chip in range(chips)]
        self.half = chips // 2

        def turned(step):
            return [
                (s, self.order[(self.place[s // 2] + step) % chips] * 2 + s % 2)
                for s in range(size)
            ]

        self.ahead = turned(1)
        self.back = turned(-1)
        self.sibling = [(s, s ^ 1) for s in range(size)]
        self.core_groups = [list(range(core, size, 2)) for core in range(2)]
        self.near, self.place_near, self.cores, self.place_cores, self.window = (
            k * size for k in range(5)
        )
        self.core_at = self.window + window
        self.side_at = self.core_at + 1
        table = []
        for side in range(2):
            for s in range(size):
                chip, core = s // 2, s % 2
                at = self.place[chip]
                near = [
                    self.order[(at + j) % chips] * 2 + (core ^ other)
                    for other in range(2)
                    for j in range(chips)
                ]
                cores = [j * 2 + (core ^ other) for other in range(2) for j in range(chips)]
                place_near = [near.index(d) for d in range(size)]
                place_cores = [cores.index(d) for d in range(size)]
                seen = [place_near[(s + 1 - window + b) % size] for b in range(window)]
                table.append(near + place_near + cores + place_cores + seen + [core, side])
        self.index = lax.axis_index("shard")
        self.side = lax.axis_index("rep") % 2
        self.table = lax.dynamic_index_in_dim(
            jnp.asarray(np.array(table, np.int32)), self.side * size + self.index, 0, False
        )

    def swap(self, value):
        return lax.ppermute(value, "shard", self.sibling)

    def gather(self, block, ties=None):
        n, h = self.chips, block.shape[0] // 2
        cw = ccw = block
        found = [(0, 0, block)]
        for k in range(1, self.half):
            if ties and k in ties:
                cw, ccw = after(cw, *ties[k]), after(ccw, *ties[k])
            cw = lax.ppermute(cw, "shard", self.ahead)
            ccw = lax.ppermute(ccw, "shard", self.back)
            found += [(n - k, 0, cw), (k, 0, ccw)]
        top = lax.ppermute(cw[:h], "shard", self.ahead)
        low = lax.ppermute(ccw[h:], "shard", self.back)
        return found + [(self.half, 0, top), (self.half, h, low)]

    def gather_shared(self, mine, other, twin, ties=None):
        own = self.gather(mine, ties)
        found = [(k, row, 0, piece) for k, row, piece in own]
        found += [(k, row, 1, twin(piece) if k else other) for k, row, piece in own]
        found += [(k + self.chips, row, part, self.swap(piece)) for k, row, part, piece in found]
        return found, [piece for _, _, piece in own]

    def scatter(self, parts, ties=None):
        n, m = self.chips, self.half
        rows = parts.shape[0] // n
        h = rows // 2
        cw, ccw = parts[m * rows : m * rows + h], parts[m * rows + h : (m + 1) * rows]
        marks = []
        for k in range(m - 1, -1, -1):
            if ties:
                others = ties(m - k, marks)
                if others:
                    cw, ccw = after(cw, *others), after(ccw, *others)
            cw = lax.ppermute(cw, "shard", self.ahead)
            ccw = lax.ppermute(ccw, "shard", self.back)
            marks.append((cw, ccw))
            if k > 0:
                cw, ccw = add_step(parts, rows, k, n - k, cw, ccw)
        return (parts, cw, ccw), marks


def add_step(parts, rows, ahead, back, cw, ccw):
    width = parts.shape[1]
    got = cw.shape[0]

    def body(ahead_ref, back_ref, cw_ref, ccw_ref, one_ref, two_ref):
        if got < rows:
            one_ref[got:] = ahead_ref[got:]
            two_ref[: rows - ccw.shape[0]] = back_ref[: rows - ccw.shape[0]]
        last = rows - ccw.shape[0]
        one_ref[:got] = (ahead_ref[:got].astype(F32) + cw_ref[...].astype(F32)).astype(BF16)
        two_ref[last:] = (back_ref[last:].astype(F32) + ccw_ref[...].astype(F32)).astype(BF16)

    return pl.pallas_call(
        body,
        grid=(1,),
        in_specs=[
            pl.BlockSpec((rows, width), lambda _: (ahead, 0)),
            pl.BlockSpec((rows, width), lambda _: (back, 0)),
            whole(cw.shape),
            whole(ccw.shape),
        ],
        out_specs=[whole((rows, width))] * 2,
        out_shape=[shaped((rows, width), BF16)] * 2,
        cost_estimate=takes(2.5), compiler_params=ROOMY,
    )(parts, parts, cw, ccw)


def summed(sums):
    parts, cw, ccw = sums
    return parts[: cw.shape[0]].astype(F32) + cw.astype(F32) + ccw.astype(F32)


def whole(shape):
    return pl.BlockSpec(shape, lambda *_: (0,) * len(shape))


def shaped(shape, kind):
    return jax.ShapeDtypeStruct(shape, kind)


def call(kernel, table, ins, outs, pieces=(), scratch=(), others=(), cost=3):
    count, more, extra = len(ins), len(pieces), len(others)

    def body(table_ref, *refs):
        behind = count + more + extra
        kernel(
            table_ref,
            refs[:count],
            refs[count : count + more],
            refs[behind : behind + len(outs)],
            refs[behind + len(outs) :],
        )

    return pl.pallas_call(
        body,
        grid_spec=pltpu.PrefetchScalarGridSpec(
            num_scalar_prefetch=1,
            grid=(1,),
            in_specs=[whole(v.shape) for v in ins] + [HELD] * (more + extra),
            out_specs=[whole(v.shape) for v in outs],
            scratch_shapes=list(scratch),
        ),
        out_shape=list(outs),
        compiler_params=ROOMY,
        cost_estimate=takes(cost),
    )(table, *ins, *pieces, *others)


def after(value, *others):
    return pl.pallas_call(
        lambda *refs: None,
        in_specs=[HELD] * (1 + len(others)),
        out_specs=HELD,
        out_shape=shaped(value.shape, value.dtype),
        input_output_aliases={0: 0},
    )(value, *others)


def fetches(pieces, refs, buffer, sems):
    return [
        pltpu.make_async_copy(
            ref, buffer.at[k, pl.ds(row, ref.shape[0])], sems.at[n]
        )
        for n, ((k, row, _), ref) in enumerate(zip(pieces, refs))
    ]


def shared_fetches(side, pieces, refs, buffer, sems):
    copies = []
    for n, ((k, row, part, _), ref) in enumerate(zip(pieces, refs)):
        rows, width = ref.shape
        start = pl.multiple_of((side if part == 0 else 1 - side) * width, LANES)
        target = buffer.at[k, pl.ds(row, rows), pl.ds(start, width)]
        copies.append(pltpu.make_async_copy(ref, target, sems.at[n]))
    return copies


def block_at(place):
    return pl.ds(pl.multiple_of(place * LANES, LANES), LANES)


def columns(block):
    return slice(block * LANES, (block + 1) * LANES)


def lane_low(shape):
    return lax.broadcasted_iota(jnp.int32, shape, len(shape) - 1) % LANES < HEAD_DIM


def rotated(values):
    quarter = HEAD_DIM // 2
    first = lax.broadcasted_iota(jnp.int32, values.shape, 1) % HEAD_DIM < quarter
    return jnp.where(
        first, -pltpu.roll(values, LANES - quarter, 1), pltpu.roll(values, quarter, 1)
    )


def pack_weight(weight, gain_one, gain_two, side):
    rows, width = weight.shape
    half = packed_width(width) // 2

    def body(side_ref, weight_ref, one_ref, two_ref, mine_ref, other_ref):
        lane = lax.broadcasted_iota(jnp.int32, (rows, LANES), 1)
        block = jnp.where(lane == 0, one_ref[...], jnp.where(lane == 1, two_ref[...], 0.0))
        first = side_ref[0] == 0
        tail = width - half

        def put(start, stop, left, right):
            mine_ref[:, start:stop] = jnp.where(first, left, right)
            other_ref[:, start:stop] = jnp.where(first, right, left)

        put(0, tail, weight_ref[:, :tail], weight_ref[:, half:])
        put(tail, tail + LANES, weight_ref[:, tail : tail + LANES], block.astype(BF16))
        if tail + LANES < half:
            left = weight_ref[:, tail + LANES : half]
            put(tail + LANES, half, left, jnp.zeros_like(left))

    gains = [g.astype(F32)[:, None] for g in (gain_one, gain_two)]
    return pl.pallas_call(
        body,
        grid_spec=pltpu.PrefetchScalarGridSpec(
            num_scalar_prefetch=1,
            grid=(1,),
            in_specs=[whole(weight.shape)] + [whole((rows, 1))] * 2,
            out_specs=[whole((rows, half))] * 2,
        ),
        out_shape=[shaped((rows, half), BF16)] * 2,
        cost_estimate=takes(3), compiler_params=ROOMY,
    )(side.astype(jnp.int32)[None], weight, *gains)


def packed_width(width):
    return -(-(width + LANES) // (2 * LANES)) * 2 * LANES


def project(ring, hidden, cosine, sine, pieces, width, others):
    size = ring.size
    rows, model = hidden.shape
    qsize = HEADS * HEAD_DIM
    step = 2 * LANES

    def kernel(table, ins, refs, outs, scratch):
        hidden_ref, cos_ref, sin_ref = ins
        q_ref, kv_ref, input_ref, factor_ref, gain_ref = outs
        buffer, sems = scratch
        copies = shared_fetches(table[ring.side_at], pieces, refs, buffer, sems)
        for copy in copies:
            copy.start()
        values = hidden_ref[...].astype(F32)
        factor = lax.rsqrt(jnp.mean(values * values, -1, keepdims=True) + EPS)
        factor_ref[...] = jnp.broadcast_to(factor, factor_ref.shape)
        for copy in copies:
            copy.wait()
        for k in range(size):
            gains = jnp.transpose(buffer[k, :, width : width + LANES].astype(F32))
            gain_ref[:, columns(k)] = gains[:8]
            part = hidden_ref[:, block_at(table[ring.near + k])].astype(F32)
            input_ref[:, columns(k)] = (part * factor * gains[:1]).astype(BF16)
        inputs = input_ref[...]
        for start in range(0, qsize, step):
            weights = buffer[:, :, start : start + step].reshape(model, step)
            q_ref[:, start : start + step] = dot(inputs, weights)
        weights = buffer[:, :, qsize:width].reshape(model, width - qsize)
        proj = dot(inputs, weights)
        for pair in range(KV_HEADS // 2):
            keys = proj[:, columns(pair)]
            keys = keys * cos_ref[...] + rotated(keys) * sin_ref[...]
            heads = proj[:, columns(KV_HEADS // 2 + pair)]
            low = lane_low(keys.shape)
            one = jnp.where(low, keys, pltpu.roll(heads, HEAD_DIM, 1))
            two = jnp.where(low, pltpu.roll(keys, HEAD_DIM, 1), heads)
            kv_ref[:, columns(2 * pair)] = one.astype(BF16)
            kv_ref[:, columns(2 * pair + 1)] = two.astype(BF16)

    return call(
        kernel,
        ring.table,
        [hidden, cosine, sine],
        [
            shaped((rows, qsize), F32),
            shaped((rows, KV_HEADS * LANES), BF16),
            shaped((rows, model), BF16),
            shaped((rows, LANES), F32),
            shaped((8, model), F32),
        ],
        [piece for *_, piece in pieces],
        [
            pltpu.VMEM((size, rows, packed_width(width)), BF16),
            pltpu.SemaphoreType.DMA((len(pieces),)),
        ],
        others,
        9,
    )


def stack_blocks(ring, pieces, others):
    rows, width = pieces[0][2].shape

    def body(*refs):
        copies = fetches(pieces, refs[: len(pieces)], refs[-2], refs[-1])
        for copy in copies:
            copy.start()
        for copy in copies:
            copy.wait()

    return pl.pallas_call(
        body,
        in_specs=[HELD] * (len(pieces) + len(others)),
        out_specs=pl.BlockSpec(memory_space=pltpu.VMEM),
        out_shape=shaped((ring.chips, rows, width), pieces[0][2].dtype),
        scratch_shapes=[pltpu.SemaphoreType.DMA((len(pieces),))],
        cost_estimate=takes(2.5), compiler_params=ROOMY,
    )(*[piece for _, _, piece in pieces], *others)


def project_out(ring, attended, hidden, gains, pieces, others):
    size = ring.size
    rows, model = hidden.shape
    step = 2 * LANES

    def kernel(table, ins, refs, outs, scratch):
        att_ref, hidden_ref, gain_ref = ins
        residual_ref, factor_ref, input_ref = outs
        buffer, sems = scratch
        copies = shared_fetches(table[ring.side_at], pieces, refs, buffer, sems)
        for copy in copies:
            copy.start()
        for copy in copies:
            copy.wait()
        inputs = att_ref[...]
        squares = jnp.zeros((rows, 1), F32)
        for start in range(0, model, step):
            weights = buffer[:, :, start : start + step].reshape(model, step)
            part = hidden_ref[:, start : start + step].astype(F32) + dot(inputs, weights)
            residual_ref[:, start : start + step] = part
            squares += jnp.sum(part * part, -1, keepdims=True)
        factor = lax.rsqrt(squares * (1.0 / model) + EPS)
        factor_ref[...] = jnp.broadcast_to(factor, factor_ref.shape)
        for k in range(size):
            device = table[ring.cores + k]
            gain = gain_ref[1:2, block_at(table[ring.place_near + device])]
            part = residual_ref[:, block_at(device)] * factor
            input_ref[:, columns(k)] = (part * gain).astype(BF16)

    return call(
        kernel,
        ring.table,
        [attended, hidden, gains],
        [shaped((rows, model), F32), shaped((rows, LANES), F32), shaped((rows, model), BF16)],
        [piece for *_, piece in pieces],
        [
            pltpu.VMEM((size, rows, model), BF16),
            pltpu.SemaphoreType.DMA((len(pieces),)),
        ],
        others,
        8,
    )


def back_out(ring, sums, residual, factor, gains, cot, pieces, others):
    size = ring.size
    rows, model = residual.shape

    def kernel(table, ins, refs, outs, scratch):
        own_ref, cw_ref, ccw_ref, residual_ref, factor_ref, gain_ref, cot_ref = ins
        grad_res_ref, half_ref, att_ref, term_ref = outs
        buffer, sems, total = scratch
        copies = shared_fetches(table[ring.side_at], pieces, refs, buffer, sems)
        for copy in copies:
            copy.start()
        factor = factor_ref[...]
        mean = jnp.zeros((rows, 1), F32)
        for d in range(size):
            place, source = (
                block_at(table[order + d]) for order in (ring.place_near, ring.place_cores)
            )
            grad = sum(ref[:, source].astype(F32) for ref in (own_ref, cw_ref, ccw_ref))
            total[:, columns(d)] = grad
            normed = residual_ref[:, columns(d)] * factor
            product = grad * normed
            term_ref[:, place] = jnp.broadcast_to(
                jnp.sum(product, 0, keepdims=True), (8, LANES)
            )
            mean += jnp.sum(product * gain_ref[1:2, place], -1, keepdims=True)
        mean *= 1.0 / model
        for d in range(size):
            place = block_at(table[ring.place_near + d])
            grad = total[:, columns(d)] * gain_ref[1:2, place]
            normed = residual_ref[:, columns(d)] * factor
            back = cot_ref[:, columns(d)].astype(F32) + factor * (grad - normed * mean)
            grad_res_ref[:, columns(d)] = back
            half_ref[:, columns(d)] = back.astype(BF16)
        for copy in copies:
            copy.wait()
        halves = half_ref[...]
        for k in range(0, size, 2):
            weights = buffer[k : k + 2].reshape(2 * rows, model)
            att_ref[:, k * LANES : (k + 2) * LANES] = dot(halves, weights, LAST).astype(BF16)

    return call(
        kernel,
        ring.table,
        [sums[0][:rows], sums[1], sums[2], residual, factor, gains, cot],
        [
            shaped((rows, model), F32),
            shaped((rows, model), BF16),
            shaped((rows, model), BF16),
            shaped((8, model), F32),
        ],
        [piece for *_, piece in pieces],
        [
            pltpu.VMEM((size, rows, model), BF16),
            pltpu.SemaphoreType.DMA((len(pieces),)),
            pltpu.VMEM((rows, model), F32),
        ],
        others,
        3.5,
    )


def finish_kv(ring, sums, cosine, sine, others):
    def kernel(table, ins, refs, outs, scratch):
        own_ref, cw_ref, ccw_ref, cos_ref, sin_ref = ins
        grad = sum(ref[...].astype(F32) for ref in (own_ref, cw_ref, ccw_ref))
        for pair in range(KV_HEADS // 2):
            one = grad[:, columns(2 * pair)]
            two = grad[:, columns(2 * pair + 1)]
            low = lane_low(one.shape)
            keys = jnp.where(low, one, pltpu.roll(two, HEAD_DIM, 1))
            values = jnp.where(low, pltpu.roll(one, HEAD_DIM, 1), two)
            keys = keys * cos_ref[...] - rotated(keys) * sin_ref[...]
            outs[0][:, columns(pair)] = keys.astype(BF16)
            outs[0][:, columns(KV_HEADS // 2 + pair)] = values.astype(BF16)

    rows = sums[1].shape[0]
    return call(
        kernel,
        ring.table,
        [sums[0][:rows], sums[1], sums[2], cosine, sine],
        [shaped((rows, 2 * KV_HEADS * HEAD_DIM), BF16)],
        others=others,
    )[0]


def back_project(
    ring, grad_queries, grad_kv, hidden, factor, gains, grad_residual, pieces, width, others
):
    size = ring.size
    rows, model = hidden.shape
    qsize = grad_queries.shape[1]

    def kernel(table, ins, refs, outs, scratch):
        gq_ref, gkv_ref, hidden_ref, factor_ref, gain_ref, grad_res_ref = ins
        grad_ref, term_ref = outs
        buffer, sems, total = scratch
        copies = shared_fetches(table[ring.side_at], pieces, refs, buffer, sems)
        for copy in copies:
            copy.start()
        for copy in copies:
            copy.wait()
        queries, keys = gq_ref[...], gkv_ref[...]
        for k in range(0, size, 2):
            weights = buffer[k : k + 2].reshape(2 * rows, packed_width(width))
            total[:, k * LANES : (k + 2) * LANES] = dot(
                queries, weights[:, :qsize], LAST
            ) + dot(keys, weights[:, qsize:width], LAST)
        factor = factor_ref[...]
        mean = jnp.zeros((rows, 1), F32)
        for k in range(size):
            normed = hidden_ref[:, block_at(table[ring.near + k])].astype(F32) * factor
            product = total[:, columns(k)] * normed
            term_ref[:, columns(k)] = jnp.broadcast_to(
                jnp.sum(product, 0, keepdims=True), (8, LANES)
            )
            mean += jnp.sum(product * gain_ref[:1, columns(k)], -1, keepdims=True)
        mean *= 1.0 / model
        for k in range(size):
            place = block_at(table[ring.near + k])
            normed = hidden_ref[:, place].astype(F32) * factor
            scaled = total[:, columns(k)] * gain_ref[:1, columns(k)]
            back = grad_res_ref[:, place] + factor * (scaled - normed * mean)
            grad_ref[:, place] = back.astype(BF16)

    return call(
        kernel,
        ring.table,
        [grad_queries, grad_kv, hidden, factor, gains, grad_residual],
        [shaped((rows, model), BF16), shaped((8, model), F32)],
        [piece for *_, piece in pieces],
        [
            pltpu.VMEM((size, rows, packed_width(width)), BF16),
            pltpu.SemaphoreType.DMA((len(pieces),)),
            pltpu.VMEM((rows, model), F32),
        ],
        others,
        4.025,
    )


def cut_columns(ring, weight, wide):
    rows = weight.shape[0]
    half = rows // 2

    def kernel(table, ins, refs, outs, scratch):
        upper = table[ring.side_at] == 0
        for chip in range(ring.chips):
            for part in range(2):
                start = (part * ring.chips + chip) * wide
                block = ins[0][:, start : start + wide].astype(F32)
                outs[0][chip, part] = jnp.where(upper, block[:half], block[half:]).astype(BF16)

    return call(
        kernel, ring.table, [weight], [shaped((ring.chips, 2, half, wide), BF16)]
    )[0]


def join_columns(ring, mine, theirs, others):
    chips, parts, half, wide = mine.shape

    def kernel(table, ins, refs, outs, scratch):
        flip = table[ring.side_at] == 0
        for chip in range(chips):
            for part in range(parts):
                start = (part * chips + chip) * wide
                one, two = ins[0][chip, part].astype(F32), ins[1][chip, part].astype(F32)
                outs[0][:half, start : start + wide] = jnp.where(flip, one, two)
                outs[0][half:, start : start + wide] = jnp.where(flip, two, one)

    return call(
        kernel,
        ring.table,
        [mine, theirs],
        [shaped((2 * half, parts * chips * wide), F32)],
        others=others,
    )[0]


def step_columns(tokens):
    return (4 if tokens <= LANES else 2) * LANES


def give_terms(ring, inputs, grads, others=()):
    tokens, model = inputs.shape
    count, extra = len(grads), len(others)
    step = step_columns(tokens)
    steps = model // 2 // step

    def body(input_ref, *refs):
        for grad_ref, out_ref in zip(refs[:count], refs[count + extra :]):
            out_ref[...] = dot(input_ref[...], grad_ref[...], FIRST).astype(BF16)

    return pl.pallas_call(
        body,
        grid=(steps,),
        in_specs=[pl.BlockSpec((tokens, step), lambda i: (0, steps + i))]
        + [whole(g.shape) for g in grads]
        + [HELD] * extra,
        out_specs=[pl.BlockSpec((step, g.shape[1]), lambda i: (i, 0)) for g in grads],
        out_shape=[shaped((model // 2, g.shape[1]), BF16) for g in grads],
        cost_estimate=takes(2.1), compiler_params=ROOMY,
    )(inputs, *grads, *others)


def keep_terms(ring, inputs, grads, gots):
    tokens, model = inputs.shape
    count = len(grads)
    step = step_columns(tokens)

    def body(input_ref, *refs):
        for part in range(count):
            term = dot(input_ref[...], refs[part][...], FIRST)
            refs[2 * count + part][...] = (term + refs[count + part][...].astype(F32)).astype(BF16)

    blocks = [pl.BlockSpec((step, g.shape[1]), lambda i: (i, 0)) for g in grads]
    return pl.pallas_call(
        body,
        grid=(model // 2 // step,),
        in_specs=[pl.BlockSpec((tokens, step), lambda i: (0, i))]
        + [whole(g.shape) for g in grads]
        + blocks,
        out_specs=blocks,
        out_shape=[shaped((model // 2, g.shape[1]), BF16) for g in grads],
        cost_estimate=takes(1.75), compiler_params=ROOMY,
    )(inputs, *grads, *gots)


def merge_terms(ring, inputs, grads, got, halves, halves_got):
    tokens, model = inputs.shape
    chips, _, half, wide = halves.shape
    rows = model // ring.size
    step = step_columns(tokens)
    each = step // rows
    high = rows + half

    def body(input_ref, grad_ref, got_ref, half_ref, half_got_ref, out_ref):
        term = dot(input_ref[...], grad_ref[...], FIRST)
        for n in range(each):
            at = slice(n * rows, (n + 1) * rows)
            total = term[at] + got_ref[at].astype(F32)
            out_ref[n * high : n * high + rows] = total.astype(BF16)
            total = half_ref[n, 0] + half_got_ref[n, 0].astype(F32)
            out_ref[n * high + rows : (n + 1) * high] = total.astype(BF16)

    block = pl.BlockSpec((each, 1, half, wide), lambda i: (i, 0, 0, 0))
    return pl.pallas_call(
        body,
        grid=(chips // each,),
        in_specs=[
            pl.BlockSpec((tokens, step), lambda i: (0, i)),
            whole(grads.shape),
            pl.BlockSpec((step, wide), lambda i: (i, 0)),
            block,
            block,
        ],
        out_specs=pl.BlockSpec((each * high, wide), lambda i: (i, 0)),
        out_shape=shaped((chips * high, wide), BF16),
        cost_estimate=takes(2), compiler_params=ROOMY,
    )(inputs, grads, got, halves, halves_got)


def halve_terms(ring, inputs, grads, gots):
    tokens, model = inputs.shape
    chips, count = ring.chips, len(grads)
    rows, wide = model // ring.size, grads[0].shape[1]
    half = rows // 2
    step = step_columns(tokens)
    each = step // rows

    def body(table, input_ref, *refs):
        upper = table[ring.side_at] == 0
        keep_ref, give_ref = refs[2 * count :]
        for part in range(count):
            term = dot(input_ref[...], refs[part][...], FIRST)
            for n in range(each):
                at = slice(n * rows, (n + 1) * rows)
                total = term[at] + refs[count + part][at].astype(F32)
                keep_ref[n, part] = jnp.where(upper, total[:half], total[half:])
                give_ref[n, part] = jnp.where(upper, total[half:], total[:half]).astype(BF16)

    return pl.pallas_call(
        body,
        grid_spec=pltpu.PrefetchScalarGridSpec(
            num_scalar_prefetch=1,
            grid=(chips // each,),
            in_specs=[pl.BlockSpec((tokens, step), lambda i, _: (0, i))]
            + [whole(g.shape) for g in grads]
            + [pl.BlockSpec((step, wide), lambda i, _: (i, 0))] * count,
            out_specs=[pl.BlockSpec((each, count, half, wide), lambda i, _: (i, 0, 0, 0))] * 2,
        ),
        out_shape=[shaped((chips, count, half, wide), kind) for kind in (F32, BF16)],
        cost_estimate=takes(3.15), compiler_params=ROOMY,
    )(ring.table, inputs, *grads, *gots)


def down_terms(ring, activation, cot, others):
    tokens, wide = activation.shape
    model = cot.shape[1]
    step, half = 2 * LANES, wide // 2

    def body(table, act_ref, cot_ref, *refs):
        keep_ref, give_ref = refs[len(others) :]
        total = dot(act_ref[...], cot_ref[...], FIRST)
        first = table[ring.core_at] == 0
        keep_ref[...] = jnp.where(first, total[:half], total[half:])
        give_ref[...] = jnp.where(first, total[half:], total[:half]).astype(BF16)

    return pl.pallas_call(
        body,
        grid_spec=pltpu.PrefetchScalarGridSpec(
            num_scalar_prefetch=1,
            grid=(model // step,),
            in_specs=[whole(activation.shape), pl.BlockSpec((tokens, step), lambda i, _: (0, i))]
            + [HELD] * len(others),
            out_specs=[pl.BlockSpec((half, step), lambda i, _: (0, i))] * 2,
        ),
        out_shape=[shaped((half, model), kind) for kind in (F32, BF16)],
        cost_estimate=takes(3.5), compiler_params=ROOMY,
    )(ring.table, activation, cot, *others)


def down_project(activation, down, others):
    tokens, wide = activation.shape
    model = down.shape[1]
    step = 2 * LANES

    def body(act_ref, down_ref, *refs):
        refs[-1][...] = dot(act_ref[...], down_ref[...]).astype(BF16)

    return pl.pallas_call(
        body,
        grid=(tokens // step,),
        in_specs=[pl.BlockSpec((step, wide), lambda i: (i, 0)), whole(down.shape)]
        + [HELD] * len(others),
        out_specs=pl.BlockSpec((step, model), lambda i: (i, 0)),
        out_shape=shaped((tokens, model), BF16),
        cost_estimate=takes(2.45), compiler_params=ROOMY,
    )(activation, down, *others)


def join_rows(ring, mine, theirs):
    rows, wide = mine.shape

    def body(table, mine_ref, theirs_ref, out_ref, sems):
        core = table[ring.core_at]
        copies = []
        for n, (place, ref) in enumerate(((core, mine_ref), (1 - core, theirs_ref))):
            target = out_ref.at[pl.ds(pl.multiple_of(place * rows, 16), rows)]
            copies.append(pltpu.make_async_copy(ref, target, sems.at[n]))
        for copy in copies:
            copy.start()
        for copy in copies:
            copy.wait()

    return pl.pallas_call(
        body,
        grid_spec=pltpu.PrefetchScalarGridSpec(
            num_scalar_prefetch=1,
            grid=(1,),
            in_specs=[HELD] * 2,
            out_specs=whole((2 * rows, wide)),
            scratch_shapes=[pltpu.SemaphoreType.DMA((2,))],
        ),
        out_shape=shaped((2 * rows, wide), mine.dtype),
        cost_estimate=takes(4), compiler_params=ROOMY,
    )(ring.table, mine, theirs)


def feed_forward(ring, twos, cots, weights, down, others):
    chips = ring.chips
    tok, model = twos[0][2].shape
    _, _, half, wide = weights[0].shape
    each = chips // 2
    steps = chips // each
    chunk = each * tok
    count = len(twos)

    def body(table, *refs):
        two_refs, cot_refs = refs[:count], refs[count : 2 * count]
        weight_refs = refs[2 * count : 2 * count + 4]
        down_ref = refs[2 * count + 4]
        outs = refs[2 * count + 5 + len(others) :]
        act_ref, gate_ref, up_ref, grad_ref, two_out, cot_out = outs[:6]
        two_buf, cot_buf, weight_buf, down_buf, two_sems, cot_sems, weight_sems = outs[6:]
        step = pl.program_id(0)
        side = table[ring.side_at]
        moves = [pltpu.make_async_copy(down_ref, down_buf, weight_sems.at[8])]
        for n, ref in enumerate(weight_refs):
            place = side if n % 2 == 0 else 1 - side
            for part in range(2):
                target = weight_buf.at[part, pl.ds(n // 2 * chips, chips), place]
                sem = weight_sems.at[2 * n + part]
                moves.append(pltpu.make_async_copy(ref.at[:, part], target, sem))
        blocks = fetches(twos, two_refs, two_buf, two_sems)
        blocks += fetches(cots, cot_refs, cot_buf, cot_sems)

        @pl.when(step == 0)
        def _():
            for move in moves + blocks:
                move.start()
            for move in moves:
                move.wait()

        for at in range(steps):

            @pl.when(step == at)
            def _():
                for (slot, _, _), block in zip(twos + cots, blocks):
                    if slot // each == at:
                        block.wait()

        two = two_buf[pl.ds(step * each, each)].reshape(chunk, model)
        cot = cot_buf[pl.ds(step * each, each)].reshape(chunk, model)
        two_out[...] = two
        cot_out[...] = cot
        gate_weight = weight_buf[0].reshape(model, wide)
        up_weight = weight_buf[1].reshape(model, wide)
        gate = dot(two, gate_weight)
        upward = dot(two, up_weight)
        grad = dot(cot, down_buf[...], LAST)
        sigma = jax.nn.sigmoid(gate)
        act_ref[...] = (gate * sigma * upward).astype(BF16)
        grad_gate = (grad * upward * (sigma * (1.0 + gate * (1.0 - sigma)))).astype(BF16)
        grad_up = (grad * gate * sigma).astype(BF16)
        gate_ref[...] = grad_gate
        up_ref[...] = grad_up
        grad_two = dot(grad_gate, gate_weight, LAST) + dot(grad_up, up_weight, LAST)
        grad_ref[...] = grad_two.astype(BF16)

    def out(width):
        return pl.BlockSpec((chunk, width), lambda i, _: (i, 0))

    widths = (wide, wide, wide, model, model, model)
    kinds = (BF16,) * 6
    return pl.pallas_call(
        body,
        grid_spec=pltpu.PrefetchScalarGridSpec(
            num_scalar_prefetch=1,
            grid=(steps,),
            in_specs=[HELD] * (2 * count + 5 + len(others)),
            out_specs=[out(w) for w in widths],
            scratch_shapes=[
                pltpu.VMEM((chips, tok, model), BF16),
                pltpu.VMEM((chips, tok, model), BF16),
                pltpu.VMEM((2, 2 * chips, 2, half, wide), BF16),
                pltpu.VMEM(down.shape, BF16),
                pltpu.SemaphoreType.DMA((count,)),
                pltpu.SemaphoreType.DMA((count,)),
                pltpu.SemaphoreType.DMA((9,)),
            ],
        ),
        out_shape=[shaped((chips * tok, w), kind) for w, kind in zip(widths, kinds)],
        cost_estimate=takes(28), compiler_params=ROOMY,
    )(
        ring.table,
        *[piece for _, _, piece in twos],
        *[piece for _, _, piece in cots],
        *weights,
        down,
        *others,
    )


def load_window(table, at, own_ref, other_ref, window, rows):
    chips = own_ref.shape[0]
    for b in range(window.shape[0] // rows):
        place = table[at + b]
        target = window.at[b * rows : (b + 1) * rows, :]

        @pl.when(place < chips)
        def _():
            target[...] = own_ref[place]

        @pl.when(place >= chips)
        def _():
            target[...] = other_ref[place - chips]


def write_bias(first_ref, bias, rows):
    keys = bias.shape[0]
    key = lax.broadcasted_iota(jnp.int32, (keys, rows), 0)
    token = lax.broadcasted_iota(jnp.int32, (keys, rows), 1)
    allowed = (key >= first_ref[...]) & (key <= token + (keys - rows))
    values = jnp.where(allowed, 0.0, -jnp.inf)
    bias[:, :rows] = values
    bias[:, rows:] = values


def stacked(block, low_side):
    turned = pltpu.roll(block, HEAD_DIM, 1)
    low = lane_low(block.shape)
    if low_side:
        one, two = jnp.where(low, block, 0.0), jnp.where(low, turned, 0.0)
    else:
        one, two = jnp.where(low, 0.0, turned), jnp.where(low, 0.0, block)
    return jnp.concatenate([one, two], 0).astype(BF16)


def attend_kernel(
    ring, table, proj_ref, own_ref, other_ref, first_ref, cos_ref, sin_ref, q_ref, out_ref, log_ref, window, turned, bias
):
    rows = proj_ref.shape[0]

    @pl.when(pl.program_id(1) == 0)
    def _():
        load_window(table, ring.window, own_ref, other_ref, window, rows)
        turned[...] = jnp.transpose(window[...].astype(F32)).astype(BF16)

    @pl.when((pl.program_id(0) == 0) & (pl.program_id(1) == 0))
    def _():
        write_bias(first_ref, bias, rows)

    block = proj_ref[...]
    block = block * cos_ref[...] + rotated(block) * sin_ref[...]
    q_ref[...] = block.astype(BF16)
    queries = stacked(block * SCALE, True)
    score = dot(window[...], queries, LAST) + bias[...]
    top = jnp.max(score, 0, keepdims=True)
    expon = jnp.exp(score - top)
    total = jnp.sum(expon, 0, keepdims=True)
    log_ref[0] = top + jnp.log(total)
    out = jnp.transpose(dot(turned[...], expon.astype(BF16)) * (1.0 / total))
    one, two = out[:rows], out[rows:]
    out_ref[...] = jnp.where(lane_low(one.shape), pltpu.roll(one, HEAD_DIM, 1), two).astype(BF16)


def attend_back_kernel(
    ring,
    table,
    q_ref,
    grad_ref,
    att_ref,
    log_ref,
    own_ref,
    other_ref,
    first_ref,
    cos_ref,
    sin_ref,
    gq_ref,
    gown_ref,
    gother_ref,
    window,
    turned,
    total,
    bias,
):
    rows = q_ref.shape[0]
    keys = window.shape[0]
    chips = own_ref.shape[0]
    step = pl.program_id(1)

    @pl.when(step == 0)
    def _():
        load_window(table, ring.window, own_ref, other_ref, window, rows)
        turned[...] = jnp.transpose(window[...].astype(F32)).astype(BF16)
        total[...] = jnp.zeros_like(total)

    @pl.when((pl.program_id(0) == 0) & (step == 0))
    def _():
        write_bias(first_ref, bias, rows)

    grad = grad_ref[...].astype(F32)
    queries = stacked(q_ref[...].astype(F32) * SCALE, True)
    grads = stacked(grad, False)
    product = jnp.transpose(grad * att_ref[...].astype(F32))
    delta = jnp.concatenate(
        [
            jnp.sum(product[:HEAD_DIM], 0, keepdims=True),
            jnp.sum(product[HEAD_DIM:], 0, keepdims=True),
        ],
        1,
    )
    score = dot(window[...], queries, LAST) + bias[...]
    probs = jnp.exp(score - log_ref[0])
    grad_probs = dot(window[...], grads, LAST)
    grad_scores = (probs * (grad_probs - delta)).astype(BF16)
    total[...] += dot(grad_scores, queries) + dot(probs.astype(BF16), grads)
    grad_queries = jnp.transpose(dot(turned[...], grad_scores) * SCALE)
    one, two = grad_queries[:rows], grad_queries[rows:]
    block = jnp.where(lane_low(one.shape), one, pltpu.roll(two, HEAD_DIM, 1))
    gq_ref[...] = (block * cos_ref[...] - rotated(block) * sin_ref[...]).astype(BF16)

    @pl.when(step == pl.num_programs(1) - 1)
    def _():
        gown_ref[...] = jnp.zeros_like(gown_ref)
        gother_ref[...] = jnp.zeros_like(gother_ref)
        for b in range(keys // rows):
            place = table[ring.window + b]
            block = total[b * rows : (b + 1) * rows, :]

            @pl.when(place < chips)
            def _():
                gown_ref[place] = block.astype(BF16)

            @pl.when(place >= chips)
            def _():
                gother_ref[place - chips] = block.astype(BF16)


def attention_call(kernel, ring, groups, ins, outs, scratch, before, others, cost):
    start, stop = groups
    inner = HEADS // KV_HEADS // 2
    given = len(ins)

    def body(table, *refs):
        kernel(ring, table, *refs[:given], *refs[given + len(before) + len(others) :])

    def spec(entry):
        shape, place = entry
        return pl.BlockSpec(
            shape, lambda g, i, table: place(g + start, (g + start) * inner + i, table)
        )

    return pl.pallas_call(
        body,
        grid_spec=pltpu.PrefetchScalarGridSpec(
            num_scalar_prefetch=1,
            grid=(stop - start, inner),
            in_specs=[spec(entry) for _, entry in ins] + [HELD] * (len(before) + len(others)),
            out_specs=[spec(entry) for _, entry in outs],
            scratch_shapes=scratch,
        ),
        out_shape=[shape for shape, _ in outs],
        input_output_aliases={1 + given + k: k for k in range(len(before))},
        cost_estimate=takes(cost), compiler_params=ROOMY,
    )(ring.table, *[value for value, _ in ins], *before, *others)


def attention_specs(ring, rows):
    return (
        ((rows, LANES), lambda g, pair, table: (0, pair)),
        ((rows, LANES), lambda g, pair, table: (0, table[ring.place_near + pair])),
        ((1, 1, 2 * rows), lambda g, pair, table: (pair, 0, 0)),
        ((ring.chips, rows, LANES), lambda g, pair, table: (0, 0, g)),
        ((1, rows), lambda g, pair, table: (0, 0)),
        ((rows, LANES), lambda g, pair, table: (0, 0)),
    )


def attend(ring, groups, others, keys, proj, own, other, first, cosine, sine, before=()):
    rows = proj.shape[0]
    pairs = HEADS // 2
    block, near_block, log_block, kv_block, row, table = attention_specs(ring, rows)
    return attention_call(
        attend_kernel,
        ring,
        groups,
        [(proj, block), (own, kv_block), (other, kv_block)]
        + [(first, row), (cosine, table), (sine, table)],
        [
            (shaped((rows, pairs * LANES), BF16), block),
            (shaped((rows, pairs * LANES), BF16), near_block),
            (shaped((pairs, 1, 2 * rows), F32), log_block),
        ],
        [
            pltpu.VMEM((keys, LANES), BF16),
            pltpu.VMEM((LANES, keys), BF16),
            pltpu.VMEM((keys, 2 * rows), F32),
        ],
        before,
        others,
        14,
    )


def attend_back(
    ring, groups, others, keys, queries, grad, attended, logs, own, other, first, cosine, sine, before=()
):
    rows = queries.shape[0]
    block, near_block, log_block, kv_block, row, table = attention_specs(ring, rows)
    return attention_call(
        attend_back_kernel,
        ring,
        groups,
        [
            (queries, block),
            (grad, near_block),
            (attended, near_block),
            (logs, log_block),
            (own, kv_block),
            (other, kv_block),
            (first, row),
            (cosine, table),
            (sine, table),
        ],
        [
            (shaped(queries.shape, BF16), block),
            (shaped(own.shape, BF16), kv_block),
            (shaped(own.shape, BF16), kv_block),
        ],
        [
            pltpu.VMEM((keys, LANES), BF16),
            pltpu.VMEM((LANES, keys), BF16),
            pltpu.VMEM((keys, LANES), F32),
            pltpu.VMEM((keys, 2 * rows), F32),
        ],
        before,
        others,
        5,
    )


def on_device(
    reps,
    shards,
    hidden_in,
    segments,
    cotangent,
    qkv_weight,
    out_weight,
    gate_up_weight,
    down_weight,
    attn_gain,
    ffn_gain,
):
    tok = hidden_in.shape[1]
    model = hidden_in.shape[2]
    rows, width = qkv_weight.shape
    blocks = min(REACH // tok, shards - 1) + 1
    ring = Ring(shards, blocks)
    chips = ring.chips
    middle = chips * rows
    ff = down_weight.shape[0] * shards
    wide = ff // chips
    half = rows // 2
    side = ring.side
    twin_map = [(i, i ^ 1) for i in range(reps)]
    side_groups = [list(range(s, reps, 2)) for s in range(2)]
    hidden, cot_local, seg_row = hidden_in[0], cotangent[0], segments[0]
    groups = ((0, KV_HEADS // 2), (KV_HEADS // 2, KV_HEADS))

    def twin(value):
        return lax.ppermute(value, "rep", twin_map)

    def rest_of_reps(value):
        if reps == 2:
            return value
        return lax.psum(value, "rep", axis_index_groups=side_groups)

    def over_reps(value):
        mine = rest_of_reps(value).astype(BF16)
        return mine.astype(F32) + twin(mine).astype(F32)

    mine = cut_columns(ring, gate_up_weight, wide)

    packed = pack_weight(qkv_weight, attn_gain, ffn_gain, side)
    qkv_pieces, qkv_marks = ring.gather_shared(*packed, twin)
    out_halves = [
        lax.dynamic_slice_in_dim(out_weight, place * (model // 2), model // 2, 1)
        for place in (side, 1 - side)
    ]
    out_pieces, out_marks = ring.gather_shared(
        after(out_halves[0], *qkv_marks[-2:]), out_halves[1], twin
    )
    mine = lax.all_to_all(
        after(mine, *out_marks[-2:]), "shard", 0, 0, axis_index_groups=ring.core_groups, tiled=True
    )

    offset = ring.index * tok
    local_seg = lax.dynamic_slice_in_dim(seg_row, offset, tok)
    starts = jnp.sum((seg_row[None, :] < local_seg[:, None]).astype(jnp.int32), 1)
    positions = offset + jnp.arange(tok, dtype=jnp.int32) - starts
    freqs = jnp.exp(
        (jnp.arange(LANES) % (HEAD_DIM // 2)).astype(F32) * (-2.0 * math.log(10000.0) / HEAD_DIM)
    )
    angles = positions.astype(F32)[:, None] * freqs[None, :]
    cosine, sine = jnp.cos(angles), jnp.sin(angles)
    first = (starts - offset + (blocks - 1) * tok)[None, :]

    proj, kv_local, input_one, factor_one, gains = project(
        ring, hidden, cosine, sine, qkv_pieces, width, tuple(out_marks[5:7])
    )
    kv_own = stack_blocks(ring, ring.gather(kv_local), ())
    kv_other = ring.swap(kv_own)
    tables = (kv_own, kv_other, first, cosine, sine)
    keys = blocks * tok
    kept = attend(ring, groups[0], (), keys, proj, *tables)
    theirs = twin(mine)
    cots = ring.gather(after(cot_local, mine))
    kept = attend(ring, groups[1], (), keys, proj, *tables, kept)
    queries, attended, logs = kept
    residual, factor_two, input_two = project_out(ring, attended, hidden, gains, out_pieces, tuple(p for *_, p in cots[1:3]))

    twos = ring.gather(input_two)
    weights = (mine, theirs, ring.swap(mine), ring.swap(theirs))
    down = join_rows(ring, down_weight, ring.swap(down_weight))
    activation, grad_gate, grad_up, grad_two, two, cot = feed_forward(
        ring, twos, cots, weights, down, ()
    )
    gu_gives = give_terms(ring, two, (grad_gate, grad_up))
    gu_gots = [ring.swap(v) for v in gu_gives]
    gu_keep, gu_give = halve_terms(ring, two, (grad_gate, grad_up), gu_gots)
    ffn_term = down_project(activation, down, (gu_give,))
    gu_recv = twin(gu_give)
    gu_sum = rest_of_reps(gu_keep + gu_recv.astype(F32)).astype(BF16)
    gu_sum = lax.all_to_all(
        gu_sum, "shard", 0, 0, axis_index_groups=ring.core_groups, tiled=True
    )
    grad_two, two_marks = ring.scatter(
        grad_two, lambda step, _: {3: (gu_give,), 4: (ffn_term,)}.get(step)
    )
    down_keep, down_give = down_terms(ring, activation, cot, two_marks[3])
    down_keep = rest_of_reps(down_keep + ring.swap(down_give).astype(F32)).astype(BF16)
    down_recv = twin(down_keep)

    grad_residual, residual_half, grad_attended, gain_two_term = back_out(
        ring, grad_two, residual, factor_two, gains, cot_local, out_pieces, (gu_recv,)
    )
    (out_give,) = give_terms(ring, attended, (residual_half,))
    out_got = ring.swap(out_give)
    out_keep, out_send = halve_terms(ring, attended, (residual_half,), (out_got,))
    out_recv = twin(out_send)
    tables = (logs, kv_own, kv_other, first, cosine, sine)
    ffn_out, ffn_marks = ring.scatter(ffn_term, lambda step, _: two_marks[-1] if step == 1 else ())
    back = attend_back(
        ring, groups[0], (), keys, queries, grad_attended, attended, *tables
    )
    back = attend_back(
        ring,
        groups[1],
        (*ffn_marks[0], gu_sum, out_send),
        keys,
        queries,
        grad_attended,
        attended,
        *tables,
        back,
    )
    grad_queries, kv_keep, kv_give = back
    gu_other = twin(gu_sum)
    (query_give,) = give_terms(ring, input_one, (grad_queries,))
    query_got = ring.swap(query_give)
    kv_got = ring.swap(after(kv_give, query_give))
    kv_term = (kv_keep.astype(F32) + kv_got.astype(F32)).astype(BF16)
    merged = merge_terms(ring, input_one, grad_queries, query_got, out_keep, out_recv)
    merged_sum, merged_marks = ring.scatter(merged)

    def kv_ties(step, marks):
        return {3: (merged, *ffn_marks[2])}.get(step)

    grad_kv, kv_marks = ring.scatter(kv_term.reshape(chips * tok, -1), kv_ties)
    grad_kv = finish_kv(ring, grad_kv, cosine, sine, merged_marks[0])
    (kv_give,) = give_terms(ring, input_one, (grad_kv,))
    (kv_term,) = keep_terms(ring, input_one, (grad_kv,), (ring.swap(kv_give),))
    grad_hidden, gain_one_term = back_project(
        ring,
        grad_queries,
        grad_kv,
        hidden,
        factor_one,
        gains,
        grad_residual,
        qkv_pieces,
        width,
        (*merged_marks[1], *ffn_marks[3]),
    )
    gain_terms = jnp.concatenate([gain_one_term[:1], gain_two_term[:1]], 0)
    gain_terms = gain_terms[:, :middle] + ring.swap(gain_terms[:, middle:])
    below = gain_terms.reshape(2, chips, rows).transpose(1, 0, 2).reshape(chips, 1, 2 * rows)
    below = jnp.pad(below, ((0, 0), (0, 31), (0, kv_term.shape[1] - 2 * rows))).astype(BF16)
    parts = jnp.concatenate([kv_term.reshape(chips, rows, -1), below], 1)
    kv_sum, last_marks = ring.scatter(
        parts.reshape(chips * (rows + 32), -1),
        lambda step, _: {3: merged_marks[2]}.get(step),
    )
    kv_sum = over_reps(summed(kv_sum))
    merged_sum = rest_of_reps(summed(merged_sum)).astype(BF16)
    other = twin(merged_sum)
    grad_queries = merged_sum[:rows].astype(F32) + other[:rows].astype(F32)
    grad_qkv = jnp.concatenate([grad_queries, kv_sum[:rows]], 1)
    mine, theirs = merged_sum[rows:], other[rows:]
    grad_out = jnp.concatenate([pick(side, mine, theirs), pick(side, theirs, mine)], 0)
    hidden_out = (residual + summed((ffn_out[0], ffn_out[1], after(ffn_out[2], grad_kv)))).astype(BF16)
    grad_down = down_keep.astype(F32) + after(down_recv, *last_marks[1]).astype(F32)
    return (
        hidden_out[None],
        grad_hidden[None],
        grad_qkv,
        grad_out.astype(F32),
        join_columns(ring, gu_sum, gu_other, (grad_kv,)),
        grad_down,
        kv_sum[rows, :rows],
        kv_sum[rows, rows : 2 * rows],
    )


def solution(mesh):
    reps, shards = mesh.shape["rep"], mesh.shape["shard"]

    def layer(*args):
        return on_device(reps, shards, *args)

    return jax.shard_map(
        layer,
        mesh=mesh,
        in_specs=(
            P("rep", "shard", None),
            P("rep", None),
            P("rep", "shard", None),
            P("shard", None),
            P("shard", None),
            P("shard", None),
            P("shard", None),
            P("shard"),
            P("shard"),
        ),
        out_specs=(
            P("rep", "shard", None),
            P("rep", "shard", None),
            P("shard", None),
            P("shard", None),
            P("shard", None),
            P("shard", None),
            P("shard"),
            P("shard"),
        ),
        check_vma=False,
    )
```

```python
import math

import jax
import jax.numpy as jnp
import numpy as np
from jax import lax
from jax.experimental import pallas as pl
from jax.experimental.pallas import tpu as pltpu
from jax.sharding import PartitionSpec as P

HEADS = 32
KV_HEADS = 4
HEAD_DIM = 64
REACH = 1024
EPS = 1e-05
F32 = jnp.float32
BF16 = jnp.bfloat16
LANES = 128
SCALE = HEAD_DIM**-0.5
LIMIT = 58 * 1024 * 1024
ROOMY = pltpu.CompilerParams(vmem_limit_bytes=LIMIT)
HELD = pl.BlockSpec(memory_space=pl.ANY)


def takes(micros):
    return pl.CostEstimate(
        flops=int(micros * 1.1e9), bytes_accessed=int(micros * 3.3e6), transcendentals=0
    )


def dot(a, b, dims=((1,), (0,))):
    return lax.dot_general(a, b, (dims, ((), ())), preferred_element_type=F32)


LAST = ((1,), (1,))
FIRST = ((0,), (0,))


def pick(flag, one, other):
    return jnp.where(flag == 0, one, other)


class Ring:
    def __init__(self, size, window):
        self.size = size
        self.chips = chips = size // 2
        rows = chips // 2
        self.order = [2 * i for i in range(rows)] + [2 * i + 1 for i in reversed(range(rows))]
        self.place = [self.order.index(chip) for chip in range(chips)]
        self.half = chips // 2

        def turned(step):
            return [
                (s, self.order[(self.place[s // 2] + step) % chips] * 2 + s % 2)
                for s in range(size)
            ]

        self.ahead = turned(1)
        self.back = turned(-1)
        self.sibling = [(s, s ^ 1) for s in range(size)]
        self.core_groups = [list(range(core, size, 2)) for core in range(2)]
        self.near, self.place_near, self.cores, self.place_cores, self.window = (
            k * size for k in range(5)
        )
        self.core_at = self.window + window
        self.side_at = self.core_at + 1
        table = []
        for side in range(2):
            for s in range(size):
                chip, core = s // 2, s % 2
                at = self.place[chip]
                near = [
                    self.order[(at + j) % chips] * 2 + (core ^ other)
                    for other in range(2)
                    for j in range(chips)
                ]
                cores = [j * 2 + (core ^ other) for other in range(2) for j in range(chips)]
                place_near = [near.index(d) for d in range(size)]
                place_cores = [cores.index(d) for d in range(size)]
                seen = [place_near[(s + 1 - window + b) % size] for b in range(window)]
                table.append(near + place_near + cores + place_cores + seen + [core, side])
        self.index = lax.axis_index("shard")
        self.side = lax.axis_index("rep") % 2
        self.table = lax.dynamic_index_in_dim(
            jnp.asarray(np.array(table, np.int32)), self.side * size + self.index, 0, False
        )

    def swap(self, value):
        return lax.ppermute(value, "shard", self.sibling)

    def gather(self, block, ties=None):
        n, h = self.chips, block.shape[0] // 2
        cw = ccw = block
        found = [(0, 0, block)]
        for k in range(1, self.half):
            if ties and k in ties:
                cw, ccw = after(cw, *ties[k]), after(ccw, *ties[k])
            cw = lax.ppermute(cw, "shard", self.ahead)
            ccw = lax.ppermute(ccw, "shard", self.back)
            found += [(n - k, 0, cw), (k, 0, ccw)]
        top = lax.ppermute(cw[:h], "shard", self.ahead)
        low = lax.ppermute(ccw[h:], "shard", self.back)
        return found + [(self.half, 0, top), (self.half, h, low)]

    def gather_shared(self, mine, other, twin, ties=None):
        own = self.gather(mine, ties)
        found = [(k, row, 0, piece) for k, row, piece in own]
        found += [(k, row, 1, twin(piece) if k else other) for k, row, piece in own]
        found += [(k + self.chips, row, part, self.swap(piece)) for k, row, part, piece in found]
        return found, [piece for _, _, piece in own]

    def scatter(self, parts, ties=None):
        n, m = self.chips, self.half
        rows = parts.shape[0] // n
        h = rows // 2
        cw, ccw = parts[m * rows : m * rows + h], parts[m * rows + h : (m + 1) * rows]
        marks = []
        for k in range(m - 1, -1, -1):
            if ties:
                others = ties(m - k, marks)
                if others:
                    cw, ccw = after(cw, *others), after(ccw, *others)
            cw = lax.ppermute(cw, "shard", self.ahead)
            ccw = lax.ppermute(ccw, "shard", self.back)
            marks.append((cw, ccw))
            if k > 0:
                cw, ccw = add_step(parts, rows, k, n - k, cw, ccw)
        return (parts, cw, ccw), marks


def add_step(parts, rows, ahead, back, cw, ccw):
    width = parts.shape[1]
    got = cw.shape[0]

    def body(ahead_ref, back_ref, cw_ref, ccw_ref, one_ref, two_ref):
        if got < rows:
            one_ref[got:] = ahead_ref[got:]
            two_ref[: rows - ccw.shape[0]] = back_ref[: rows - ccw.shape[0]]
        last = rows - ccw.shape[0]
        one_ref[:got] = (ahead_ref[:got].astype(F32) + cw_ref[...].astype(F32)).astype(BF16)
        two_ref[last:] = (back_ref[last:].astype(F32) + ccw_ref[...].astype(F32)).astype(BF16)

    return pl.pallas_call(
        body,
        grid=(1,),
        in_specs=[
            pl.BlockSpec((rows, width), lambda _: (ahead, 0)),
            pl.BlockSpec((rows, width), lambda _: (back, 0)),
            whole(cw.shape),
            whole(ccw.shape),
        ],
        out_specs=[whole((rows, width))] * 2,
        out_shape=[shaped((rows, width), BF16)] * 2,
        cost_estimate=takes(2.5), compiler_params=ROOMY,
    )(parts, parts, cw, ccw)


def summed(sums):
    parts, cw, ccw = sums
    return parts[: cw.shape[0]].astype(F32) + cw.astype(F32) + ccw.astype(F32)


def whole(shape):
    return pl.BlockSpec(shape, lambda *_: (0,) * len(shape))


def shaped(shape, kind):
    return jax.ShapeDtypeStruct(shape, kind)


def call(kernel, table, ins, outs, pieces=(), scratch=(), others=(), cost=3):
    count, more, extra = len(ins), len(pieces), len(others)

    def body(table_ref, *refs):
        behind = count + more + extra
        kernel(
            table_ref,
            refs[:count],
            refs[count : count + more],
            refs[behind : behind + len(outs)],
            refs[behind + len(outs) :],
        )

    return pl.pallas_call(
        body,
        grid_spec=pltpu.PrefetchScalarGridSpec(
            num_scalar_prefetch=1,
            grid=(1,),
            in_specs=[whole(v.shape) for v in ins] + [HELD] * (more + extra),
            out_specs=[whole(v.shape) for v in outs],
            scratch_shapes=list(scratch),
        ),
        out_shape=list(outs),
        compiler_params=ROOMY,
        cost_estimate=takes(cost),
    )(table, *ins, *pieces, *others)


def after(value, *others):
    return pl.pallas_call(
        lambda *refs: None,
        in_specs=[HELD] * (1 + len(others)),
        out_specs=HELD,
        out_shape=shaped(value.shape, value.dtype),
        input_output_aliases={0: 0},
    )(value, *others)


def fetches(pieces, refs, buffer, sems):
    return [
        pltpu.make_async_copy(
            ref, buffer.at[k, pl.ds(row, ref.shape[0])], sems.at[n]
        )
        for n, ((k, row, _), ref) in enumerate(zip(pieces, refs))
    ]


def shared_fetches(side, pieces, refs, buffer, sems):
    copies = []
    for n, ((k, row, part, _), ref) in enumerate(zip(pieces, refs)):
        rows, width = ref.shape
        start = pl.multiple_of((side if part == 0 else 1 - side) * width, LANES)
        target = buffer.at[k, pl.ds(row, rows), pl.ds(start, width)]
        copies.append(pltpu.make_async_copy(ref, target, sems.at[n]))
    return copies


def block_at(place):
    return pl.ds(pl.multiple_of(place * LANES, LANES), LANES)


def columns(block):
    return slice(block * LANES, (block + 1) * LANES)


def lane_low(shape):
    return lax.broadcasted_iota(jnp.int32, shape, len(shape) - 1) % LANES < HEAD_DIM


def rotated(values):
    quarter = HEAD_DIM // 2
    first = lax.broadcasted_iota(jnp.int32, values.shape, 1) % HEAD_DIM < quarter
    return jnp.where(
        first, -pltpu.roll(values, LANES - quarter, 1), pltpu.roll(values, quarter, 1)
    )


def pack_weight(weight, gain_one, gain_two, side):
    rows, width = weight.shape
    half = packed_width(width) // 2

    def body(side_ref, weight_ref, one_ref, two_ref, mine_ref, other_ref):
        lane = lax.broadcasted_iota(jnp.int32, (rows, LANES), 1)
        block = jnp.where(lane == 0, one_ref[...], jnp.where(lane == 1, two_ref[...], 0.0))
        first = side_ref[0] == 0
        tail = width - half

        def put(start, stop, left, right):
            mine_ref[:, start:stop] = jnp.where(first, left, right)
            other_ref[:, start:stop] = jnp.where(first, right, left)

        put(0, tail, weight_ref[:, :tail], weight_ref[:, half:])
        put(tail, tail + LANES, weight_ref[:, tail : tail + LANES], block.astype(BF16))
        if tail + LANES < half:
            left = weight_ref[:, tail + LANES : half]
            put(tail + LANES, half, left, jnp.zeros_like(left))

    gains = [g.astype(F32)[:, None] for g in (gain_one, gain_two)]
    return pl.pallas_call(
        body,
        grid_spec=pltpu.PrefetchScalarGridSpec(
            num_scalar_prefetch=1,
            grid=(1,),
            in_specs=[whole(weight.shape)] + [whole((rows, 1))] * 2,
            out_specs=[whole((rows, half))] * 2,
        ),
        out_shape=[shaped((rows, half), BF16)] * 2,
        cost_estimate=takes(3), compiler_params=ROOMY,
    )(side.astype(jnp.int32)[None], weight, *gains)


def packed_width(width):
    return -(-(width + LANES) // (2 * LANES)) * 2 * LANES


def project(ring, hidden, cosine, sine, pieces, width, others):
    size = ring.size
    rows, model = hidden.shape
    qsize = HEADS * HEAD_DIM
    step = 2 * LANES

    def kernel(table, ins, refs, outs, scratch):
        hidden_ref, cos_ref, sin_ref = ins
        q_ref, kv_ref, input_ref, factor_ref, gain_ref = outs
        buffer, sems = scratch
        copies = shared_fetches(table[ring.side_at], pieces, refs, buffer, sems)
        for copy in copies:
            copy.start()
        values = hidden_ref[...].astype(F32)
        factor = lax.rsqrt(jnp.mean(values * values, -1, keepdims=True) + EPS)
        factor_ref[...] = jnp.broadcast_to(factor, factor_ref.shape)
        for copy in copies:
            copy.wait()
        for k in range(size):
            gains = jnp.transpose(buffer[k, :, width : width + LANES].astype(F32))
            gain_ref[:, columns(k)] = gains[:8]
            part = hidden_ref[:, block_at(table[ring.near + k])].astype(F32)
            input_ref[:, columns(k)] = (part * factor * gains[:1]).astype(BF16)
        inputs = input_ref[...]
        for start in range(0, qsize, step):
            weights = buffer[:, :, start : start + step].reshape(model, step)
            q_ref[:, start : start + step] = dot(inputs, weights)
        weights = buffer[:, :, qsize:width].reshape(model, width - qsize)
        proj = dot(inputs, weights)
        for pair in range(KV_HEADS // 2):
            keys = proj[:, columns(pair)]
            keys = keys * cos_ref[...] + rotated(keys) * sin_ref[...]
            heads = proj[:, columns(KV_HEADS // 2 + pair)]
            low = lane_low(keys.shape)
            one = jnp.where(low, keys, pltpu.roll(heads, HEAD_DIM, 1))
            two = jnp.where(low, pltpu.roll(keys, HEAD_DIM, 1), heads)
            kv_ref[:, columns(2 * pair)] = one.astype(BF16)
            kv_ref[:, columns(2 * pair + 1)] = two.astype(BF16)

    return call(
        kernel,
        ring.table,
        [hidden, cosine, sine],
        [
            shaped((rows, qsize), F32),
            shaped((rows, KV_HEADS * LANES), BF16),
            shaped((rows, model), BF16),
            shaped((rows, LANES), F32),
            shaped((8, model), F32),
        ],
        [piece for *_, piece in pieces],
        [
            pltpu.VMEM((size, rows, packed_width(width)), BF16),
            pltpu.SemaphoreType.DMA((len(pieces),)),
        ],
        others,
        9,
    )


def stack_blocks(ring, pieces, others):
    rows, width = pieces[0][2].shape

    def body(*refs):
        copies = fetches(pieces, refs[: len(pieces)], refs[-2], refs[-1])
        for copy in copies:
            copy.start()
        for copy in copies:
            copy.wait()

    return pl.pallas_call(
        body,
        in_specs=[HELD] * (len(pieces) + len(others)),
        out_specs=pl.BlockSpec(memory_space=pltpu.VMEM),
        out_shape=shaped((ring.chips, rows, width), pieces[0][2].dtype),
        scratch_shapes=[pltpu.SemaphoreType.DMA((len(pieces),))],
        cost_estimate=takes(2.5), compiler_params=ROOMY,
    )(*[piece for _, _, piece in pieces], *others)


def project_out(ring, attended, hidden, gains, pieces, others):
    size = ring.size
    rows, model = hidden.shape
    step = 2 * LANES

    def kernel(table, ins, refs, outs, scratch):
        att_ref, hidden_ref, gain_ref = ins
        residual_ref, factor_ref, input_ref = outs
        buffer, sems = scratch
        copies = shared_fetches(table[ring.side_at], pieces, refs, buffer, sems)
        for copy in copies:
            copy.start()
        for copy in copies:
            copy.wait()
        inputs = att_ref[...]
        squares = jnp.zeros((rows, 1), F32)
        for start in range(0, model, step):
            weights = buffer[:, :, start : start + step].reshape(model, step)
            part = hidden_ref[:, start : start + step].astype(F32) + dot(inputs, weights)
            residual_ref[:, start : start + step] = part
            squares += jnp.sum(part * part, -1, keepdims=True)
        factor = lax.rsqrt(squares * (1.0 / model) + EPS)
        factor_ref[...] = jnp.broadcast_to(factor, factor_ref.shape)
        for k in range(size):
            device = table[ring.cores + k]
            gain = gain_ref[1:2, block_at(table[ring.place_near + device])]
            part = residual_ref[:, block_at(device)] * factor
            input_ref[:, columns(k)] = (part * gain).astype(BF16)

    return call(
        kernel,
        ring.table,
        [attended, hidden, gains],
        [shaped((rows, model), F32), shaped((rows, LANES), F32), shaped((rows, model), BF16)],
        [piece for *_, piece in pieces],
        [
            pltpu.VMEM((size, rows, model), BF16),
            pltpu.SemaphoreType.DMA((len(pieces),)),
        ],
        others,
        8,
    )


def back_out(ring, sums, residual, factor, gains, cot, pieces, others):
    size = ring.size
    rows, model = residual.shape

    def kernel(table, ins, refs, outs, scratch):
        own_ref, cw_ref, ccw_ref, residual_ref, factor_ref, gain_ref, cot_ref = ins
        grad_res_ref, half_ref, att_ref, term_ref = outs
        buffer, sems, total = scratch
        copies = shared_fetches(table[ring.side_at], pieces, refs, buffer, sems)
        for n in sorted(range(len(copies)), key=lambda n: pieces[n][0]):
            copies[n].start()
        factor = factor_ref[...]
        mean = jnp.zeros((rows, 1), F32)
        for d in range(size):
            place, source = (
                block_at(table[order + d]) for order in (ring.place_near, ring.place_cores)
            )
            grad = sum(ref[:, source].astype(F32) for ref in (own_ref, cw_ref, ccw_ref))
            total[:, columns(d)] = grad
            normed = residual_ref[:, columns(d)] * factor
            product = grad * normed
            term_ref[:, place] = jnp.broadcast_to(
                jnp.sum(product, 0, keepdims=True), (8, LANES)
            )
            mean += jnp.sum(product * gain_ref[1:2, place], -1, keepdims=True)
        mean *= 1.0 / model
        for d in range(size):
            place = block_at(table[ring.place_near + d])
            grad = total[:, columns(d)] * gain_ref[1:2, place]
            normed = residual_ref[:, columns(d)] * factor
            back = cot_ref[:, columns(d)].astype(F32) + factor * (grad - normed * mean)
            grad_res_ref[:, columns(d)] = back
            half_ref[:, columns(d)] = back.astype(BF16)
        halves = half_ref[...]
        for k in range(0, size, 2):
            for piece, copy in zip(pieces, copies):
                if piece[0] // 2 == k // 2:
                    copy.wait()
            weights = buffer[k : k + 2].reshape(2 * rows, model)
            att_ref[:, k * LANES : (k + 2) * LANES] = dot(halves, weights, LAST).astype(BF16)

    return call(
        kernel,
        ring.table,
        [sums[0][:rows], sums[1], sums[2], residual, factor, gains, cot],
        [
            shaped((rows, model), F32),
            shaped((rows, model), BF16),
            shaped((rows, model), BF16),
            shaped((8, model), F32),
        ],
        [piece for *_, piece in pieces],
        [
            pltpu.VMEM((size, rows, model), BF16),
            pltpu.SemaphoreType.DMA((len(pieces),)),
            pltpu.VMEM((rows, model), F32),
        ],
        others,
        3.5,
    )


def finish_kv(ring, sums, cosine, sine, others):
    def kernel(table, ins, refs, outs, scratch):
        own_ref, cw_ref, ccw_ref, cos_ref, sin_ref = ins
        grad = sum(ref[...].astype(F32) for ref in (own_ref, cw_ref, ccw_ref))
        for pair in range(KV_HEADS // 2):
            one = grad[:, columns(2 * pair)]
            two = grad[:, columns(2 * pair + 1)]
            low = lane_low(one.shape)
            keys = jnp.where(low, one, pltpu.roll(two, HEAD_DIM, 1))
            values = jnp.where(low, pltpu.roll(one, HEAD_DIM, 1), two)
            keys = keys * cos_ref[...] - rotated(keys) * sin_ref[...]
            outs[0][:, columns(pair)] = keys.astype(BF16)
            outs[0][:, columns(KV_HEADS // 2 + pair)] = values.astype(BF16)

    rows = sums[1].shape[0]
    return call(
        kernel,
        ring.table,
        [sums[0][:rows], sums[1], sums[2], cosine, sine],
        [shaped((rows, 2 * KV_HEADS * HEAD_DIM), BF16)],
        others=others,
    )[0]


def back_project(
    ring, grad_queries, grad_kv, hidden, factor, gains, grad_residual, pieces, width, others
):
    size = ring.size
    rows, model = hidden.shape
    qsize = grad_queries.shape[1]

    def kernel(table, ins, refs, outs, scratch):
        gq_ref, gkv_ref, hidden_ref, factor_ref, gain_ref, grad_res_ref = ins
        grad_ref, term_ref = outs
        buffer, sems, total = scratch
        copies = shared_fetches(table[ring.side_at], pieces, refs, buffer, sems)
        for n in sorted(range(len(copies)), key=lambda n: pieces[n][0]):
            copies[n].start()
        queries, keys = gq_ref[...], gkv_ref[...]
        for k in range(0, size, 2):
            for piece, copy in zip(pieces, copies):
                if piece[0] // 2 == k // 2:
                    copy.wait()
            weights = buffer[k : k + 2].reshape(2 * rows, packed_width(width))
            total[:, k * LANES : (k + 2) * LANES] = dot(
                queries, weights[:, :qsize], LAST
            ) + dot(keys, weights[:, qsize:width], LAST)
        factor = factor_ref[...]
        mean = jnp.zeros((rows, 1), F32)
        for k in range(size):
            normed = hidden_ref[:, block_at(table[ring.near + k])].astype(F32) * factor
            product = total[:, columns(k)] * normed
            term_ref[:, columns(k)] = jnp.broadcast_to(
                jnp.sum(product, 0, keepdims=True), (8, LANES)
            )
            mean += jnp.sum(product * gain_ref[:1, columns(k)], -1, keepdims=True)
        mean *= 1.0 / model
        for k in range(size):
            place = block_at(table[ring.near + k])
            normed = hidden_ref[:, place].astype(F32) * factor
            scaled = total[:, columns(k)] * gain_ref[:1, columns(k)]
            back = grad_res_ref[:, place] + factor * (scaled - normed * mean)
            grad_ref[:, place] = back.astype(BF16)

    return call(
        kernel,
        ring.table,
        [grad_queries, grad_kv, hidden, factor, gains, grad_residual],
        [shaped((rows, model), BF16), shaped((8, model), F32)],
        [piece for *_, piece in pieces],
        [
            pltpu.VMEM((size, rows, packed_width(width)), BF16),
            pltpu.SemaphoreType.DMA((len(pieces),)),
            pltpu.VMEM((rows, model), F32),
        ],
        others,
        4.025,
    )


def cut_columns(ring, weight, wide):
    rows = weight.shape[0]
    half = rows // 2

    def kernel(table, ins, refs, outs, scratch):
        upper = table[ring.side_at] == 0
        for chip in range(ring.chips):
            for part in range(2):
                start = (part * ring.chips + chip) * wide
                block = ins[0][:, start : start + wide].astype(F32)
                outs[0][chip, part] = jnp.where(upper, block[:half], block[half:]).astype(BF16)

    return call(
        kernel, ring.table, [weight], [shaped((ring.chips, 2, half, wide), BF16)]
    )[0]


def join_columns(ring, mine, theirs, others):
    chips, parts, half, wide = mine.shape

    def kernel(table, ins, refs, outs, scratch):
        flip = table[ring.side_at] == 0
        for chip in range(chips):
            for part in range(parts):
                start = (part * chips + chip) * wide
                one, two = ins[0][chip, part].astype(F32), ins[1][chip, part].astype(F32)
                outs[0][:half, start : start + wide] = jnp.where(flip, one, two)
                outs[0][half:, start : start + wide] = jnp.where(flip, two, one)

    return call(
        kernel,
        ring.table,
        [mine, theirs],
        [shaped((2 * half, parts * chips * wide), F32)],
        others=others,
    )[0]


def step_columns(tokens):
    return (4 if tokens <= LANES else 2) * LANES


def give_terms(ring, inputs, grads, others=()):
    tokens, model = inputs.shape
    count, extra = len(grads), len(others)
    step = step_columns(tokens)
    steps = model // 2 // step

    def body(input_ref, *refs):
        for grad_ref, out_ref in zip(refs[:count], refs[count + extra :]):
            out_ref[...] = dot(input_ref[...], grad_ref[...], FIRST).astype(BF16)

    return pl.pallas_call(
        body,
        grid=(steps,),
        in_specs=[pl.BlockSpec((tokens, step), lambda i: (0, steps + i))]
        + [whole(g.shape) for g in grads]
        + [HELD] * extra,
        out_specs=[pl.BlockSpec((step, g.shape[1]), lambda i: (i, 0)) for g in grads],
        out_shape=[shaped((model // 2, g.shape[1]), BF16) for g in grads],
        cost_estimate=takes(2.1), compiler_params=ROOMY,
    )(inputs, *grads, *others)


def keep_terms(ring, inputs, grads, gots):
    tokens, model = inputs.shape
    count = len(grads)
    step = step_columns(tokens)

    def body(input_ref, *refs):
        for part in range(count):
            term = dot(input_ref[...], refs[part][...], FIRST)
            refs[2 * count + part][...] = (term + refs[count + part][...].astype(F32)).astype(BF16)

    blocks = [pl.BlockSpec((step, g.shape[1]), lambda i: (i, 0)) for g in grads]
    return pl.pallas_call(
        body,
        grid=(model // 2 // step,),
        in_specs=[pl.BlockSpec((tokens, step), lambda i: (0, i))]
        + [whole(g.shape) for g in grads]
        + blocks,
        out_specs=blocks,
        out_shape=[shaped((model // 2, g.shape[1]), BF16) for g in grads],
        cost_estimate=takes(1.75), compiler_params=ROOMY,
    )(inputs, *grads, *gots)


def merge_terms(ring, inputs, grads, got, halves, halves_got):
    tokens, model = inputs.shape
    chips, _, half, wide = halves.shape
    rows = model // ring.size
    step = step_columns(tokens)
    each = step // rows
    high = rows + half

    def body(input_ref, grad_ref, got_ref, half_ref, half_got_ref, out_ref):
        term = dot(input_ref[...], grad_ref[...], FIRST)
        for n in range(each):
            at = slice(n * rows, (n + 1) * rows)
            total = term[at] + got_ref[at].astype(F32)
            out_ref[n * high : n * high + rows] = total.astype(BF16)
            total = half_ref[n, 0] + half_got_ref[n, 0].astype(F32)
            out_ref[n * high + rows : (n + 1) * high] = total.astype(BF16)

    block = pl.BlockSpec((each, 1, half, wide), lambda i: (i, 0, 0, 0))
    return pl.pallas_call(
        body,
        grid=(chips // each,),
        in_specs=[
            pl.BlockSpec((tokens, step), lambda i: (0, i)),
            whole(grads.shape),
            pl.BlockSpec((step, wide), lambda i: (i, 0)),
            block,
            block,
        ],
        out_specs=pl.BlockSpec((each * high, wide), lambda i: (i, 0)),
        out_shape=shaped((chips * high, wide), BF16),
        cost_estimate=takes(2), compiler_params=ROOMY,
    )(inputs, grads, got, halves, halves_got)


def halve_terms(ring, inputs, grads, gots):
    tokens, model = inputs.shape
    chips, count = ring.chips, len(grads)
    rows, wide = model // ring.size, grads[0].shape[1]
    half = rows // 2
    step = step_columns(tokens)
    each = step // rows

    def body(table, input_ref, *refs):
        upper = table[ring.side_at] == 0
        keep_ref, give_ref = refs[2 * count :]
        for part in range(count):
            term = dot(input_ref[...], refs[part][...], FIRST)
            for n in range(each):
                at = slice(n * rows, (n + 1) * rows)
                total = term[at] + refs[count + part][at].astype(F32)
                keep_ref[n, part] = jnp.where(upper, total[:half], total[half:])
                give_ref[n, part] = jnp.where(upper, total[half:], total[:half]).astype(BF16)

    return pl.pallas_call(
        body,
        grid_spec=pltpu.PrefetchScalarGridSpec(
            num_scalar_prefetch=1,
            grid=(chips // each,),
            in_specs=[pl.BlockSpec((tokens, step), lambda i, _: (0, i))]
            + [whole(g.shape) for g in grads]
            + [pl.BlockSpec((step, wide), lambda i, _: (i, 0))] * count,
            out_specs=[pl.BlockSpec((each, count, half, wide), lambda i, _: (i, 0, 0, 0))] * 2,
        ),
        out_shape=[shaped((chips, count, half, wide), kind) for kind in (F32, BF16)],
        cost_estimate=takes(3.15), compiler_params=ROOMY,
    )(ring.table, inputs, *grads, *gots)


def down_terms(ring, activation, cot, others):
    tokens, wide = activation.shape
    model = cot.shape[1]
    step, half = 2 * LANES, wide // 2

    def body(table, act_ref, cot_ref, *refs):
        keep_ref, give_ref = refs[len(others) :]
        total = dot(act_ref[...], cot_ref[...], FIRST)
        first = table[ring.core_at] == 0
        keep_ref[...] = jnp.where(first, total[:half], total[half:])
        give_ref[...] = jnp.where(first, total[half:], total[:half]).astype(BF16)

    return pl.pallas_call(
        body,
        grid_spec=pltpu.PrefetchScalarGridSpec(
            num_scalar_prefetch=1,
            grid=(model // step,),
            in_specs=[whole(activation.shape), pl.BlockSpec((tokens, step), lambda i, _: (0, i))]
            + [HELD] * len(others),
            out_specs=[pl.BlockSpec((half, step), lambda i, _: (0, i))] * 2,
        ),
        out_shape=[shaped((half, model), kind) for kind in (F32, BF16)],
        cost_estimate=takes(3.5), compiler_params=ROOMY,
    )(ring.table, activation, cot, *others)


def down_project(activation, down, others):
    tokens, wide = activation.shape
    model = down.shape[1]
    step = 2 * LANES

    def body(act_ref, down_ref, *refs):
        refs[-1][...] = dot(act_ref[...], down_ref[...]).astype(BF16)

    return pl.pallas_call(
        body,
        grid=(tokens // step,),
        in_specs=[pl.BlockSpec((step, wide), lambda i: (i, 0)), whole(down.shape)]
        + [HELD] * len(others),
        out_specs=pl.BlockSpec((step, model), lambda i: (i, 0)),
        out_shape=shaped((tokens, model), BF16),
        cost_estimate=takes(2.45), compiler_params=ROOMY,
    )(activation, down, *others)


def join_rows(ring, mine, theirs):
    rows, wide = mine.shape

    def body(table, mine_ref, theirs_ref, out_ref, sems):
        core = table[ring.core_at]
        copies = []
        for n, (place, ref) in enumerate(((core, mine_ref), (1 - core, theirs_ref))):
            target = out_ref.at[pl.ds(pl.multiple_of(place * rows, 16), rows)]
            copies.append(pltpu.make_async_copy(ref, target, sems.at[n]))
        for copy in copies:
            copy.start()
        for copy in copies:
            copy.wait()

    return pl.pallas_call(
        body,
        grid_spec=pltpu.PrefetchScalarGridSpec(
            num_scalar_prefetch=1,
            grid=(1,),
            in_specs=[HELD] * 2,
            out_specs=whole((2 * rows, wide)),
            scratch_shapes=[pltpu.SemaphoreType.DMA((2,))],
        ),
        out_shape=shaped((2 * rows, wide), mine.dtype),
        cost_estimate=takes(4), compiler_params=ROOMY,
    )(ring.table, mine, theirs)


def feed_forward(ring, twos, cots, weights, down, others):
    chips = ring.chips
    tok, model = twos[0][2].shape
    _, _, half, wide = weights[0].shape
    each = chips // 2
    steps = chips // each
    chunk = each * tok
    count = len(twos)

    def body(table, *refs):
        two_refs, cot_refs = refs[:count], refs[count : 2 * count]
        weight_refs = refs[2 * count : 2 * count + 4]
        down_ref = refs[2 * count + 4]
        outs = refs[2 * count + 5 + len(others) :]
        act_ref, gate_ref, up_ref, grad_ref, two_out, cot_out = outs[:6]
        two_buf, cot_buf, weight_buf, down_buf, two_sems, cot_sems, weight_sems = outs[6:]
        step = pl.program_id(0)
        side = table[ring.side_at]
        moves = [pltpu.make_async_copy(down_ref, down_buf, weight_sems.at[8])]
        for n, ref in enumerate(weight_refs):
            place = side if n % 2 == 0 else 1 - side
            for part in range(2):
                target = weight_buf.at[part, pl.ds(n // 2 * chips, chips), place]
                sem = weight_sems.at[2 * n + part]
                moves.append(pltpu.make_async_copy(ref.at[:, part], target, sem))
        blocks = fetches(twos, two_refs, two_buf, two_sems)
        blocks += fetches(cots, cot_refs, cot_buf, cot_sems)

        @pl.when(step == 0)
        def _():
            for move in moves + blocks:
                move.start()
            for move in moves:
                move.wait()

        for at in range(steps):

            @pl.when(step == at)
            def _():
                for (slot, _, _), block in zip(twos + cots, blocks):
                    if slot // each == at:
                        block.wait()

        two = two_buf[pl.ds(step * each, each)].reshape(chunk, model)
        cot = cot_buf[pl.ds(step * each, each)].reshape(chunk, model)
        two_out[...] = two
        cot_out[...] = cot
        gate_weight = weight_buf[0].reshape(model, wide)
        up_weight = weight_buf[1].reshape(model, wide)
        gate = dot(two, gate_weight)
        upward = dot(two, up_weight)
        grad = dot(cot, down_buf[...], LAST)
        sigma = jax.nn.sigmoid(gate)
        act_ref[...] = (gate * sigma * upward).astype(BF16)
        grad_gate = (grad * upward * (sigma * (1.0 + gate * (1.0 - sigma)))).astype(BF16)
        grad_up = (grad * gate * sigma).astype(BF16)
        gate_ref[...] = grad_gate
        up_ref[...] = grad_up
        grad_two = dot(grad_gate, gate_weight, LAST) + dot(grad_up, up_weight, LAST)
        grad_ref[...] = grad_two.astype(BF16)

    def out(width):
        return pl.BlockSpec((chunk, width), lambda i, _: (i, 0))

    widths = (wide, wide, wide, model, model, model)
    kinds = (BF16,) * 6
    return pl.pallas_call(
        body,
        grid_spec=pltpu.PrefetchScalarGridSpec(
            num_scalar_prefetch=1,
            grid=(steps,),
            in_specs=[HELD] * (2 * count + 5 + len(others)),
            out_specs=[out(w) for w in widths],
            scratch_shapes=[
                pltpu.VMEM((chips, tok, model), BF16),
                pltpu.VMEM((chips, tok, model), BF16),
                pltpu.VMEM((2, 2 * chips, 2, half, wide), BF16),
                pltpu.VMEM(down.shape, BF16),
                pltpu.SemaphoreType.DMA((count,)),
                pltpu.SemaphoreType.DMA((count,)),
                pltpu.SemaphoreType.DMA((9,)),
            ],
        ),
        out_shape=[shaped((chips * tok, w), kind) for w, kind in zip(widths, kinds)],
        cost_estimate=takes(28), compiler_params=ROOMY,
    )(
        ring.table,
        *[piece for _, _, piece in twos],
        *[piece for _, _, piece in cots],
        *weights,
        down,
        *others,
    )


def load_window(table, at, own_ref, other_ref, window, rows):
    chips = own_ref.shape[0]
    for b in range(window.shape[0] // rows):
        place = table[at + b]
        target = window.at[b * rows : (b + 1) * rows, :]

        @pl.when(place < chips)
        def _():
            target[...] = own_ref[place]

        @pl.when(place >= chips)
        def _():
            target[...] = other_ref[place - chips]


def write_bias(first_ref, bias, rows):
    keys = bias.shape[0]
    key = lax.broadcasted_iota(jnp.int32, (keys, rows), 0)
    token = lax.broadcasted_iota(jnp.int32, (keys, rows), 1)
    allowed = (key >= first_ref[...]) & (key <= token + (keys - rows))
    values = jnp.where(allowed, 0.0, -jnp.inf)
    bias[:, :rows] = values
    bias[:, rows:] = values


def stacked(block, low_side):
    turned = pltpu.roll(block, HEAD_DIM, 1)
    low = lane_low(block.shape)
    if low_side:
        one, two = jnp.where(low, block, 0.0), jnp.where(low, turned, 0.0)
    else:
        one, two = jnp.where(low, 0.0, turned), jnp.where(low, 0.0, block)
    return jnp.concatenate([one, two], 0).astype(BF16)


def attend_kernel(
    ring, table, proj_ref, own_ref, other_ref, first_ref, cos_ref, sin_ref, q_ref, out_ref, log_ref, window, turned, bias
):
    rows = proj_ref.shape[0]

    @pl.when(pl.program_id(1) == 0)
    def _():
        load_window(table, ring.window, own_ref, other_ref, window, rows)
        turned[...] = jnp.transpose(window[...].astype(F32)).astype(BF16)

    @pl.when((pl.program_id(0) == 0) & (pl.program_id(1) == 0))
    def _():
        write_bias(first_ref, bias, rows)

    block = proj_ref[...]
    block = block * cos_ref[...] + rotated(block) * sin_ref[...]
    q_ref[...] = block.astype(BF16)
    queries = stacked(block * SCALE, True)
    score = dot(window[...], queries, LAST) + bias[...]
    top = jnp.max(score, 0, keepdims=True)
    expon = jnp.exp(score - top)
    total = jnp.sum(expon, 0, keepdims=True)
    log_ref[0] = top + jnp.log(total)
    out = jnp.transpose(dot(turned[...], expon.astype(BF16)) * (1.0 / total))
    one, two = out[:rows], out[rows:]
    out_ref[...] = jnp.where(lane_low(one.shape), pltpu.roll(one, HEAD_DIM, 1), two).astype(BF16)


def attend_back_kernel(
    ring,
    table,
    q_ref,
    grad_ref,
    att_ref,
    log_ref,
    own_ref,
    other_ref,
    first_ref,
    cos_ref,
    sin_ref,
    gq_ref,
    gown_ref,
    gother_ref,
    window,
    turned,
    total,
    bias,
):
    rows = q_ref.shape[0]
    keys = window.shape[0]
    chips = own_ref.shape[0]
    step = pl.program_id(1)

    @pl.when(step == 0)
    def _():
        load_window(table, ring.window, own_ref, other_ref, window, rows)
        turned[...] = jnp.transpose(window[...].astype(F32)).astype(BF16)
        total[...] = jnp.zeros_like(total)

    @pl.when((pl.program_id(0) == 0) & (step == 0))
    def _():
        write_bias(first_ref, bias, rows)

    grad = grad_ref[...].astype(F32)
    queries = stacked(q_ref[...].astype(F32) * SCALE, True)
    grads = stacked(grad, False)
    product = jnp.transpose(grad * att_ref[...].astype(F32))
    delta = jnp.concatenate(
        [
            jnp.sum(product[:HEAD_DIM], 0, keepdims=True),
            jnp.sum(product[HEAD_DIM:], 0, keepdims=True),
        ],
        1,
    )
    score = dot(window[...], queries, LAST) + bias[...]
    probs = jnp.exp(score - log_ref[0])
    grad_probs = dot(window[...], grads, LAST)
    grad_scores = (probs * (grad_probs - delta)).astype(BF16)
    total[...] += dot(grad_scores, queries) + dot(probs.astype(BF16), grads)
    grad_queries = jnp.transpose(dot(turned[...], grad_scores) * SCALE)
    one, two = grad_queries[:rows], grad_queries[rows:]
    block = jnp.where(lane_low(one.shape), one, pltpu.roll(two, HEAD_DIM, 1))
    gq_ref[...] = (block * cos_ref[...] - rotated(block) * sin_ref[...]).astype(BF16)

    @pl.when(step == pl.num_programs(1) - 1)
    def _():
        gown_ref[...] = jnp.zeros_like(gown_ref)
        gother_ref[...] = jnp.zeros_like(gother_ref)
        for b in range(keys // rows):
            place = table[ring.window + b]
            block = total[b * rows : (b + 1) * rows, :]

            @pl.when(place < chips)
            def _():
                gown_ref[place] = block.astype(BF16)

            @pl.when(place >= chips)
            def _():
                gother_ref[place - chips] = block.astype(BF16)


def attention_call(kernel, ring, groups, ins, outs, scratch, before, others, cost):
    start, stop = groups
    inner = HEADS // KV_HEADS // 2
    given = len(ins)

    def body(table, *refs):
        kernel(ring, table, *refs[:given], *refs[given + len(before) + len(others) :])

    def spec(entry):
        shape, place = entry
        return pl.BlockSpec(
            shape, lambda g, i, table: place(g + start, (g + start) * inner + i, table)
        )

    return pl.pallas_call(
        body,
        grid_spec=pltpu.PrefetchScalarGridSpec(
            num_scalar_prefetch=1,
            grid=(stop - start, inner),
            in_specs=[spec(entry) for _, entry in ins] + [HELD] * (len(before) + len(others)),
            out_specs=[spec(entry) for _, entry in outs],
            scratch_shapes=scratch,
        ),
        out_shape=[shape for shape, _ in outs],
        input_output_aliases={1 + given + k: k for k in range(len(before))},
        cost_estimate=takes(cost), compiler_params=ROOMY,
    )(ring.table, *[value for value, _ in ins], *before, *others)


def attention_specs(ring, rows):
    return (
        ((rows, LANES), lambda g, pair, table: (0, pair)),
        ((rows, LANES), lambda g, pair, table: (0, table[ring.place_near + pair])),
        ((1, 1, 2 * rows), lambda g, pair, table: (pair, 0, 0)),
        ((ring.chips, rows, LANES), lambda g, pair, table: (0, 0, g)),
        ((1, rows), lambda g, pair, table: (0, 0)),
        ((rows, LANES), lambda g, pair, table: (0, 0)),
    )


def attend(ring, groups, others, keys, proj, own, other, first, cosine, sine, before=()):
    rows = proj.shape[0]
    pairs = HEADS // 2
    block, near_block, log_block, kv_block, row, table = attention_specs(ring, rows)
    return attention_call(
        attend_kernel,
        ring,
        groups,
        [(proj, block), (own, kv_block), (other, kv_block)]
        + [(first, row), (cosine, table), (sine, table)],
        [
            (shaped((rows, pairs * LANES), BF16), block),
            (shaped((rows, pairs * LANES), BF16), near_block),
            (shaped((pairs, 1, 2 * rows), F32), log_block),
        ],
        [
            pltpu.VMEM((keys, LANES), BF16),
            pltpu.VMEM((LANES, keys), BF16),
            pltpu.VMEM((keys, 2 * rows), F32),
        ],
        before,
        others,
        14,
    )


def attend_back(
    ring, groups, others, keys, queries, grad, attended, logs, own, other, first, cosine, sine, before=()
):
    rows = queries.shape[0]
    block, near_block, log_block, kv_block, row, table = attention_specs(ring, rows)
    return attention_call(
        attend_back_kernel,
        ring,
        groups,
        [
            (queries, block),
            (grad, near_block),
            (attended, near_block),
            (logs, log_block),
            (own, kv_block),
            (other, kv_block),
            (first, row),
            (cosine, table),
            (sine, table),
        ],
        [
            (shaped(queries.shape, BF16), block),
            (shaped(own.shape, BF16), kv_block),
            (shaped(own.shape, BF16), kv_block),
        ],
        [
            pltpu.VMEM((keys, LANES), BF16),
            pltpu.VMEM((LANES, keys), BF16),
            pltpu.VMEM((keys, LANES), F32),
            pltpu.VMEM((keys, 2 * rows), F32),
        ],
        before,
        others,
        5,
    )


def on_device(
    reps,
    shards,
    hidden_in,
    segments,
    cotangent,
    qkv_weight,
    out_weight,
    gate_up_weight,
    down_weight,
    attn_gain,
    ffn_gain,
):
    tok = hidden_in.shape[1]
    model = hidden_in.shape[2]
    rows, width = qkv_weight.shape
    blocks = min(REACH // tok, shards - 1) + 1
    ring = Ring(shards, blocks)
    chips = ring.chips
    middle = chips * rows
    ff = down_weight.shape[0] * shards
    wide = ff // chips
    half = rows // 2
    side = ring.side
    twin_map = [(i, i ^ 1) for i in range(reps)]
    side_groups = [list(range(s, reps, 2)) for s in range(2)]
    hidden, cot_local, seg_row = hidden_in[0], cotangent[0], segments[0]
    groups = ((0, KV_HEADS // 2), (KV_HEADS // 2, KV_HEADS))

    def twin(value):
        return lax.ppermute(value, "rep", twin_map)

    def rest_of_reps(value):
        if reps == 2:
            return value
        return lax.psum(value, "rep", axis_index_groups=side_groups)

    def over_reps(value):
        mine = rest_of_reps(value).astype(BF16)
        return mine.astype(F32) + twin(mine).astype(F32)

    mine = cut_columns(ring, gate_up_weight, wide)

    packed = pack_weight(qkv_weight, attn_gain, ffn_gain, side)
    qkv_pieces, qkv_marks = ring.gather_shared(*packed, twin)
    out_halves = [
        lax.dynamic_slice_in_dim(out_weight, place * (model // 2), model // 2, 1)
        for place in (side, 1 - side)
    ]
    out_pieces, out_marks = ring.gather_shared(
        after(out_halves[0], *qkv_marks[-2:]), out_halves[1], twin
    )
    mine = lax.all_to_all(
        after(mine, *out_marks[-2:]), "shard", 0, 0, axis_index_groups=ring.core_groups, tiled=True
    )

    offset = ring.index * tok
    local_seg = lax.dynamic_slice_in_dim(seg_row, offset, tok)
    starts = jnp.sum((seg_row[None, :] < local_seg[:, None]).astype(jnp.int32), 1)
    positions = offset + jnp.arange(tok, dtype=jnp.int32) - starts
    freqs = jnp.exp(
        (jnp.arange(LANES) % (HEAD_DIM // 2)).astype(F32) * (-2.0 * math.log(10000.0) / HEAD_DIM)
    )
    angles = positions.astype(F32)[:, None] * freqs[None, :]
    cosine, sine = jnp.cos(angles), jnp.sin(angles)
    first = (starts - offset + (blocks - 1) * tok)[None, :]

    proj, kv_local, input_one, factor_one, gains = project(
        ring, hidden, cosine, sine, qkv_pieces, width, tuple(out_marks[5:7])
    )
    kv_own = stack_blocks(ring, ring.gather(kv_local), ())
    kv_other = ring.swap(kv_own)
    tables = (kv_own, kv_other, first, cosine, sine)
    keys = blocks * tok
    kept = attend(ring, groups[0], (), keys, proj, *tables)
    theirs = twin(mine)
    cots = ring.gather(after(cot_local, mine))
    kept = attend(ring, groups[1], (), keys, proj, *tables, kept)
    queries, attended, logs = kept
    residual, factor_two, input_two = project_out(ring, attended, hidden, gains, out_pieces, tuple(p for *_, p in cots[1:3]))

    twos = ring.gather(input_two)
    weights = (mine, theirs, ring.swap(mine), ring.swap(theirs))
    down = join_rows(ring, down_weight, ring.swap(down_weight))
    activation, grad_gate, grad_up, grad_two, two, cot = feed_forward(
        ring, twos, cots, weights, down, ()
    )
    gu_gives = give_terms(ring, two, (grad_gate, grad_up))
    gu_gots = [ring.swap(v) for v in gu_gives]
    gu_keep, gu_give = halve_terms(ring, two, (grad_gate, grad_up), gu_gots)
    ffn_term = down_project(activation, down, (gu_give,))
    gu_recv = twin(gu_give)
    gu_sum = rest_of_reps(gu_keep + gu_recv.astype(F32)).astype(BF16)
    gu_sum = lax.all_to_all(
        gu_sum, "shard", 0, 0, axis_index_groups=ring.core_groups, tiled=True
    )
    grad_two, two_marks = ring.scatter(
        grad_two, lambda step, _: {3: (gu_give,), 4: (ffn_term,)}.get(step)
    )
    down_keep, down_give = down_terms(ring, activation, cot, two_marks[3])
    down_keep = rest_of_reps(down_keep + ring.swap(down_give).astype(F32)).astype(BF16)
    down_recv = twin(down_keep)

    grad_residual, residual_half, grad_attended, gain_two_term = back_out(
        ring, grad_two, residual, factor_two, gains, cot_local, out_pieces, (gu_recv,)
    )
    (out_give,) = give_terms(ring, attended, (residual_half,))
    out_got = ring.swap(out_give)
    out_keep, out_send = halve_terms(ring, attended, (residual_half,), (out_got,))
    out_recv = twin(out_send)
    tables = (logs, kv_own, kv_other, first, cosine, sine)
    ffn_out, ffn_marks = ring.scatter(ffn_term, lambda step, _: two_marks[-1] if step == 1 else ())
    back = attend_back(
        ring, groups[0], (), keys, queries, grad_attended, attended, *tables
    )
    back = attend_back(
        ring,
        groups[1],
        (*ffn_marks[0], gu_sum, out_send),
        keys,
        queries,
        grad_attended,
        attended,
        *tables,
        back,
    )
    grad_queries, kv_keep, kv_give = back
    gu_other = twin(gu_sum)
    (query_give,) = give_terms(ring, input_one, (grad_queries,))
    query_got = ring.swap(query_give)
    kv_got = ring.swap(after(kv_give, query_give))
    kv_term = (kv_keep.astype(F32) + kv_got.astype(F32)).astype(BF16)
    merged = merge_terms(ring, input_one, grad_queries, query_got, out_keep, out_recv)
    merged_sum, merged_marks = ring.scatter(merged)

    def kv_ties(step, marks):
        return {3: (merged, *ffn_marks[2])}.get(step)

    grad_kv, kv_marks = ring.scatter(kv_term.reshape(chips * tok, -1), kv_ties)
    grad_kv = finish_kv(ring, grad_kv, cosine, sine, merged_marks[0])
    (kv_give,) = give_terms(ring, input_one, (grad_kv,))
    (kv_term,) = keep_terms(ring, input_one, (grad_kv,), (ring.swap(kv_give),))
    grad_hidden, gain_one_term = back_project(
        ring,
        grad_queries,
        grad_kv,
        hidden,
        factor_one,
        gains,
        grad_residual,
        qkv_pieces,
        width,
        (*merged_marks[1], *ffn_marks[3]),
    )
    gain_terms = jnp.concatenate([gain_one_term[:1], gain_two_term[:1]], 0)
    gain_terms = gain_terms[:, :middle] + ring.swap(gain_terms[:, middle:])
    below = gain_terms.reshape(2, chips, rows).transpose(1, 0, 2).reshape(chips, 1, 2 * rows)
    below = jnp.pad(below, ((0, 0), (0, 31), (0, kv_term.shape[1] - 2 * rows))).astype(BF16)
    parts = jnp.concatenate([kv_term.reshape(chips, rows, -1), below], 1)
    kv_sum, last_marks = ring.scatter(
        parts.reshape(chips * (rows + 32), -1),
        lambda step, _: {3: merged_marks[2]}.get(step),
    )
    kv_sum = over_reps(summed(kv_sum))
    merged_sum = rest_of_reps(summed(merged_sum)).astype(BF16)
    other = twin(merged_sum)
    grad_queries = merged_sum[:rows].astype(F32) + other[:rows].astype(F32)
    grad_qkv = jnp.concatenate([grad_queries, kv_sum[:rows]], 1)
    mine, theirs = merged_sum[rows:], other[rows:]
    grad_out = jnp.concatenate([pick(side, mine, theirs), pick(side, theirs, mine)], 0)
    hidden_out = (residual + summed((ffn_out[0], ffn_out[1], after(ffn_out[2], grad_kv)))).astype(BF16)
    grad_down = down_keep.astype(F32) + after(down_recv, *last_marks[1]).astype(F32)
    return (
        hidden_out[None],
        grad_hidden[None],
        grad_qkv,
        grad_out.astype(F32),
        join_columns(ring, gu_sum, gu_other, (grad_kv,)),
        grad_down,
        kv_sum[rows, :rows],
        kv_sum[rows, rows : 2 * rows],
    )


def solution(mesh):
    reps, shards = mesh.shape["rep"], mesh.shape["shard"]

    def layer(*args):
        return on_device(reps, shards, *args)

    return jax.shard_map(
        layer,
        mesh=mesh,
        in_specs=(
            P("rep", "shard", None),
            P("rep", None),
            P("rep", "shard", None),
            P("shard", None),
            P("shard", None),
            P("shard", None),
            P("shard", None),
            P("shard"),
            P("shard"),
        ),
        out_specs=(
            P("rep", "shard", None),
            P("rep", "shard", None),
            P("shard", None),
            P("shard", None),
            P("shard", None),
            P("shard", None),
            P("shard"),
            P("shard"),
        ),
        check_vma=False,
    )
```
